32 devices in a mesh: video: 4 (over y, x), tm: 2 (over core), space: 4 (over z).
Axes of the slice: x: 2, y: 2, z: 4, core: 2. Of those that a mesh axis runs over, the one named last changes fastest.
Arguments:
- feature_maps: bfloat16 [8, 128, 240, 128], P(('video', 'tm'), 'space'), parts along dimension 0, may hold values from -27 to 27
- query_frame: int32 [2048], P('video'), parts along dimension 0, may hold values from 0 to 1
- query_row: int32 [2048], P('video'), parts along dimension 0, may hold values from 0 to 127
- query_col: int32 [2048], P('video'), parts along dimension 0, may hold values from 0 to 239
- ema_decay: float32 [8, 128], P(('video', 'tm')), parts along dimension 0, may hold values from 0.14 to 1
- dw_kernel: float32 [3, 128], replicated, may hold values from -3 to 3
- pw_weight: bfloat16 [128, 128], replicated, may hold values from -0.5 to 0.5
- out_weight: float32 [2, 128], replicated, may hold values from -2 to 2
Outputs:
- tracks: float32 [8, 2, 512], P(('video', 'tm')), parts along dimension 0
The draws below stay inside these ranges and needn't reach their ends.
There are 4 independent parts, one for each index of `video`. The reference program is written for one: setup_inputs(seed, part) draws one part's arguments, and reference() takes and returns one part's arrays. A program takes and returns all parts, laid end to end along the dimension named above; an argument that names none is the same for every part. Nothing has to cross between parts.
All inputs are finite; a program needn't handle non-finite values.
Results may differ from the reference program's by a relative error of at most 0.0026.
Values may be sent and summed in bfloat16 or wider, within the bound.
No kernel may reach another device: no remote copies, remote signals or barrier semaphores. Data moves between devices by JAX's collectives and lax.ppermute only.
A program may use at most 128 MiB of HBM per device.

```python
import math
import jax
import jax.numpy as jnp
import numpy as np
from jax import lax

CH = 128
WIDTH = 240
ROWS_DEV = 32
QUERIES = 512
KT = 3
HEIGHT = 128
CLIP_IMAGES = 2
N_SPACE = 4


def draw_feature_maps(key, part):
    base_values = jnp.clip(jax.random.normal(key, (CLIP_IMAGES, HEIGHT, WIDTH, CH), jnp.float32), -6.0, 6.0)
    return base_values.astype(jnp.bfloat16)


def draw_ema_decay(key, part):
    share = 0.5
    chooser = jax.random.uniform(jax.random.fold_in(key, 1), (1, CH), jnp.float32)
    slow_rate = jnp.exp(jax.random.uniform(jax.random.fold_in(key, 2), (1, CH), jnp.float32, math.log(0.1) / CLIP_IMAGES, -0.001))
    fast_rate = jax.random.uniform(jax.random.fold_in(key, 3), (1, CH), jnp.float32, 0.3, 0.85)
    reference_speed = jnp.where(chooser < share, slow_rate, fast_rate)
    arbitrary_shift = jax.random.uniform(jax.random.fold_in(key, 4), (CLIP_IMAGES, CH), jnp.float32, 0.97, 1.0)
    group_pick = jax.random.uniform(jax.random.fold_in(key, 5), (CLIP_IMAGES, 1), jnp.float32)
    group_length = jax.random.uniform(jax.random.fold_in(key, 6), (CLIP_IMAGES, 1), jnp.float32, 0.5, 0.8)
    image_group = jnp.where(group_pick < 3.0 / CLIP_IMAGES, group_length, 1.0)
    return reference_speed * arbitrary_shift * image_group


def place_ends(values, stream_key, low, largest):
    spot = [jax.random.randint(jax.random.fold_in(stream_key, axis), (), 0, length) for axis, length in enumerate(values.shape)]
    widest = values.shape.index(max(values.shape))
    next_to = spot[:widest] + [(spot[widest] + 1) % values.shape[widest]] + spot[widest + 1:]
    return values.at[tuple(spot)].set(low).at[tuple(next_to)].set(largest)


def cumulative_ranks(count, slope):
    loads = [(1 << 20) // math.isqrt(standing ** slope) + 1 for standing in range(1, count + 1)]
    width = 1 + sum(loads) // (1 << 30)
    return np.cumsum(np.array([max(1, weight // width) for weight in loads]))


def ranked_ids(rng, dims, amount, slope):
    table = cumulative_ranks(amount, slope)
    pick = jax.random.randint(jax.random.fold_in(rng, 1), dims, 0, int(table[amount - 1]))
    grade = jnp.searchsorted(jnp.asarray(table, jnp.int32), pick, side="right")
    return jax.random.permutation(jax.random.fold_in(rng, 2), amount)[grade].astype(jnp.int32)


def bell_draw(own_key, extent, scale, most, kind=jnp.bfloat16):
    result = jax.random.normal(own_key, extent, jnp.float32) * scale
    return jnp.minimum(jnp.maximum(result, -most), most).astype(kind)


def setup_inputs(seed: int = 0, part: int = 0) -> dict:
    key_list = jax.random.split(jax.random.key(seed), 9)
    own_keys = jax.random.split(jax.random.fold_in(key_list[8], part), 9)
    feature_maps = draw_feature_maps(jax.random.fold_in(jax.random.fold_in(key_list[8], part), 71), part)
    query_frame = place_ends(ranked_ids(own_keys[1], (QUERIES,), CLIP_IMAGES, 2), jax.random.fold_in(own_keys[1], 3), 0, CLIP_IMAGES - 1).astype(jnp.int32)
    query_row = place_ends(jax.random.randint(own_keys[2], (QUERIES,), 0, HEIGHT), jax.random.fold_in(own_keys[2], 1), 0, HEIGHT - 1).astype(jnp.int32)
    query_col = place_ends(jax.random.randint(own_keys[3], (QUERIES,), 0, WIDTH), jax.random.fold_in(own_keys[3], 1), 0, WIDTH - 1).astype(jnp.int32)
    ema_decay = draw_ema_decay(jax.random.fold_in(jax.random.fold_in(key_list[8], part), 71), part)
    dw_kernel = bell_draw(key_list[5], (KT, CH), 0.5, 3.0, jnp.float32)
    pw_weight = bell_draw(key_list[6], (CH, CH), CH ** -0.5, 0.5)
    out_weight = bell_draw(key_list[7], (2, CH), 0.3, 2.0, jnp.float32)
    return dict(feature_maps=feature_maps, query_frame=query_frame, query_row=query_row, query_col=query_col, ema_decay=ema_decay, dw_kernel=dw_kernel, pw_weight=pw_weight, out_weight=out_weight)


def reference(feature_maps, query_frame, query_row, query_col, ema_decay, dw_kernel, pw_weight, out_weight):
    query_feats = feature_maps[query_frame, query_row, query_col]
    scale = 1.0 / math.sqrt(CH)
    col_coord = jnp.arange(WIDTH, dtype=jnp.int32).astype(jnp.float32) / WIDTH
    row_blocks = (jnp.arange(HEIGHT, dtype=jnp.int32).astype(jnp.float32) / HEIGHT).reshape(N_SPACE, ROWS_DEV)

    def per_block(items):
        frame_map, block_rows = items
        scores = jnp.dot(query_feats, frame_map.T, preferred_element_type=jnp.float32) * scale
        highest = lax.optimization_barrier(jnp.max(scores, axis=1))
        weights_exp = jnp.exp(scores - highest[:, None])
        totals = lax.optimization_barrier(jnp.sum(weights_exp, axis=1))
        grid = weights_exp.reshape(QUERIES, ROWS_DEV, WIDTH)
        col_part = lax.optimization_barrier(jnp.sum(lax.optimization_barrier(jnp.sum(grid, axis=1)) * col_coord[None, :], axis=1))
        line_portion = lax.optimization_barrier(jnp.sum(lax.optimization_barrier(jnp.sum(grid, axis=2)) * block_rows[None, :], axis=1))
        pos_sum = jnp.stack([col_part, line_portion], 1)
        feat_sum = jnp.dot(weights_exp.astype(jnp.bfloat16), frame_map, preferred_element_type=jnp.float32)
        return (highest, totals, pos_sum, feat_sum)

    def per_frame(frame_map):
        blocks = frame_map.reshape(N_SPACE, ROWS_DEV * WIDTH, CH)
        highest, totals, pos_sum, feat_sum = lax.map(per_block, (blocks, row_blocks))
        top_value = lax.optimization_barrier(jnp.max(highest, axis=0))
        factor = jnp.exp(highest - top_value[None])
        grand_total = lax.optimization_barrier(jnp.sum(factor * totals, axis=0))
        position = lax.optimization_barrier(jnp.sum(factor[..., None] * pos_sum, axis=0)) / grand_total[:, None]
        focused_result = (lax.optimization_barrier(jnp.sum(factor[..., None] * feat_sum, axis=0)) / grand_total[:, None]).astype(jnp.bfloat16)
        return (position, focused_result)
    position, focused_result = lax.map(per_frame, feature_maps)
    padded = jnp.pad(focused_result.astype(jnp.float32), ((1, 1), (0, 0), (0, 0)))
    depth = jnp.zeros((CLIP_IMAGES, QUERIES, CH), jnp.float32)
    for tap in range(KT):
        depth = depth + dw_kernel[tap][None, None, :] * padded[tap:tap + CLIP_IMAGES]
    hidden = jax.nn.gelu(depth).astype(jnp.bfloat16)
    mixed = jnp.dot(hidden.reshape(-1, CH), pw_weight, preferred_element_type=jnp.float32).reshape(CLIP_IMAGES, QUERIES, CH)
    refined = focused_result.astype(jnp.float32) + mixed

    def ema_step(carried, items):
        retain, update = items
        carried = retain[None, :] * carried + (1.0 - retain[None, :]) * update
        return (carried, carried)
    start_state = jnp.zeros((QUERIES, CH), jnp.float32)
    final_state, memory = lax.scan(ema_step, start_state, (ema_decay, refined))
    delta = jnp.einsum('tqc,kc->tkq', memory, out_weight, precision=lax.Precision.HIGHEST)
    return jnp.transpose(position, (0, 2, 1)) + delta
```

```python
import functools
import math

import jax
import jax.numpy as jnp
from jax import lax
from jax.experimental import pallas as pl
from jax.experimental.pallas import tpu as pltpu
from jax.sharding import PartitionSpec as P

F32 = jnp.float32
BF16 = jnp.bfloat16
LANES = 128
AUX_ROWS = 8
VMEM_LIMIT = 40 * 1024 * 1024
NT = (((1,), (1,)), ((), ()))


def pick_chunk(total, limit):
    best = None
    for size in range(LANES, limit + 1, LANES):
        if total % size == 0 and (best is None or size % 256 == 0 or best % 256):
            best = size
    return best if best is not None else total


def gather_kernel(rows_here, map_width, frame_ref, row_ref, col_ref, map_ref, *out_refs):
    positions = map_ref.shape[0]
    queries = frame_ref.shape[1]
    tm = lax.axis_index("tm")
    row = row_ref[...] - lax.axis_index("space") * rows_here
    here = (frame_ref[...] == tm) & (row >= 0) & (row < rows_here)
    target = jnp.where(here, row * map_width + col_ref[...], -1)
    target = jnp.transpose(jnp.broadcast_to(target, (LANES, queries)))
    chunk = pick_chunk(positions, 1536)
    picked = None
    for base in range(0, positions, chunk):
        parts = []
        for lane_base in range(base, base + chunk, LANES):
            lane = lax.broadcasted_iota(jnp.int32, (queries, LANES), 1) + lane_base
            parts.append(jnp.where(lane == target, 1.0, 0.0).astype(BF16))
        hot = jnp.concatenate(parts, axis=1)
        term = jnp.dot(hot, map_ref[base : base + chunk, :], preferred_element_type=F32)
        picked = term if picked is None else picked + term
    if len(out_refs) == 1:
        out_refs[0][...] = picked.astype(BF16)
        return
    half = queries // 2
    first, second = picked[:half].astype(F32), picked[half:].astype(F32)
    out_refs[0][...] = jnp.where(tm == 0, first, second).astype(BF16)
    out_refs[1][...] = jnp.where(tm == 0, second, first).astype(BF16)


def volume_kernel(n_groups, rows_here, height, width, *refs):
    *query_refs, map_ref, coord_ref, decay_ref, out_ref = refs
    positions, channels = map_ref.shape
    factor = math.log2(math.e) / math.sqrt(channels)
    part_queries = query_refs[0].shape[0]
    n_parts = len(query_refs)
    group = part_queries * n_parts // n_groups
    feat_rows = out_ref.shape[1] - AUX_ROWS
    first_row = (lax.axis_index("space") * rows_here).astype(F32)
    tm = lax.axis_index("tm")
    chunk = pick_chunk(positions, 1280)
    state = [None] * n_parts
    for base in range(0, positions, chunk):
        keys = map_ref[base : base + chunk, :]
        values = jnp.concatenate([keys, coord_ref[base : base + chunk, :]], axis=1)
        for part in range(n_parts):
            scores = lax.dot_general(
                query_refs[part][...], keys, NT, preferred_element_type=F32
            )
            top = jnp.max(scores, axis=1, keepdims=True) * factor
            if state[part] is not None:
                old_top, old_sum = state[part]
                top = jnp.maximum(top, old_top)
            weights = jnp.exp2(scores * factor - top).astype(BF16)
            sums = jnp.dot(weights, values, preferred_element_type=F32)
            if state[part] is not None:
                sums = sums + jnp.exp2(old_top - top) * old_sum
            state[part] = (top, sums)
    decay = [decay_ref[...]]
    sub = lax.broadcasted_iota(jnp.int32, (AUX_ROWS, LANES), 0)
    for part in range(n_parts):
        top, sums = state[part]
        feats = sums[:, :channels] / sums[:, channels + 2 : channels + 3]
        extra = sums[:, channels:]
        lane = lax.broadcasted_iota(jnp.int32, extra.shape, 1)
        extra = jnp.transpose(jnp.where(lane == 3, top, extra))
        total = extra[2:3]
        rows = [extra[3:4]]
        rows += [total, extra[0:1] / total / width, (extra[1:2] / total + first_row) / height]
        aux = jnp.zeros((AUX_ROWS, part_queries), F32)
        wide = lax.broadcasted_iota(jnp.int32, aux.shape, 0)
        for index, values in enumerate(rows):
            aux = jnp.where(wide == index, values, aux)
        where = part if n_parts == 1 else jnp.where(tm == 0, part, 1 - part)
        groups_here = n_groups // n_parts
        for index in range(groups_here):
            shift = (part_queries - index * group) % part_queries
            block = pltpu.roll(aux, shift, 1) if shift else aux
            block = block[:, :LANES]
            for offset, piece in enumerate(decay):
                block = jnp.where(sub == len(rows) + offset, piece, block)
            pieces = [feats[index * group : (index + 1) * group]]
            if feat_rows > group:
                pieces.append(jnp.zeros((feat_rows - group, LANES), F32))
            pieces.append(block)
            out_ref[where * groups_here + index] = jnp.concatenate(pieces, axis=0).astype(
                out_ref.dtype
            )


def tail_kernel(n_tm, n_space, group, dw_ref, pw_ref, ow_ref, in_ref, out_ref):
    feat_rows = in_ref.shape[1] - AUX_ROWS
    n_blocks = n_tm * n_space
    blocks = [in_ref[index].astype(F32) for index in range(n_blocks)]
    aux = [block[feat_rows:] for block in blocks]
    positions, shares, decays = [], [], []
    for frame in range(n_tm):
        mine = aux[frame * n_space : (frame + 1) * n_space]
        top = mine[0][0:1]
        for block in mine[1:]:
            top = jnp.maximum(top, block[0:1])
        weight = [jnp.exp2(b[0:1] - top) * b[1:2] for b in mine]
        total = sum(weight[1:], weight[0])
        share = [w / total for w in weight]
        shares += share
        across = [s * b[2:3] for s, b in zip(share, mine)]
        down = [s * b[3:4] for s, b in zip(share, mine)]
        positions.append((sum(across[1:], across[0]), sum(down[1:], down[0])))
        decays.append(mine[0][4:5])
    pad_blocks = -(-n_blocks // 8) * 8
    table = jnp.zeros((pad_blocks, LANES), F32)
    sub = lax.broadcasted_iota(jnp.int32, table.shape, 0)
    for index, share in enumerate(shares):
        table = jnp.where(sub == index, share, table)
    table = jnp.transpose(table)
    attended = []
    for frame in range(n_tm):
        value = None
        for index in range(frame * n_space, (frame + 1) * n_space):
            term = table[:group, index : index + 1] * blocks[index][:group]
            value = term if value is None else value + term
        attended.append(value.astype(BF16).astype(F32))
    taps = dw_ref.shape[0]
    hidden = []
    for frame in range(n_tm):
        depth = None
        for tap in range(taps):
            source = frame + tap - taps // 2
            if 0 <= source < n_tm:
                term = dw_ref[tap : tap + 1, :] * attended[source]
                depth = term if depth is None else depth + term
        hidden.append(jax.nn.gelu(depth).astype(BF16).astype(F32))
    hidden = jnp.concatenate(hidden, axis=0).astype(BF16)
    mixed = jnp.dot(hidden, pw_ref[...], preferred_element_type=F32)
    memory = None
    out = jnp.zeros(out_ref.shape, F32)
    out_sub = lax.broadcasted_iota(jnp.int32, out.shape, 0)
    n_out = ow_ref.shape[0]
    for frame in range(n_tm):
        refined = attended[frame] + mixed[frame * group : (frame + 1) * group]
        fresh = (1.0 - decays[frame]) * refined
        memory = fresh if memory is None else decays[frame] * memory + fresh
        padded = memory
        if group < LANES:
            padded = jnp.concatenate([memory, jnp.zeros((LANES - group, LANES), F32)], axis=0)
        delta = lax.dot_general(
            ow_ref[...], padded, NT, preferred_element_type=F32, precision=lax.Precision.HIGHEST
        )
        for axis in range(n_out):
            line = positions[frame][axis] + delta[axis : axis + 1]
            out = jnp.where(out_sub == frame * n_out + axis, line, out)
    out_ref[...] = out


def call(kernel, out_shape, n_in, **cost):
    vmem = pl.BlockSpec(memory_space=pltpu.VMEM)
    return pl.pallas_call(
        kernel,
        out_shape=out_shape,
        in_specs=[vmem] * n_in,
        out_specs=jax.tree.map(lambda _: vmem, out_shape),
        compiler_params=pltpu.CompilerParams(vmem_limit_bytes=VMEM_LIMIT),
        cost_estimate=pl.CostEstimate(**cost),
    )


def swap(value, axis, bit):
    return lax.ppermute(value, axis, [(i, i ^ bit) for i in range(lax.axis_size(axis))])


def all_sum(value, axis):
    count = lax.axis_size(axis)
    if count & (count - 1):
        return lax.psum(value, axis)
    bit = 1
    while bit < count:
        value = value + swap(value, axis, bit)
        bit *= 2
    return value


def local(
    feature_maps, query_frame, query_row, query_col, ema_decay, dw_kernel, pw_weight, out_weight
):
    frames_here, rows_here, map_width, channels = feature_maps.shape
    assert frames_here == 1 and channels == LANES
    queries = query_frame.shape[0]
    n_tm, n_space = lax.axis_size("tm"), lax.axis_size("space")
    n_groups = n_tm * n_space
    group = queries // n_groups
    height = rows_here * n_space
    positions = rows_here * map_width
    maps = feature_maps.reshape(positions, channels)
    halves = 2 if n_tm == 2 else 1
    part = jax.ShapeDtypeStruct((queries // halves, channels), BF16)

    picked = call(
        functools.partial(gather_kernel, rows_here, map_width),
        [part] * halves,
        4,
        flops=2 * queries * positions * channels,
        bytes_accessed=2 * positions * channels,
        transcendentals=0,
    )(query_frame[None], query_row[None], query_col[None], maps)

    place = jnp.arange(positions, dtype=jnp.int32)[:, None]
    lane = jnp.arange(LANES, dtype=jnp.int32)[None, :]
    coords = jnp.where(
        lane == 0,
        place % map_width,
        jnp.where(lane == 1, place // map_width, jnp.where(lane == 2, 1, 0)),
    ).astype(BF16)

    if halves == 2:
        mine = picked[0] + swap(picked[1], "tm", 1)
        mine = all_sum(mine, "space")
        feats = [mine, swap(mine, "tm", 1)]
    else:
        feats = [all_sum(all_sum(picked[0], "tm"), "space")]

    feat_rows = -(-group // 8) * 8
    blocks = call(
        functools.partial(volume_kernel, n_groups, rows_here, height, map_width),
        jax.ShapeDtypeStruct((n_groups, feat_rows + AUX_ROWS, LANES), F32),
        halves + 3,
        flops=6 * queries * positions * channels,
        bytes_accessed=4 * positions * channels,
        transcendentals=queries * positions,
    )(*feats, maps, coords, ema_decay)

    blocks = lax.all_to_all(blocks, ("tm", "space"), 0, 0, tiled=True)

    n_out = out_weight.shape[0]
    out_rows = -(-n_tm * n_out // 8) * 8
    lines = call(
        functools.partial(tail_kernel, n_tm, n_space, group),
        jax.ShapeDtypeStruct((out_rows, LANES), F32),
        4,
        flops=2 * n_tm * group * channels * channels,
        bytes_accessed=4 * n_groups * (feat_rows + AUX_ROWS) * LANES,
        transcendentals=n_tm * group * channels,
    )(dw_kernel, pw_weight, out_weight, blocks)

    lines = lax.all_gather(lines, ("tm", "space"), axis=0)
    own = lax.dynamic_slice_in_dim(lines, lax.axis_index("tm") * n_out, n_out, axis=1)
    own = own[:, :, :group]
    return jnp.transpose(own, (1, 0, 2)).reshape(1, n_out, queries)


def solution(mesh):
    placed = (
        P(("video", "tm"), "space", None, None),
        P("video"),
        P("video"),
        P("video"),
        P(("video", "tm"), None),
        P(),
        P(),
        P(),
    )
    return jax.shard_map(
        local, mesh=mesh, in_specs=placed, out_specs=P(("video", "tm"), None, None), check_vma=False
    )
```

```python
import functools
import math

import jax
import jax.numpy as jnp
from jax import lax
from jax.experimental import pallas as pl
from jax.experimental.pallas import tpu as pltpu
from jax.sharding import PartitionSpec as P

F32 = jnp.float32
BF16 = jnp.bfloat16
LANES = 128
AUX_ROWS = 8
VMEM_LIMIT = 40 * 1024 * 1024
NT = (((1,), (1,)), ((), ()))


def pick_chunk(total, limit):
    best = None
    for size in range(LANES, limit + 1, LANES):
        if total % size == 0 and (best is None or size % 256 == 0 or best % 256):
            best = size
    return best if best is not None else total


def gather_kernel(rows_here, map_width, frame_ref, row_ref, col_ref, map_ref, *out_refs):
    positions = map_ref.shape[0]
    queries = frame_ref.shape[1]
    tm = lax.axis_index("tm")
    row = row_ref[...] - lax.axis_index("space") * rows_here
    here = (frame_ref[...] == tm) & (row >= 0) & (row < rows_here)
    target = jnp.where(here, row * map_width + col_ref[...], -1)
    target = jnp.transpose(jnp.broadcast_to(target, (LANES, queries)))
    chunk = pick_chunk(positions, 1536)
    picked = None
    for base in range(0, positions, chunk):
        parts = []
        for lane_base in range(base, base + chunk, LANES):
            lane = lax.broadcasted_iota(jnp.int32, (queries, LANES), 1) + lane_base
            parts.append(jnp.where(lane == target, 1.0, 0.0).astype(BF16))
        hot = jnp.concatenate(parts, axis=1)
        term = jnp.dot(hot, map_ref[base : base + chunk, :], preferred_element_type=F32)
        picked = term if picked is None else picked + term
    if len(out_refs) == 1:
        out_refs[0][...] = picked.astype(BF16)
        return
    half = queries // 2
    first, second = picked[:half].astype(F32), picked[half:].astype(F32)
    out_refs[0][...] = jnp.where(tm == 0, first, second).astype(BF16)
    out_refs[1][...] = jnp.where(tm == 0, second, first).astype(BF16)


def volume_kernel(n_groups, rows_here, height, width, *refs):
    *query_refs, map_ref, coord_ref, decay_ref, out_ref = refs
    positions, channels = map_ref.shape
    factor = math.log2(math.e) / math.sqrt(channels)
    part_queries = query_refs[0].shape[0]
    n_parts = len(query_refs)
    group = part_queries * n_parts // n_groups
    feat_rows = out_ref.shape[1] - AUX_ROWS
    first_row = (lax.axis_index("space") * rows_here).astype(F32)
    tm = lax.axis_index("tm")
    chunk = pick_chunk(positions, 1280)
    state = [None] * n_parts
    for base in range(0, positions, chunk):
        keys = map_ref[base : base + chunk, :]
        values = jnp.concatenate([keys, coord_ref[base : base + chunk, :]], axis=1)
        for part in range(n_parts):
            scores = lax.dot_general(
                query_refs[part][...], keys, NT, preferred_element_type=F32
            )
            top = jnp.max(scores, axis=1, keepdims=True) * factor
            if state[part] is not None:
                old_top, old_sum = state[part]
                top = jnp.maximum(top, old_top)
            weights = jnp.exp2(scores * factor - top).astype(BF16)
            sums = jnp.dot(weights, values, preferred_element_type=F32)
            if state[part] is not None:
                sums = sums + jnp.exp2(old_top - top) * old_sum
            state[part] = (top, sums)
    decay = [decay_ref[...]]
    sub = lax.broadcasted_iota(jnp.int32, (AUX_ROWS, LANES), 0)
    for part in range(n_parts):
        top, sums = state[part]
        feats = sums[:, :channels] / sums[:, channels + 2 : channels + 3]
        extra = sums[:, channels:]
        lane = lax.broadcasted_iota(jnp.int32, extra.shape, 1)
        extra = jnp.transpose(jnp.where(lane == 3, top, extra))
        total = extra[2:3]
        rows = [extra[3:4]]
        rows += [total, extra[0:1] / total / width, (extra[1:2] / total + first_row) / height]
        aux = jnp.zeros((AUX_ROWS, part_queries), F32)
        wide = lax.broadcasted_iota(jnp.int32, aux.shape, 0)
        for index, values in enumerate(rows):
            aux = jnp.where(wide == index, values, aux)
        where = part if n_parts == 1 else jnp.where(tm == 0, part, 1 - part)
        groups_here = n_groups // n_parts
        for index in range(groups_here):
            shift = (part_queries - index * group) % part_queries
            block = pltpu.roll(aux, shift, 1) if shift else aux
            block = block[:, :LANES]
            for offset, piece in enumerate(decay):
                block = jnp.where(sub == len(rows) + offset, piece, block)
            pieces = [feats[index * group : (index + 1) * group]]
            if feat_rows > group:
                pieces.append(jnp.zeros((feat_rows - group, LANES), F32))
            pieces.append(block)
            out_ref[where * groups_here + index] = jnp.concatenate(pieces, axis=0).astype(
                out_ref.dtype
            )


def tail_kernel(n_tm, n_space, group, dw_ref, pw_ref, ow_ref, in_ref, out_ref):
    feat_rows = in_ref.shape[1] - AUX_ROWS
    n_blocks = n_tm * n_space
    blocks = [in_ref[index].astype(F32) for index in range(n_blocks)]
    aux = [block[feat_rows:] for block in blocks]
    positions, shares, decays = [], [], []
    for frame in range(n_tm):
        mine = aux[frame * n_space : (frame + 1) * n_space]
        top = mine[0][0:1]
        for block in mine[1:]:
            top = jnp.maximum(top, block[0:1])
        weight = [jnp.exp2(b[0:1] - top) * b[1:2] for b in mine]
        total = sum(weight[1:], weight[0])
        share = [w / total for w in weight]
        shares += share
        across = [s * b[2:3] for s, b in zip(share, mine)]
        down = [s * b[3:4] for s, b in zip(share, mine)]
        positions.append((sum(across[1:], across[0]), sum(down[1:], down[0])))
        decays.append(mine[0][4:5])
    pad_blocks = -(-n_blocks // 8) * 8
    table = jnp.zeros((pad_blocks, LANES), F32)
    sub = lax.broadcasted_iota(jnp.int32, table.shape, 0)
    for index, share in enumerate(shares):
        table = jnp.where(sub == index, share, table)
    table = jnp.transpose(table)
    attended = []
    for frame in range(n_tm):
        value = None
        for index in range(frame * n_space, (frame + 1) * n_space):
            term = table[:group, index : index + 1] * blocks[index][:group]
            value = term if value is None else value + term
        attended.append(value.astype(BF16).astype(F32))
    taps = dw_ref.shape[0]
    hidden = []
    for frame in range(n_tm):
        depth = None
        for tap in range(taps):
            source = frame + tap - taps // 2
            if 0 <= source < n_tm:
                term = dw_ref[tap : tap + 1, :] * attended[source]
                depth = term if depth is None else depth + term
        hidden.append(jax.nn.gelu(depth).astype(BF16).astype(F32))
    hidden = jnp.concatenate(hidden, axis=0).astype(BF16)
    mixed = jnp.dot(hidden, pw_ref[...], preferred_element_type=F32)
    memory = None
    out = jnp.zeros(out_ref.shape, F32)
    out_sub = lax.broadcasted_iota(jnp.int32, out.shape, 0)
    n_out = ow_ref.shape[0]
    for frame in range(n_tm):
        refined = attended[frame] + mixed[frame * group : (frame + 1) * group]
        fresh = (1.0 - decays[frame]) * refined
        memory = fresh if memory is None else decays[frame] * memory + fresh
        padded = memory
        if group < LANES:
            padded = jnp.concatenate([memory, jnp.zeros((LANES - group, LANES), F32)], axis=0)
        delta = lax.dot_general(
            ow_ref[...], padded, NT, preferred_element_type=F32, precision=lax.Precision.HIGHEST
        )
        for axis in range(n_out):
            line = positions[frame][axis] + delta[axis : axis + 1]
            out = jnp.where(out_sub == frame * n_out + axis, line, out)
    out_ref[...] = out


def call(kernel, out_shape, n_in, **cost):
    vmem = pl.BlockSpec(memory_space=pltpu.VMEM)
    return pl.pallas_call(
        kernel,
        out_shape=out_shape,
        in_specs=[vmem] * n_in,
        out_specs=jax.tree.map(lambda _: vmem, out_shape),
        compiler_params=pltpu.CompilerParams(vmem_limit_bytes=VMEM_LIMIT),
        cost_estimate=pl.CostEstimate(**cost),
    )


def hot_rows(target, map_ref, base, chunk):
    rows = target.shape[0]
    lane = lax.broadcasted_iota(jnp.int32, (rows, LANES), 1)
    parts = []
    for lane_base in range(base, base + chunk, LANES):
        parts.append(jnp.where(lane + lane_base == target, 1.0, 0.0).astype(BF16))
    hot = jnp.concatenate(parts, axis=1)
    return jnp.dot(hot, map_ref[base : base + chunk, :], preferred_element_type=F32)


def store_by_partner(picked, scratch_ref, out_ref):
    n_space = lax.axis_size("space")
    space = lax.axis_index("space")
    group = picked.shape[0] // n_space
    scratch_ref[...] = picked
    for k in range(n_space):
        start = pl.multiple_of((space ^ k) * group, group)
        out_ref[k * group : (k + 1) * group, :] = scratch_ref[pl.ds(start, group), :].astype(BF16)


def pick_send_kernel(
    rows_here,
    map_width,
    frame_hbm,
    row_hbm,
    col_hbm,
    map_hbm,
    send_ref,
    target_ref,
    map_ref,
    index_ref,
    scratch_ref,
    index_sem,
    map_sem,
):
    index_copies = []
    for i, ref in enumerate((frame_hbm, row_hbm, col_hbm)):
        copy = pltpu.make_async_copy(ref, index_ref.at[i], index_sem.at[i])
        copy.start()
        index_copies.append(copy)
    positions = map_ref.shape[0]
    chunk = pick_chunk(positions, 1536)
    map_copies = []
    for i in range(positions // chunk):
        window = pl.ds(i * chunk, chunk)
        copy = pltpu.make_async_copy(map_hbm.at[window], map_ref.at[window], map_sem.at[i])
        copy.start()
        map_copies.append(copy)
    for copy in index_copies:
        copy.wait()
    tm = lax.axis_index("tm")
    row = index_ref[1] - lax.axis_index("space") * rows_here
    here = (index_ref[0] == tm) & (row >= 0) & (row < rows_here)
    target = jnp.where(here, row * map_width + index_ref[2], -1)
    half = target.shape[1] // 2
    first, second = target[:, :half], target[:, half:]
    target_ref[...] = jnp.where(tm == 0, first, second)
    target = jnp.where(tm == 0, second, first)
    target = jnp.transpose(jnp.broadcast_to(target, (LANES, half)))
    picked = None
    for i, copy in enumerate(map_copies):
        copy.wait()
        term = hot_rows(target, map_ref, i * chunk, chunk)
        picked = term if picked is None else picked + term
    store_by_partner(picked, scratch_ref, send_ref)


def pick_keep_kernel(target_ref, map_ref, keep_ref, scratch_ref):
    half = target_ref.shape[1]
    positions = map_ref.shape[0]
    chunk = pick_chunk(positions, 1536)
    target = jnp.transpose(jnp.broadcast_to(target_ref[...], (LANES, half)))
    picked = None
    for base in range(0, positions, chunk):
        term = hot_rows(target, map_ref, base, chunk)
        picked = term if picked is None else picked + term
    store_by_partner(picked, scratch_ref, keep_ref)


def coord_kernel(map_width, after_ref, out_ref):
    positions = out_ref.shape[0]
    chunk = pick_chunk(positions, 512)
    lane = lax.broadcasted_iota(jnp.int32, (chunk, LANES), 1)
    local_place = lax.broadcasted_iota(jnp.int32, (chunk, LANES), 0).astype(F32)

    @pl.loop(0, positions // chunk)
    def _(step):
        place = local_place + (step * chunk).astype(F32)
        row = jnp.floor((place + 0.5) * (1.0 / map_width))
        rest = jnp.where(lane == 2, 1.0, 0.0)
        value = jnp.where(lane == 0, place - row * map_width, jnp.where(lane == 1, row, rest))
        out_ref[pl.ds(pl.multiple_of(step * chunk, chunk), chunk), :] = value.astype(BF16)


def half_kernel(n_space, rows_here, height, width, *refs):
    query_refs, (map_ref, coord_ref, decay_ref) = refs[:n_space], refs[n_space : n_space + 3]
    out_refs = refs[n_space + 3 :]
    positions, channels = map_ref.shape
    factor = math.log2(math.e) / math.sqrt(channels)
    group = query_refs[0].shape[0]
    query = jnp.concatenate([ref[...] for ref in query_refs], axis=0)
    first_row = (lax.axis_index("space") * rows_here).astype(F32)
    chunk = pick_chunk(positions, 1280)

    def score(base):
        keys = map_ref[base : base + chunk, :]
        return lax.dot_general(query, keys, NT, preferred_element_type=F32)

    top = sums = None
    ahead = score(0)
    for base in range(0, positions, chunk):
        scores = ahead
        if base + chunk < positions:
            ahead = score(base + chunk)
        window = slice(base, base + chunk)
        values = jnp.concatenate([map_ref[window, :], coord_ref[window, :]], axis=1)
        new_top = jnp.max(scores, axis=1, keepdims=True) * factor
        if top is not None:
            new_top = jnp.maximum(new_top, top)
        weights = jnp.exp2(scores * factor - new_top).astype(BF16)
        terms = jnp.dot(weights, values, preferred_element_type=F32)
        sums = terms if sums is None else terms + jnp.exp2(top - new_top) * sums
        top = new_top
    feats = sums[:, :channels] / sums[:, channels + 2 : channels + 3]
    extra = sums[:, channels:]
    lane = lax.broadcasted_iota(jnp.int32, extra.shape, 1)
    extra = jnp.transpose(jnp.where(lane == 3, top, extra))
    total = extra[2:3]
    across = extra[0:1] / total / width
    down = (extra[1:2] / total + first_row) / height
    aux = jnp.zeros((AUX_ROWS, extra.shape[1]), F32)
    sub = lax.broadcasted_iota(jnp.int32, aux.shape, 0)
    for index, values in enumerate([extra[3:4], total, across, down]):
        aux = jnp.where(sub == index, values, aux)
    sub = lax.broadcasted_iota(jnp.int32, (AUX_ROWS, LANES), 0)
    for index, out_ref in enumerate(out_refs):
        shift = (aux.shape[1] - index * group) % aux.shape[1]
        block = pltpu.roll(aux, shift, 1) if shift else aux
        out_ref[:group, :] = feats[index * group : (index + 1) * group]
        out_ref[group:, :] = jnp.where(sub == 4, decay_ref[...], block[:, :LANES])


def merge(blocks, group):
    aux = [block[group:] for block in blocks]
    top = aux[0][0:1]
    for block in aux[1:]:
        top = jnp.maximum(top, block[0:1])
    weight = [jnp.exp2(b[0:1] - top) * b[1:2] for b in aux]
    total = sum(weight[1:], weight[0])
    share = [w / total for w in weight]
    across = [s * b[2:3] for s, b in zip(share, aux)]
    down = [s * b[3:4] for s, b in zip(share, aux)]
    across, down = sum(across[1:], across[0]), sum(down[1:], down[0])
    table = jnp.zeros((8, LANES), F32)
    sub = lax.broadcasted_iota(jnp.int32, table.shape, 0)
    for index, value in enumerate(share):
        table = jnp.where(sub == index, value, table)
    table = jnp.transpose(table)
    attended = None
    for index, block in enumerate(blocks):
        term = table[:group, index : index + 1] * block[:group]
        attended = term if attended is None else attended + term
    return across, down, attended.astype(BF16).astype(F32), aux[0][4:5]


def pair_tail_kernel(n_space, group, *refs):
    dw_ref, pw_ref, ow_ref = refs[:3]
    same = merge([ref[...].astype(F32) for ref in refs[3 : 3 + n_space]], group)
    other = merge([ref[...].astype(F32) for ref in refs[3 + n_space : 3 + 2 * n_space]], group)
    same_ref, other_ref = refs[3 + 2 * n_space :]
    early = lax.axis_index("tm") == 0
    frames = [
        [jnp.where(early, a, b) for a, b in zip(same, other)],
        [jnp.where(early, b, a) for a, b in zip(same, other)],
    ]
    taps = dw_ref.shape[0]
    hidden = []
    for frame in range(2):
        depth = None
        for tap in range(taps):
            source = frame + tap - taps // 2
            if 0 <= source < 2:
                term = dw_ref[tap : tap + 1, :] * frames[source][2]
                depth = term if depth is None else depth + term
        hidden.append(jax.nn.gelu(depth).astype(BF16))
    hidden = jnp.concatenate(hidden, axis=0)
    mixed = jnp.dot(hidden, pw_ref[...], preferred_element_type=F32)
    memory = None
    lines = []
    for frame, (across, down, attended, decay) in enumerate(frames):
        refined = attended + mixed[frame * group : (frame + 1) * group]
        fresh = (1.0 - decay) * refined
        memory = fresh if memory is None else decay * memory + fresh
        padded = memory
        if group < LANES:
            padded = jnp.concatenate([memory, jnp.zeros((LANES - group, LANES), F32)], axis=0)
        delta = lax.dot_general(
            ow_ref[...], padded, NT, preferred_element_type=F32, precision=lax.Precision.HIGHEST
        )
        sub = lax.broadcasted_iota(jnp.int32, delta.shape, 0)
        lines.append(delta + jnp.where(sub == 0, across, down))
    same_ref[...] = jnp.where(early, lines[0], lines[1])
    other_ref[...] = jnp.where(early, lines[1], lines[0])


def lay_kernel(n_space, group, *refs):
    same = [ref[...] for ref in refs[:n_space]]
    other = [ref[...] for ref in refs[n_space : 2 * n_space]]
    out_ref = refs[2 * n_space]
    early = lax.axis_index("tm") == 0
    space = lax.axis_index("space")
    lines = [jnp.where(early, a, b) for a, b in zip(same, other)]
    lines += [jnp.where(early, b, a) for a, b in zip(same, other)]
    bit = 1
    while bit < n_space:
        turn = (space & bit) != 0
        lines = [jnp.where(turn, lines[i ^ bit], lines[i]) for i in range(2 * n_space)]
        bit *= 2
    per_tile = LANES // group
    lane = lax.broadcasted_iota(jnp.int32, lines[0].shape, 1)
    for tile in range(2 * n_space // per_tile):
        value = lines[tile * per_tile]
        for index in range(1, per_tile):
            moved = pltpu.roll(lines[tile * per_tile + index], index * group, 1)
            value = jnp.where(lane >= index * group, moved, value)
        out_ref[0, :, tile * LANES : (tile + 1) * LANES] = value


def swap(value, axis, bit):
    return lax.ppermute(value, axis, [(i, i ^ bit) for i in range(lax.axis_size(axis))])


def all_sum(value, axis):
    count = lax.axis_size(axis)
    if count & (count - 1):
        return lax.psum(value, axis)
    bit = 1
    while bit < count:
        value = value + swap(value, axis, bit)
        bit *= 2
    return value


def local_general(
    feature_maps, query_frame, query_row, query_col, ema_decay, dw_kernel, pw_weight, out_weight
):
    frames_here, rows_here, map_width, channels = feature_maps.shape
    assert frames_here == 1 and channels == LANES
    queries = query_frame.shape[0]
    n_tm, n_space = lax.axis_size("tm"), lax.axis_size("space")
    n_groups = n_tm * n_space
    group = queries // n_groups
    height = rows_here * n_space
    positions = rows_here * map_width
    maps = feature_maps.reshape(positions, channels)
    halves = 2 if n_tm == 2 else 1
    part = jax.ShapeDtypeStruct((queries // halves, channels), BF16)

    picked = call(
        functools.partial(gather_kernel, rows_here, map_width),
        [part] * halves,
        4,
        flops=2 * queries * positions * channels,
        bytes_accessed=2 * positions * channels,
        transcendentals=0,
    )(query_frame[None], query_row[None], query_col[None], maps)

    place = jnp.arange(positions, dtype=jnp.int32)[:, None]
    lane = jnp.arange(LANES, dtype=jnp.int32)[None, :]
    coords = jnp.where(
        lane == 0,
        place % map_width,
        jnp.where(lane == 1, place // map_width, jnp.where(lane == 2, 1, 0)),
    ).astype(BF16)

    if halves == 2:
        mine = picked[0] + swap(picked[1], "tm", 1)
        mine = all_sum(mine, "space")
        feats = [mine, swap(mine, "tm", 1)]
    else:
        feats = [all_sum(all_sum(picked[0], "tm"), "space")]

    feat_rows = -(-group // 8) * 8
    blocks = call(
        functools.partial(volume_kernel, n_groups, rows_here, height, map_width),
        jax.ShapeDtypeStruct((n_groups, feat_rows + AUX_ROWS, LANES), F32),
        halves + 3,
        flops=6 * queries * positions * channels,
        bytes_accessed=4 * positions * channels,
        transcendentals=queries * positions,
    )(*feats, maps, coords, ema_decay)

    blocks = lax.all_to_all(blocks, ("tm", "space"), 0, 0, tiled=True)

    n_out = out_weight.shape[0]
    out_rows = -(-n_tm * n_out // 8) * 8
    lines = call(
        functools.partial(tail_kernel, n_tm, n_space, group),
        jax.ShapeDtypeStruct((out_rows, LANES), F32),
        4,
        flops=2 * n_tm * group * channels * channels,
        bytes_accessed=4 * n_groups * (feat_rows + AUX_ROWS) * LANES,
        transcendentals=n_tm * group * channels,
    )(dw_kernel, pw_weight, out_weight, blocks)

    lines = lax.all_gather(lines, ("tm", "space"), axis=0)
    own = lax.dynamic_slice_in_dim(lines, lax.axis_index("tm") * n_out, n_out, axis=1)
    own = own[:, :, :group]
    return jnp.transpose(own, (1, 0, 2)).reshape(1, n_out, queries)


def partner(value, flip, bits):
    n_space = lax.axis_size("space")
    pairs = []
    for tm in range(2):
        for space in range(n_space):
            pairs.append((tm * n_space + space, (tm ^ flip) * n_space + (space ^ bits)))
    return lax.ppermute(value, ("tm", "space"), pairs)


def local_pair(
    feature_maps, query_frame, query_row, query_col, ema_decay, dw_kernel, pw_weight, out_weight
):
    _, rows_here, map_width, channels = feature_maps.shape
    queries = query_frame.shape[0]
    n_space = lax.axis_size("space")
    half = queries // 2
    group = half // n_space
    height = rows_here * n_space
    positions = rows_here * map_width
    maps = feature_maps.reshape(positions, channels)
    vmem = pl.BlockSpec(memory_space=pltpu.VMEM)
    hbm = pl.BlockSpec(memory_space=pltpu.HBM)
    params = pltpu.CompilerParams(vmem_limit_bytes=VMEM_LIMIT)
    n_chunks = positions // pick_chunk(positions, 1536)

    half_shape = jax.ShapeDtypeStruct((half, channels), BF16)
    send, target, maps_near = pl.pallas_call(
        functools.partial(pick_send_kernel, rows_here, map_width),
        out_shape=[
            half_shape,
            jax.ShapeDtypeStruct((1, half), jnp.int32),
            jax.ShapeDtypeStruct(maps.shape, BF16),
        ],
        in_specs=[hbm] * 4,
        out_specs=[vmem] * 3,
        scratch_shapes=[
            pltpu.VMEM((3, 1, queries), jnp.int32),
            pltpu.VMEM((half, channels), F32),
            pltpu.SemaphoreType.DMA((3,)),
            pltpu.SemaphoreType.DMA((n_chunks,)),
        ],
        compiler_params=params,
        cost_estimate=pl.CostEstimate(
            flops=queries * positions * channels,
            bytes_accessed=4 * positions * channels,
            transcendentals=0,
        ),
    )(query_frame[None], query_row[None], query_col[None], maps)
    arrived = partner(send, 1, 0)
    keep = pl.pallas_call(
        pick_keep_kernel,
        out_shape=half_shape,
        in_specs=[vmem] * 2,
        out_specs=vmem,
        scratch_shapes=[pltpu.VMEM((half, channels), F32)],
        compiler_params=params,
        cost_estimate=pl.CostEstimate(
            flops=queries * positions * channels,
            bytes_accessed=2 * positions * channels,
            transcendentals=0,
        ),
    )(target, maps_near)
    coords = call(
        functools.partial(coord_kernel, map_width),
        jax.ShapeDtypeStruct((positions, LANES), BF16),
        1,
        flops=8 * positions * LANES,
        bytes_accessed=2 * positions * LANES,
        transcendentals=0,
    )(target)

    def piece(k):
        window = slice(k * group, (k + 1) * group)
        return keep[window] + arrived[window]

    own = piece(0)
    shares = [partner(piece(k), 0, k) for k in range(1, n_space)]
    for share in shares:
        own = own + share
    mine = [own] + [partner(own, 0, k) for k in range(1, n_space)]
    theirs = [partner(value, 1, 0) for value in mine]

    def blocks_of(feats):
        shape = jax.ShapeDtypeStruct((group + AUX_ROWS, LANES), F32)
        return call(
            functools.partial(half_kernel, n_space, rows_here, height, map_width),
            [shape] * n_space,
            n_space + 3,
            flops=3 * queries * positions * channels,
            bytes_accessed=4 * positions * channels,
            transcendentals=half * positions,
        )(*feats, maps_near, coords, ema_decay)

    near = blocks_of(mine)
    near = [near[0]] + [partner(near[k], 0, k) for k in range(1, n_space)]
    far = blocks_of(theirs)
    far = [partner(far[k], 1, k) for k in range(n_space)]

    n_out = out_weight.shape[0]
    line = jax.ShapeDtypeStruct((n_out, LANES), F32)
    same, other = call(
        functools.partial(pair_tail_kernel, n_space, group),
        [line, line],
        3 + 2 * n_space,
        flops=8 * group * channels * channels,
        bytes_accessed=8 * n_space * (group + AUX_ROWS) * LANES,
        transcendentals=2 * group * channels,
    )(dw_kernel, pw_weight, out_weight, *near, *far)
    lines = [same] + [partner(same, 0, k) for k in range(1, n_space)]
    lines += [partner(other, 1, k) for k in range(n_space)]
    return call(
        functools.partial(lay_kernel, n_space, group),
        jax.ShapeDtypeStruct((1, n_out, queries), F32),
        2 * n_space,
        flops=n_out * queries,
        bytes_accessed=8 * n_out * queries,
        transcendentals=0,
    )(*lines)


def local(feature_maps, query_frame, *rest):
    n_tm, n_space = lax.axis_size("tm"), lax.axis_size("space")
    group = query_frame.shape[0] // (n_tm * n_space)
    paired = n_tm == 2 and n_space & (n_space - 1) == 0 and n_space <= 8
    if paired and group % 16 == 0 and LANES % group == 0:
        return local_pair(feature_maps, query_frame, *rest)
    return local_general(feature_maps, query_frame, *rest)


def solution(mesh):
    placed = (
        P(("video", "tm"), "space", None, None),
        P("video"),
        P("video"),
        P("video"),
        P(("video", "tm"), None),
        P(),
        P(),
        P(),
    )
    return jax.shard_map(
        local, mesh=mesh, in_specs=placed, out_specs=P(("video", "tm"), None, None), check_vma=False
    )
```

```python
import functools
import math

import jax
import jax.numpy as jnp
from jax import lax
from jax.experimental import pallas as pl
from jax.experimental.pallas import tpu as pltpu
from jax.sharding import PartitionSpec as P

F32 = jnp.float32
BF16 = jnp.bfloat16
LANES = 128
AUX_ROWS = 8
PIECE_ROWS = 16
VMEM_LIMIT = 40 * 1024 * 1024
NT = (((1,), (1,)), ((), ()))


def pick_chunk(total, limit):
    best = None
    for size in range(LANES, limit + 1, LANES):
        if total % size == 0 and (best is None or size % 256 == 0 or best % 256):
            best = size
    return best if best is not None else total


def gather_kernel(rows_here, map_width, frame_ref, row_ref, col_ref, map_ref, *out_refs):
    positions = map_ref.shape[0]
    queries = frame_ref.shape[1]
    tm = lax.axis_index("tm")
    row = row_ref[...] - lax.axis_index("space") * rows_here
    here = (frame_ref[...] == tm) & (row >= 0) & (row < rows_here)
    target = jnp.where(here, row * map_width + col_ref[...], -1)
    target = jnp.transpose(jnp.broadcast_to(target, (LANES, queries)))
    chunk = pick_chunk(positions, 1536)
    picked = None
    for base in range(0, positions, chunk):
        parts = []
        for lane_base in range(base, base + chunk, LANES):
            lane = lax.broadcasted_iota(jnp.int32, (queries, LANES), 1) + lane_base
            parts.append(jnp.where(lane == target, 1.0, 0.0).astype(BF16))
        hot = jnp.concatenate(parts, axis=1)
        term = jnp.dot(hot, map_ref[base : base + chunk, :], preferred_element_type=F32)
        picked = term if picked is None else picked + term
    if len(out_refs) == 1:
        out_refs[0][...] = picked.astype(BF16)
        return
    half = queries // 2
    first, second = picked[:half].astype(F32), picked[half:].astype(F32)
    out_refs[0][...] = jnp.where(tm == 0, first, second).astype(BF16)
    out_refs[1][...] = jnp.where(tm == 0, second, first).astype(BF16)


def volume_kernel(n_groups, rows_here, height, width, *refs):
    *query_refs, map_ref, coord_ref, decay_ref, out_ref = refs
    positions, channels = map_ref.shape
    factor = math.log2(math.e) / math.sqrt(channels)
    part_queries = query_refs[0].shape[0]
    n_parts = len(query_refs)
    group = part_queries * n_parts // n_groups
    feat_rows = out_ref.shape[1] - AUX_ROWS
    first_row = (lax.axis_index("space") * rows_here).astype(F32)
    tm = lax.axis_index("tm")
    chunk = pick_chunk(positions, 1280)
    state = [None] * n_parts
    for base in range(0, positions, chunk):
        keys = map_ref[base : base + chunk, :]
        values = jnp.concatenate([keys, coord_ref[base : base + chunk, :]], axis=1)
        for part in range(n_parts):
            scores = lax.dot_general(
                query_refs[part][...], keys, NT, preferred_element_type=F32
            )
            top = jnp.max(scores, axis=1, keepdims=True) * factor
            if state[part] is not None:
                old_top, old_sum = state[part]
                top = jnp.maximum(top, old_top)
            weights = jnp.exp2(scores * factor - top).astype(BF16)
            sums = jnp.dot(weights, values, preferred_element_type=F32)
            if state[part] is not None:
                sums = sums + jnp.exp2(old_top - top) * old_sum
            state[part] = (top, sums)
    decay = [decay_ref[...]]
    sub = lax.broadcasted_iota(jnp.int32, (AUX_ROWS, LANES), 0)
    for part in range(n_parts):
        top, sums = state[part]
        feats = sums[:, :channels] / sums[:, channels + 2 : channels + 3]
        extra = sums[:, channels:]
        lane = lax.broadcasted_iota(jnp.int32, extra.shape, 1)
        extra = jnp.transpose(jnp.where(lane == 3, top, extra))
        total = extra[2:3]
        rows = [extra[3:4]]
        rows += [total, extra[0:1] / total / width, (extra[1:2] / total + first_row) / height]
        aux = jnp.zeros((AUX_ROWS, part_queries), F32)
        wide = lax.broadcasted_iota(jnp.int32, aux.shape, 0)
        for index, values in enumerate(rows):
            aux = jnp.where(wide == index, values, aux)
        where = part if n_parts == 1 else jnp.where(tm == 0, part, 1 - part)
        groups_here = n_groups // n_parts
        for index in range(groups_here):
            shift = (part_queries - index * group) % part_queries
            block = pltpu.roll(aux, shift, 1) if shift else aux
            block = block[:, :LANES]
            for offset, piece in enumerate(decay):
                block = jnp.where(sub == len(rows) + offset, piece, block)
            pieces = [feats[index * group : (index + 1) * group]]
            if feat_rows > group:
                pieces.append(jnp.zeros((feat_rows - group, LANES), F32))
            pieces.append(block)
            out_ref[where * groups_here + index] = jnp.concatenate(pieces, axis=0).astype(
                out_ref.dtype
            )


def tail_kernel(n_tm, n_space, group, dw_ref, pw_ref, ow_ref, in_ref, out_ref):
    feat_rows = in_ref.shape[1] - AUX_ROWS
    n_blocks = n_tm * n_space
    blocks = [in_ref[index].astype(F32) for index in range(n_blocks)]
    aux = [block[feat_rows:] for block in blocks]
    positions, shares, decays = [], [], []
    for frame in range(n_tm):
        mine = aux[frame * n_space : (frame + 1) * n_space]
        top = mine[0][0:1]
        for block in mine[1:]:
            top = jnp.maximum(top, block[0:1])
        weight = [jnp.exp2(b[0:1] - top) * b[1:2] for b in mine]
        total = sum(weight[1:], weight[0])
        share = [w / total for w in weight]
        shares += share
        across = [s * b[2:3] for s, b in zip(share, mine)]
        down = [s * b[3:4] for s, b in zip(share, mine)]
        positions.append((sum(across[1:], across[0]), sum(down[1:], down[0])))
        decays.append(mine[0][4:5])
    pad_blocks = -(-n_blocks // 8) * 8
    table = jnp.zeros((pad_blocks, LANES), F32)
    sub = lax.broadcasted_iota(jnp.int32, table.shape, 0)
    for index, share in enumerate(shares):
        table = jnp.where(sub == index, share, table)
    table = jnp.transpose(table)
    attended = []
    for frame in range(n_tm):
        value = None
        for index in range(frame * n_space, (frame + 1) * n_space):
            term = table[:group, index : index + 1] * blocks[index][:group]
            value = term if value is None else value + term
        attended.append(value.astype(BF16).astype(F32))
    taps = dw_ref.shape[0]
    hidden = []
    for frame in range(n_tm):
        depth = None
        for tap in range(taps):
            source = frame + tap - taps // 2
            if 0 <= source < n_tm:
                term = dw_ref[tap : tap + 1, :] * attended[source]
                depth = term if depth is None else depth + term
        hidden.append(jax.nn.gelu(depth).astype(BF16).astype(F32))
    hidden = jnp.concatenate(hidden, axis=0).astype(BF16)
    mixed = jnp.dot(hidden, pw_ref[...], preferred_element_type=F32)
    memory = None
    out = jnp.zeros(out_ref.shape, F32)
    out_sub = lax.broadcasted_iota(jnp.int32, out.shape, 0)
    n_out = ow_ref.shape[0]
    for frame in range(n_tm):
        refined = attended[frame] + mixed[frame * group : (frame + 1) * group]
        fresh = (1.0 - decays[frame]) * refined
        memory = fresh if memory is None else decays[frame] * memory + fresh
        padded = memory
        if group < LANES:
            padded = jnp.concatenate([memory, jnp.zeros((LANES - group, LANES), F32)], axis=0)
        delta = lax.dot_general(
            ow_ref[...], padded, NT, preferred_element_type=F32, precision=lax.Precision.HIGHEST
        )
        for axis in range(n_out):
            line = positions[frame][axis] + delta[axis : axis + 1]
            out = jnp.where(out_sub == frame * n_out + axis, line, out)
    out_ref[...] = out


def call(kernel, out_shape, n_in, **cost):
    vmem = pl.BlockSpec(memory_space=pltpu.VMEM)
    return pl.pallas_call(
        kernel,
        out_shape=out_shape,
        in_specs=[vmem] * n_in,
        out_specs=jax.tree.map(lambda _: vmem, out_shape),
        compiler_params=pltpu.CompilerParams(vmem_limit_bytes=VMEM_LIMIT),
        cost_estimate=pl.CostEstimate(**cost),
    )


def hot_rows(target, map_ref, base, chunk):
    rows = target.shape[0]
    lane = lax.broadcasted_iota(jnp.int32, (rows, LANES), 1)
    parts = []
    for lane_base in range(base, base + chunk, LANES):
        parts.append(jnp.where(lane + lane_base == target, 1.0, 0.0).astype(BF16))
    hot = jnp.concatenate(parts, axis=1)
    return jnp.dot(hot, map_ref[base : base + chunk, :], preferred_element_type=F32)


def pick_kernel(core_flip, target_ref, map_ref, out_ref):
    half = target_ref.shape[1] // 2
    positions = map_ref.shape[0]
    chunk = pick_chunk(positions, 1536)
    second = lax.axis_index("tm") != core_flip
    target = jnp.where(second, target_ref[:, half:], target_ref[:, :half])
    target = jnp.transpose(jnp.broadcast_to(target, (LANES, half)))
    picked = None
    for base in range(0, positions, chunk):
        term = hot_rows(target, map_ref, base, chunk)
        picked = term if picked is None else picked + term
    out_ref[...] = picked.astype(BF16)


def coord_kernel(map_width, after_ref, out_ref):
    positions = out_ref.shape[0]
    chunk = pick_chunk(positions, 512)
    lane = lax.broadcasted_iota(jnp.int32, (chunk, LANES), 1)
    local_place = lax.broadcasted_iota(jnp.int32, (chunk, LANES), 0).astype(F32)

    @pl.loop(0, positions // chunk)
    def _(step):
        place = local_place + (step * chunk).astype(F32)
        row = jnp.floor((place + 0.5) * (1.0 / map_width))
        rest = jnp.where(lane == 2, 1.0, 0.0)
        value = jnp.where(lane == 0, place - row * map_width, jnp.where(lane == 1, row, rest))
        out_ref[pl.ds(pl.multiple_of(step * chunk, chunk), chunk), :] = value.astype(BF16)


def split(value):
    pieces = []
    for _ in range(3):
        piece = value.astype(BF16).astype(F32)
        pieces.append(piece)
        value = value - piece
    return pieces


def by_partner(values, n_space):
    space = lax.axis_index("space")
    bit = 1
    while bit < n_space:
        turn = (space & bit) != 0
        values = [jnp.where(turn, values[i ^ bit], values[i]) for i in range(len(values))]
        bit *= 2
    return values


def half_kernel(n_space, rows_here, height, width, query_ref, map_ref, coord_ref, *out_refs):
    positions, channels = map_ref.shape
    factor = math.log2(math.e) / math.sqrt(channels)
    query = query_ref[...]
    group = query.shape[0] // n_space
    first_row = (lax.axis_index("space") * rows_here).astype(F32)
    chunk = pick_chunk(positions, 1280)

    def score(base):
        keys = map_ref[base : base + chunk, :]
        return lax.dot_general(query, keys, NT, preferred_element_type=F32)

    top = sums = None
    ahead = score(0)
    for base in range(0, positions, chunk):
        scores = ahead
        if base + chunk < positions:
            ahead = score(base + chunk)
        window = slice(base, base + chunk)
        values = jnp.concatenate([map_ref[window, :], coord_ref[window, :]], axis=1)
        new_top = jnp.max(scores, axis=1, keepdims=True) * factor
        if top is not None:
            new_top = jnp.maximum(new_top, top)
        weights = jnp.exp2(scores * factor - new_top).astype(BF16)
        terms = jnp.dot(weights, values, preferred_element_type=F32)
        sums = terms if sums is None else terms + jnp.exp2(top - new_top) * sums
        top = new_top
    feats = sums[:, :channels] / sums[:, channels + 2 : channels + 3]
    extra = sums[:, channels:]
    lane = lax.broadcasted_iota(jnp.int32, extra.shape, 1)
    extra = jnp.transpose(jnp.where(lane == 3, top, extra))
    total = extra[2:3]
    across = extra[0:1] / total / width
    down = (extra[1:2] / total + first_row) / height
    rows = [piece for value in (extra[3:4], total, across, down) for piece in split(value)]
    aux = jnp.zeros((PIECE_ROWS, extra.shape[1]), F32)
    sub = lax.broadcasted_iota(jnp.int32, aux.shape, 0)
    for index, values in enumerate(rows):
        aux = jnp.where(sub == index, values, aux)
    blocks = []
    for index in range(n_space):
        shift = (aux.shape[1] - index * group) % aux.shape[1]
        block = pltpu.roll(aux, shift, 1) if shift else aux
        blocks.append(
            jnp.concatenate([feats[index * group : (index + 1) * group], block[:, :LANES]], axis=0)
        )
    for out_ref, block in zip(out_refs, by_partner(blocks, n_space)):
        out_ref[...] = block


def merge(blocks, group):
    aux = [block[group:] for block in blocks]
    tops = [b[0:1] + b[1:2] + b[2:3] for b in aux]
    top = functools.reduce(jnp.maximum, tops)
    weight = [jnp.exp2(t - top) * (b[3:4] + b[4:5] + b[5:6]) for t, b in zip(tops, aux)]
    total = sum(weight[1:], weight[0])
    share = [w / total for w in weight]
    across = [s * (b[6:7] + b[7:8] + b[8:9]) for s, b in zip(share, aux)]
    down = [s * (b[9:10] + b[10:11] + b[11:12]) for s, b in zip(share, aux)]
    across, down = sum(across[1:], across[0]), sum(down[1:], down[0])
    table = jnp.zeros((8, LANES), F32)
    sub = lax.broadcasted_iota(jnp.int32, table.shape, 0)
    for index, value in enumerate(share):
        table = jnp.where(sub == index, value, table)
    table = jnp.transpose(table)
    attended = None
    for index, block in enumerate(blocks):
        term = table[:group, index : index + 1] * block[:group]
        attended = term if attended is None else attended + term
    return across, down, attended.astype(BF16).astype(F32)


def merge_kernel(group, decay_ref, *refs):
    block_refs, (out_ref, place_ref) = refs[:-2], refs[-2:]
    blocks = [ref[...] for ref in block_refs]
    size = group + PIECE_ROWS
    near = merge([block[:size] for block in blocks], group)
    far = merge([block[size:] for block in blocks], group)
    out_ref[:group, :] = near[2]
    out_ref[group : 2 * group, :] = far[2]
    out_ref[2 * group :, :] = jnp.broadcast_to(decay_ref[...], (8, LANES))
    lane = lax.broadcasted_iota(jnp.int32, (1, LANES), 1)
    for index in range(2):
        moved = pltpu.roll(jnp.broadcast_to(far[index], (8, LANES)), group, 1)[0:1]
        place_ref[index : index + 1, :] = jnp.where(lane < group, near[index], moved)


def track_kernel(group, dw_ref, pw_ref, ow_ref, place_ref, mine_ref, theirs_ref, out_ref):
    early = lax.axis_index("tm") == 0
    mine = mine_ref[: 2 * group]
    theirs = jnp.concatenate([theirs_ref[group : 2 * group], theirs_ref[:group]], axis=0)
    attended = [jnp.where(early, mine, theirs), jnp.where(early, theirs, mine)]
    decay_mine, decay_theirs = mine_ref[2 * group : 2 * group + 1], theirs_ref[2 * group : 2 * group + 1]
    decay = [
        jnp.where(early, decay_mine, decay_theirs),
        jnp.where(early, decay_theirs, decay_mine),
    ]
    taps = dw_ref.shape[0]
    hidden = []
    for frame in range(2):
        depth = None
        for tap in range(taps):
            source = frame + tap - taps // 2
            if 0 <= source < 2:
                term = dw_ref[tap : tap + 1, :] * attended[source]
                depth = term if depth is None else depth + term
        hidden.append(jax.nn.gelu(depth).astype(BF16))
    hidden = jnp.concatenate(hidden, axis=0)
    mixed = jnp.dot(hidden, pw_ref[...], preferred_element_type=F32)
    first = (1.0 - decay[0]) * (attended[0] + mixed[: 2 * group])
    second = decay[1] * first + (1.0 - decay[1]) * (attended[1] + mixed[2 * group :])
    memory = jnp.where(early, first, second)
    delta = lax.dot_general(
        ow_ref[...], memory, NT, preferred_element_type=F32, precision=lax.Precision.HIGHEST
    )
    out_ref[...] = place_ref[...] + delta


def lay_kernel(n_space, group, *refs):
    out_ref = refs[n_space]
    lines = by_partner([ref[...] for ref in refs[:n_space]], n_space)
    early = lax.axis_index("tm") == 0
    swapped = [pltpu.roll(line, group, 1) for line in lines]
    halves = [jnp.where(early, a, b) for a, b in zip(lines, swapped)]
    halves += [jnp.where(early, b, a) for a, b in zip(lines, swapped)]
    lane = lax.broadcasted_iota(jnp.int32, lines[0].shape, 1)
    for tile in range(n_space):
        low, high = halves[2 * tile], pltpu.roll(halves[2 * tile + 1], group, 1)
        out_ref[0, :, tile * LANES : (tile + 1) * LANES] = jnp.where(lane < group, low, high)


def swap(value, axis, bit):
    return lax.ppermute(value, axis, [(i, i ^ bit) for i in range(lax.axis_size(axis))])


def all_sum(value, axis):
    count = lax.axis_size(axis)
    if count & (count - 1):
        return lax.psum(value, axis)
    bit = 1
    while bit < count:
        value = value + swap(value, axis, bit)
        bit *= 2
    return value


def local_general(
    feature_maps, query_frame, query_row, query_col, ema_decay, dw_kernel, pw_weight, out_weight
):
    frames_here, rows_here, map_width, channels = feature_maps.shape
    assert frames_here == 1 and channels == LANES
    queries = query_frame.shape[0]
    n_tm, n_space = lax.axis_size("tm"), lax.axis_size("space")
    n_groups = n_tm * n_space
    group = queries // n_groups
    height = rows_here * n_space
    positions = rows_here * map_width
    maps = feature_maps.reshape(positions, channels)
    halves = 2 if n_tm == 2 else 1
    part = jax.ShapeDtypeStruct((queries // halves, channels), BF16)

    picked = call(
        functools.partial(gather_kernel, rows_here, map_width),
        [part] * halves,
        4,
        flops=2 * queries * positions * channels,
        bytes_accessed=2 * positions * channels,
        transcendentals=0,
    )(query_frame[None], query_row[None], query_col[None], maps)

    place = jnp.arange(positions, dtype=jnp.int32)[:, None]
    lane = jnp.arange(LANES, dtype=jnp.int32)[None, :]
    coords = jnp.where(
        lane == 0,
        place % map_width,
        jnp.where(lane == 1, place // map_width, jnp.where(lane == 2, 1, 0)),
    ).astype(BF16)

    if halves == 2:
        mine = picked[0] + swap(picked[1], "tm", 1)
        mine = all_sum(mine, "space")
        feats = [mine, swap(mine, "tm", 1)]
    else:
        feats = [all_sum(all_sum(picked[0], "tm"), "space")]

    feat_rows = -(-group // 8) * 8
    blocks = call(
        functools.partial(volume_kernel, n_groups, rows_here, height, map_width),
        jax.ShapeDtypeStruct((n_groups, feat_rows + AUX_ROWS, LANES), F32),
        halves + 3,
        flops=6 * queries * positions * channels,
        bytes_accessed=4 * positions * channels,
        transcendentals=queries * positions,
    )(*feats, maps, coords, ema_decay)

    blocks = lax.all_to_all(blocks, ("tm", "space"), 0, 0, tiled=True)

    n_out = out_weight.shape[0]
    out_rows = -(-n_tm * n_out // 8) * 8
    lines = call(
        functools.partial(tail_kernel, n_tm, n_space, group),
        jax.ShapeDtypeStruct((out_rows, LANES), F32),
        4,
        flops=2 * n_tm * group * channels * channels,
        bytes_accessed=4 * n_groups * (feat_rows + AUX_ROWS) * LANES,
        transcendentals=n_tm * group * channels,
    )(dw_kernel, pw_weight, out_weight, blocks)

    lines = lax.all_gather(lines, ("tm", "space"), axis=0)
    own = lax.dynamic_slice_in_dim(lines, lax.axis_index("tm") * n_out, n_out, axis=1)
    own = own[:, :, :group]
    return jnp.transpose(own, (1, 0, 2)).reshape(1, n_out, queries)


def partner(value, flip, bits):
    n_space = lax.axis_size("space")
    pairs = []
    for tm in range(2):
        for space in range(n_space):
            pairs.append((tm * n_space + space, (tm ^ flip) * n_space + (space ^ bits)))
    return lax.ppermute(value, ("tm", "space"), pairs)


def local_pair(
    feature_maps, query_frame, query_row, query_col, ema_decay, dw_kernel, pw_weight, out_weight
):
    _, rows_here, map_width, channels = feature_maps.shape
    queries = query_frame.shape[0]
    n_space = lax.axis_size("space")
    half = queries // 2
    group = half // n_space
    height = rows_here * n_space
    positions = rows_here * map_width
    maps = feature_maps.reshape(positions, channels)

    row = query_row - lax.axis_index("space") * rows_here
    here = (query_frame == lax.axis_index("tm")) & (row >= 0) & (row < rows_here)
    target = jnp.where(here, row * map_width + query_col, -1)[None]

    def pick(core_flip):
        return call(
            functools.partial(pick_kernel, core_flip),
            jax.ShapeDtypeStruct((half, channels), BF16),
            2,
            flops=queries * positions * channels,
            bytes_accessed=2 * positions * channels,
            transcendentals=0,
        )(target, maps)

    arrived = partner(pick(1), 1, 0)
    coords = call(
        functools.partial(coord_kernel, map_width),
        jax.ShapeDtypeStruct((positions, LANES), BF16),
        1,
        flops=8 * positions * LANES,
        bytes_accessed=2 * positions * LANES,
        transcendentals=0,
    )(target)
    mine = all_sum(pick(0) + arrived, "space")
    theirs = partner(mine, 1, 0)

    def blocks_of(feats):
        shape = jax.ShapeDtypeStruct((group + PIECE_ROWS, LANES), F32)
        return call(
            functools.partial(half_kernel, n_space, rows_here, height, map_width),
            [shape] * n_space,
            3,
            flops=3 * queries * positions * channels,
            bytes_accessed=4 * positions * channels,
            transcendentals=half * positions,
        )(feats, maps, coords)

    near, far = blocks_of(mine), blocks_of(theirs)
    blocks = [jnp.concatenate([a, b], axis=0) for a, b in zip(near, far)]
    for k in reversed(range(1, n_space)):
        blocks[k] = partner(blocks[k].astype(jnp.float16), 0, k).astype(F32)

    n_out = out_weight.shape[0]
    attended, place = call(
        functools.partial(merge_kernel, group),
        [
            jax.ShapeDtypeStruct((2 * group + 8, LANES), F32),
            jax.ShapeDtypeStruct((n_out, LANES), F32),
        ],
        1 + n_space,
        flops=4 * n_space * group * channels,
        bytes_accessed=8 * n_space * group * channels,
        transcendentals=0,
    )(ema_decay, *blocks)
    line = call(
        functools.partial(track_kernel, group),
        jax.ShapeDtypeStruct((n_out, LANES), F32),
        6,
        flops=16 * group * channels * channels,
        bytes_accessed=16 * group * channels,
        transcendentals=4 * group * channels,
    )(dw_kernel, pw_weight, out_weight, place, attended, partner(attended, 1, 0))
    lines = [line] + [partner(line, 0, k) for k in range(1, n_space)]
    return call(
        functools.partial(lay_kernel, n_space, group),
        jax.ShapeDtypeStruct((1, n_out, queries), F32),
        n_space,
        flops=n_out * queries,
        bytes_accessed=8 * n_out * queries,
        transcendentals=0,
    )(*lines)


def local(feature_maps, query_frame, *rest):
    n_tm, n_space = lax.axis_size("tm"), lax.axis_size("space")
    group = query_frame.shape[0] // (n_tm * n_space)
    paired = n_tm == 2 and n_space & (n_space - 1) == 0 and n_space <= 8
    if paired and 2 * group == LANES:
        return local_pair(feature_maps, query_frame, *rest)
    return local_general(feature_maps, query_frame, *rest)


def solution(mesh):
    placed = (
        P(("video", "tm"), "space", None, None),
        P("video"),
        P("video"),
        P("video"),
        P(("video", "tm"), None),
        P(),
        P(),
        P(),
    )
    return jax.shard_map(
        local, mesh=mesh, in_specs=placed, out_specs=P(("video", "tm"), None, None), check_vma=False
    )
```

```python
import functools
import math

import jax
import jax.numpy as jnp
from jax import lax
from jax.experimental import pallas as pl
from jax.experimental.pallas import tpu as pltpu
from jax.sharding import PartitionSpec as P

F32 = jnp.float32
BF16 = jnp.bfloat16
LANES = 128
AUX_ROWS = 8
PIECE_ROWS = 16
VMEM_LIMIT = 40 * 1024 * 1024
NT = (((1,), (1,)), ((), ()))


def pick_chunk(total, limit):
    best = None
    for size in range(LANES, limit + 1, LANES):
        if total % size == 0 and (best is None or size % 256 == 0 or best % 256):
            best = size
    return best if best is not None else total


def gather_kernel(rows_here, map_width, frame_ref, row_ref, col_ref, map_ref, *out_refs):
    positions = map_ref.shape[0]
    queries = frame_ref.shape[1]
    tm = lax.axis_index("tm")
    row = row_ref[...] - lax.axis_index("space") * rows_here
    here = (frame_ref[...] == tm) & (row >= 0) & (row < rows_here)
    target = jnp.where(here, row * map_width + col_ref[...], -1)
    target = jnp.transpose(jnp.broadcast_to(target, (LANES, queries)))
    chunk = pick_chunk(positions, 1536)
    picked = None
    for base in range(0, positions, chunk):
        parts = []
        for lane_base in range(base, base + chunk, LANES):
            lane = lax.broadcasted_iota(jnp.int32, (queries, LANES), 1) + lane_base
            parts.append(jnp.where(lane == target, 1.0, 0.0).astype(BF16))
        hot = jnp.concatenate(parts, axis=1)
        term = jnp.dot(hot, map_ref[base : base + chunk, :], preferred_element_type=F32)
        picked = term if picked is None else picked + term
    if len(out_refs) == 1:
        out_refs[0][...] = picked.astype(BF16)
        return
    half = queries // 2
    first, second = picked[:half].astype(F32), picked[half:].astype(F32)
    out_refs[0][...] = jnp.where(tm == 0, first, second).astype(BF16)
    out_refs[1][...] = jnp.where(tm == 0, second, first).astype(BF16)


def volume_kernel(n_groups, rows_here, height, width, *refs):
    *query_refs, map_ref, coord_ref, decay_ref, out_ref = refs
    positions, channels = map_ref.shape
    factor = math.log2(math.e) / math.sqrt(channels)
    part_queries = query_refs[0].shape[0]
    n_parts = len(query_refs)
    group = part_queries * n_parts // n_groups
    feat_rows = out_ref.shape[1] - AUX_ROWS
    first_row = (lax.axis_index("space") * rows_here).astype(F32)
    tm = lax.axis_index("tm")
    chunk = pick_chunk(positions, 1280)
    state = [None] * n_parts
    for base in range(0, positions, chunk):
        keys = map_ref[base : base + chunk, :]
        values = jnp.concatenate([keys, coord_ref[base : base + chunk, :]], axis=1)
        for part in range(n_parts):
            scores = lax.dot_general(
                query_refs[part][...], keys, NT, preferred_element_type=F32
            )
            top = jnp.max(scores, axis=1, keepdims=True) * factor
            if state[part] is not None:
                old_top, old_sum = state[part]
                top = jnp.maximum(top, old_top)
            weights = jnp.exp2(scores * factor - top).astype(BF16)
            sums = jnp.dot(weights, values, preferred_element_type=F32)
            if state[part] is not None:
                sums = sums + jnp.exp2(old_top - top) * old_sum
            state[part] = (top, sums)
    decay = [decay_ref[...]]
    sub = lax.broadcasted_iota(jnp.int32, (AUX_ROWS, LANES), 0)
    for part in range(n_parts):
        top, sums = state[part]
        feats = sums[:, :channels] / sums[:, channels + 2 : channels + 3]
        extra = sums[:, channels:]
        lane = lax.broadcasted_iota(jnp.int32, extra.shape, 1)
        extra = jnp.transpose(jnp.where(lane == 3, top, extra))
        total = extra[2:3]
        rows = [extra[3:4]]
        rows += [total, extra[0:1] / total / width, (extra[1:2] / total + first_row) / height]
        aux = jnp.zeros((AUX_ROWS, part_queries), F32)
        wide = lax.broadcasted_iota(jnp.int32, aux.shape, 0)
        for index, values in enumerate(rows):
            aux = jnp.where(wide == index, values, aux)
        where = part if n_parts == 1 else jnp.where(tm == 0, part, 1 - part)
        groups_here = n_groups // n_parts
        for index in range(groups_here):
            shift = (part_queries - index * group) % part_queries
            block = pltpu.roll(aux, shift, 1) if shift else aux
            block = block[:, :LANES]
            for offset, piece in enumerate(decay):
                block = jnp.where(sub == len(rows) + offset, piece, block)
            pieces = [feats[index * group : (index + 1) * group]]
            if feat_rows > group:
                pieces.append(jnp.zeros((feat_rows - group, LANES), F32))
            pieces.append(block)
            out_ref[where * groups_here + index] = jnp.concatenate(pieces, axis=0).astype(
                out_ref.dtype
            )


def tail_kernel(n_tm, n_space, group, dw_ref, pw_ref, ow_ref, in_ref, out_ref):
    feat_rows = in_ref.shape[1] - AUX_ROWS
    n_blocks = n_tm * n_space
    blocks = [in_ref[index].astype(F32) for index in range(n_blocks)]
    aux = [block[feat_rows:] for block in blocks]
    positions, shares, decays = [], [], []
    for frame in range(n_tm):
        mine = aux[frame * n_space : (frame + 1) * n_space]
        top = mine[0][0:1]
        for block in mine[1:]:
            top = jnp.maximum(top, block[0:1])
        weight = [jnp.exp2(b[0:1] - top) * b[1:2] for b in mine]
        total = sum(weight[1:], weight[0])
        share = [w / total for w in weight]
        shares += share
        across = [s * b[2:3] for s, b in zip(share, mine)]
        down = [s * b[3:4] for s, b in zip(share, mine)]
        positions.append((sum(across[1:], across[0]), sum(down[1:], down[0])))
        decays.append(mine[0][4:5])
    pad_blocks = -(-n_blocks // 8) * 8
    table = jnp.zeros((pad_blocks, LANES), F32)
    sub = lax.broadcasted_iota(jnp.int32, table.shape, 0)
    for index, share in enumerate(shares):
        table = jnp.where(sub == index, share, table)
    table = jnp.transpose(table)
    attended = []
    for frame in range(n_tm):
        value = None
        for index in range(frame * n_space, (frame + 1) * n_space):
            term = table[:group, index : index + 1] * blocks[index][:group]
            value = term if value is None else value + term
        attended.append(value.astype(BF16).astype(F32))
    taps = dw_ref.shape[0]
    hidden = []
    for frame in range(n_tm):
        depth = None
        for tap in range(taps):
            source = frame + tap - taps // 2
            if 0 <= source < n_tm:
                term = dw_ref[tap : tap + 1, :] * attended[source]
                depth = term if depth is None else depth + term
        hidden.append(jax.nn.gelu(depth).astype(BF16).astype(F32))
    hidden = jnp.concatenate(hidden, axis=0).astype(BF16)
    mixed = jnp.dot(hidden, pw_ref[...], preferred_element_type=F32)
    memory = None
    out = jnp.zeros(out_ref.shape, F32)
    out_sub = lax.broadcasted_iota(jnp.int32, out.shape, 0)
    n_out = ow_ref.shape[0]
    for frame in range(n_tm):
        refined = attended[frame] + mixed[frame * group : (frame + 1) * group]
        fresh = (1.0 - decays[frame]) * refined
        memory = fresh if memory is None else decays[frame] * memory + fresh
        padded = memory
        if group < LANES:
            padded = jnp.concatenate([memory, jnp.zeros((LANES - group, LANES), F32)], axis=0)
        delta = lax.dot_general(
            ow_ref[...], padded, NT, preferred_element_type=F32, precision=lax.Precision.HIGHEST
        )
        for axis in range(n_out):
            line = positions[frame][axis] + delta[axis : axis + 1]
            out = jnp.where(out_sub == frame * n_out + axis, line, out)
    out_ref[...] = out


def call(kernel, out_shape, n_in, **cost):
    vmem = pl.BlockSpec(memory_space=pltpu.VMEM)
    return pl.pallas_call(
        kernel,
        out_shape=out_shape,
        in_specs=[vmem] * n_in,
        out_specs=jax.tree.map(lambda _: vmem, out_shape),
        compiler_params=pltpu.CompilerParams(vmem_limit_bytes=VMEM_LIMIT),
        cost_estimate=pl.CostEstimate(**cost),
    )


def hot_rows(target, map_ref, base, chunk):
    rows = target.shape[0]
    lane = lax.broadcasted_iota(jnp.int32, (rows, LANES), 1)
    parts = []
    for lane_base in range(base, base + chunk, LANES):
        parts.append(jnp.where(lane + lane_base == target, 1.0, 0.0).astype(BF16))
    hot = jnp.concatenate(parts, axis=1)
    return jnp.dot(hot, map_ref[base : base + chunk, :], preferred_element_type=F32)


def pick_kernel(core_flip, target_ref, map_ref, out_ref):
    half = target_ref.shape[1] // 2
    positions = map_ref.shape[0]
    chunk = pick_chunk(positions, 1536)
    second = lax.axis_index("tm") != core_flip
    target = jnp.where(second, target_ref[:, half:], target_ref[:, :half])
    target = jnp.transpose(jnp.broadcast_to(target, (LANES, half)))
    picked = None
    for base in range(0, positions, chunk):
        term = hot_rows(target, map_ref, base, chunk)
        picked = term if picked is None else picked + term
    out_ref[...] = picked.astype(BF16)


def coord_kernel(map_width, after_ref, out_ref):
    positions = out_ref.shape[0]
    chunk = pick_chunk(positions, 512)
    lane = lax.broadcasted_iota(jnp.int32, (chunk, LANES), 1)
    local_place = lax.broadcasted_iota(jnp.int32, (chunk, LANES), 0).astype(F32)

    @pl.loop(0, positions // chunk)
    def _(step):
        place = local_place + (step * chunk).astype(F32)
        row = jnp.floor((place + 0.5) * (1.0 / map_width))
        rest = jnp.where(lane == 2, 1.0, 0.0)
        value = jnp.where(lane == 0, place - row * map_width, jnp.where(lane == 1, row, rest))
        out_ref[pl.ds(pl.multiple_of(step * chunk, chunk), chunk), :] = value.astype(BF16)


def split(value):
    pieces = []
    for _ in range(3):
        piece = value.astype(BF16).astype(F32)
        pieces.append(piece)
        value = value - piece
    return pieces


def half_kernel(rows_here, height, width, query_ref, map_ref, coord_ref, out_ref):
    positions, channels = map_ref.shape
    factor = math.log2(math.e) / math.sqrt(channels)
    query = query_ref[...]
    first_row = (lax.axis_index("space") * rows_here).astype(F32)
    chunk = pick_chunk(positions, 1280)

    def score(base):
        keys = map_ref[base : base + chunk, :]
        return lax.dot_general(query, keys, NT, preferred_element_type=F32)

    top = sums = None
    ahead = score(0)
    for base in range(0, positions, chunk):
        scores = ahead
        if base + chunk < positions:
            ahead = score(base + chunk)
        window = slice(base, base + chunk)
        values = jnp.concatenate([map_ref[window, :], coord_ref[window, :]], axis=1)
        new_top = jnp.max(scores, axis=1, keepdims=True) * factor
        if top is not None:
            new_top = jnp.maximum(new_top, top)
        weights = jnp.exp2(scores * factor - new_top).astype(BF16)
        terms = jnp.dot(weights, values, preferred_element_type=F32)
        sums = terms if sums is None else terms + jnp.exp2(top - new_top) * sums
        top = new_top
    feats = sums[:, :channels] / sums[:, channels + 2 : channels + 3]
    extra = sums[:, channels:]
    lane = lax.broadcasted_iota(jnp.int32, extra.shape, 1)
    extra = jnp.transpose(jnp.where(lane == 3, top, extra))
    total = extra[2:3]
    across = extra[0:1] / total / width
    down = (extra[1:2] / total + first_row) / height
    store_block(out_ref, feats, [extra[3:4], total, across, down])


def store_block(out_ref, feats, lines):
    queries = feats.shape[0]
    out_ref[:queries, :] = feats
    rows = [piece for line in lines for piece in split(line)]
    sub = lax.broadcasted_iota(jnp.int32, (PIECE_ROWS, queries), 0)
    aux = jnp.zeros((PIECE_ROWS, queries), F32)
    for index, row in enumerate(rows):
        aux = jnp.where(sub == index, row, aux)
    for tile in range(queries // LANES):
        base = queries + tile * PIECE_ROWS
        out_ref[base : base + PIECE_ROWS, :] = aux[:, tile * LANES : (tile + 1) * LANES]


def merged(bit, own_ref, came_ref):
    queries = own_ref.shape[0] * LANES // (LANES + PIECE_ROWS)
    high = (lax.axis_index("space") & bit) != 0
    own, came = own_ref[...].astype(F32), came_ref[...].astype(F32)
    pair = [jnp.where(high, came, own), jnp.where(high, own, came)]
    feats, lines = [], []
    for tile in range(queries // LANES):
        base = queries + tile * PIECE_ROWS
        parts = []
        for block in pair:
            aux = block[base : base + PIECE_ROWS]
            parts.append(
                [aux[i : i + 1] + aux[i + 1 : i + 2] + aux[i + 2 : i + 3] for i in (0, 3, 6, 9)]
            )
        (top_a, total_a, *place_a), (top_b, total_b, *place_b) = parts
        top = jnp.maximum(top_a, top_b)
        weight_a, weight_b = jnp.exp2(top_a - top) * total_a, jnp.exp2(top_b - top) * total_b
        total = weight_a + weight_b
        share_a, share_b = weight_a / total, weight_b / total
        places = [share_a * a + share_b * b for a, b in zip(place_a, place_b)]
        lines.append([top, total, *places])
        sub = lax.broadcasted_iota(jnp.int32, (8, LANES), 0)
        table = jnp.transpose(jnp.where(sub == 0, share_a, jnp.where(sub == 1, share_b, 0.0)))
        window = slice(tile * LANES, (tile + 1) * LANES)
        feats.append(table[:, 0:1] * pair[0][window] + table[:, 1:2] * pair[1][window])
    return jnp.concatenate(feats, axis=0), [jnp.concatenate(v, axis=1) for v in zip(*lines)]


def my_bit(step, n_space):
    bits = n_space.bit_length() - 1
    return jnp.left_shift(1, lax.rem(lax.axis_index("tm") + step, bits))


def merge_kernel(n_space, step, own_ref, came_ref, out_ref):
    store_block(out_ref, *merged(my_bit(step, n_space), own_ref, came_ref))


def last_merge_kernel(n_space, step, decay_ref, near_own, near_came, far_own, far_came, *outs):
    out_ref, place_ref = outs
    bit = my_bit(step, n_space)
    base = 0
    for own_ref, came_ref in ((near_own, near_came), (far_own, far_came)):
        feats, lines = merged(bit, own_ref, came_ref)
        window = slice(base, base + feats.shape[0])
        out_ref[window, :] = feats.astype(BF16)
        place_ref[0:1, window] = lines[2]
        place_ref[1:2, window] = lines[3]
        base += feats.shape[0]
    sub = lax.broadcasted_iota(jnp.int32, (PIECE_ROWS, LANES), 0)
    rows = jnp.zeros((PIECE_ROWS, LANES), F32)
    for index, piece in enumerate(split(decay_ref[...])):
        rows = jnp.where(sub == index, piece, rows)
    out_ref[base:, :] = rows.astype(BF16)


def track_kernel(dw_ref, pw_ref, ow_ref, place_ref, mine_ref, theirs_ref, out_ref):
    early = lax.axis_index("tm") == 0
    queries = place_ref.shape[1]
    half = queries // 2
    mine, theirs = mine_ref[...].astype(F32), theirs_ref[...].astype(F32)

    def retention(rows):
        return rows[queries : queries + 1] + rows[queries + 1 : queries + 2] + rows[queries + 2 : queries + 3]

    decay_mine, decay_theirs = retention(mine), retention(theirs)
    mine = mine[:queries]
    theirs = jnp.concatenate([theirs[half:queries], theirs[:half]], axis=0)
    attended = [jnp.where(early, mine, theirs), jnp.where(early, theirs, mine)]
    decay = [
        jnp.where(early, decay_mine, decay_theirs),
        jnp.where(early, decay_theirs, decay_mine),
    ]
    taps = dw_ref.shape[0]
    refined = []
    for frame in range(2):
        depth = None
        for tap in range(taps):
            source = frame + tap - taps // 2
            if 0 <= source < 2:
                term = dw_ref[tap : tap + 1, :] * attended[source]
                depth = term if depth is None else depth + term
        hidden = jax.nn.gelu(depth).astype(BF16)
        mixed = jnp.dot(hidden, pw_ref[...], preferred_element_type=F32)
        refined.append(attended[frame] + mixed)
    first = (1.0 - decay[0]) * refined[0]
    second = decay[1] * first + (1.0 - decay[1]) * refined[1]
    memory = jnp.where(early, first, second)
    delta = lax.dot_general(
        ow_ref[...], memory, NT, preferred_element_type=F32, precision=lax.Precision.HIGHEST
    )
    line = place_ref[...] + delta
    low, high = line[:, :half], line[:, half:]
    out_ref[0, :, :half] = jnp.where(early, low, high)
    out_ref[0, :, half:] = jnp.where(early, high, low)


def swap(value, axis, bit):
    return lax.ppermute(value, axis, [(i, i ^ bit) for i in range(lax.axis_size(axis))])


def all_sum(value, axis):
    count = lax.axis_size(axis)
    if count & (count - 1):
        return lax.psum(value, axis)
    bit = 1
    while bit < count:
        value = value + swap(value, axis, bit)
        bit *= 2
    return value


def local_general(
    feature_maps, query_frame, query_row, query_col, ema_decay, dw_kernel, pw_weight, out_weight
):
    frames_here, rows_here, map_width, channels = feature_maps.shape
    assert frames_here == 1 and channels == LANES
    queries = query_frame.shape[0]
    n_tm, n_space = lax.axis_size("tm"), lax.axis_size("space")
    n_groups = n_tm * n_space
    group = queries // n_groups
    height = rows_here * n_space
    positions = rows_here * map_width
    maps = feature_maps.reshape(positions, channels)
    halves = 2 if n_tm == 2 else 1
    part = jax.ShapeDtypeStruct((queries // halves, channels), BF16)

    picked = call(
        functools.partial(gather_kernel, rows_here, map_width),
        [part] * halves,
        4,
        flops=2 * queries * positions * channels,
        bytes_accessed=2 * positions * channels,
        transcendentals=0,
    )(query_frame[None], query_row[None], query_col[None], maps)

    place = jnp.arange(positions, dtype=jnp.int32)[:, None]
    lane = jnp.arange(LANES, dtype=jnp.int32)[None, :]
    coords = jnp.where(
        lane == 0,
        place % map_width,
        jnp.where(lane == 1, place // map_width, jnp.where(lane == 2, 1, 0)),
    ).astype(BF16)

    if halves == 2:
        mine = picked[0] + swap(picked[1], "tm", 1)
        mine = all_sum(mine, "space")
        feats = [mine, swap(mine, "tm", 1)]
    else:
        feats = [all_sum(all_sum(picked[0], "tm"), "space")]

    feat_rows = -(-group // 8) * 8
    blocks = call(
        functools.partial(volume_kernel, n_groups, rows_here, height, map_width),
        jax.ShapeDtypeStruct((n_groups, feat_rows + AUX_ROWS, LANES), F32),
        halves + 3,
        flops=6 * queries * positions * channels,
        bytes_accessed=4 * positions * channels,
        transcendentals=queries * positions,
    )(*feats, maps, coords, ema_decay)

    blocks = lax.all_to_all(blocks, ("tm", "space"), 0, 0, tiled=True)

    n_out = out_weight.shape[0]
    out_rows = -(-n_tm * n_out // 8) * 8
    lines = call(
        functools.partial(tail_kernel, n_tm, n_space, group),
        jax.ShapeDtypeStruct((out_rows, LANES), F32),
        4,
        flops=2 * n_tm * group * channels * channels,
        bytes_accessed=4 * n_groups * (feat_rows + AUX_ROWS) * LANES,
        transcendentals=n_tm * group * channels,
    )(dw_kernel, pw_weight, out_weight, blocks)

    lines = lax.all_gather(lines, ("tm", "space"), axis=0)
    own = lax.dynamic_slice_in_dim(lines, lax.axis_index("tm") * n_out, n_out, axis=1)
    own = own[:, :, :group]
    return jnp.transpose(own, (1, 0, 2)).reshape(1, n_out, queries)


def core_swap(value):
    return lax.ppermute(value, "tm", [(0, 1), (1, 0)])


def space_swap(value, step):
    n_space = lax.axis_size("space")
    bits = n_space.bit_length() - 1
    pairs = []
    for tm in range(2):
        for space in range(n_space):
            to = space ^ (1 << (tm + step) % bits)
            pairs.append((tm * n_space + space, tm * n_space + to))
    return lax.ppermute(value, ("tm", "space"), pairs)


def local_pair(
    feature_maps, query_frame, query_row, query_col, ema_decay, dw_kernel, pw_weight, out_weight
):
    _, rows_here, map_width, channels = feature_maps.shape
    queries = query_frame.shape[0]
    n_space = lax.axis_size("space")
    half = queries // 2
    height = rows_here * n_space
    positions = rows_here * map_width
    maps = feature_maps.reshape(positions, channels)

    row = query_row - lax.axis_index("space") * rows_here
    here = (query_frame == lax.axis_index("tm")) & (row >= 0) & (row < rows_here)
    target = jnp.where(here, row * map_width + query_col, -1)[None]

    def pick(core_flip):
        return call(
            functools.partial(pick_kernel, core_flip),
            jax.ShapeDtypeStruct((half, channels), BF16),
            2,
            flops=queries * positions * channels,
            bytes_accessed=2 * positions * channels,
            transcendentals=0,
        )(target, maps)

    arrived = core_swap(pick(1))
    coords = call(
        functools.partial(coord_kernel, map_width),
        jax.ShapeDtypeStruct((positions, LANES), BF16),
        1,
        flops=8 * positions * LANES,
        bytes_accessed=2 * positions * LANES,
        transcendentals=0,
    )(target)
    mine = pick(0) + arrived
    steps = n_space.bit_length() - 1
    for step in range(steps):
        mine = mine + space_swap(mine, step)
    theirs = core_swap(mine)

    block = jax.ShapeDtypeStruct((half + half // LANES * PIECE_ROWS, LANES), F32)

    def blocks_of(feats):
        return call(
            functools.partial(half_kernel, rows_here, height, map_width),
            block,
            3,
            flops=3 * queries * positions * channels,
            bytes_accessed=4 * positions * channels,
            transcendentals=half * positions,
        )(feats, maps, coords)

    def sent(value, step):
        value = lax.optimization_barrier(value.astype(jnp.float16))
        return value.astype(F32), space_swap(value, step).astype(F32)

    def merge(pair, step):
        return call(
            functools.partial(merge_kernel, n_space, step),
            block,
            2,
            flops=4 * half * channels,
            bytes_accessed=12 * half * channels,
            transcendentals=0,
        )(*pair)

    pairs = [sent(blocks_of(mine), 0), sent(blocks_of(theirs), 0)]
    for step in range(1, steps):
        pairs = [sent(merge(pair, step - 1), step) for pair in pairs]

    n_out = out_weight.shape[0]
    attended, place = call(
        functools.partial(last_merge_kernel, n_space, steps - 1),
        [
            jax.ShapeDtypeStruct((queries + PIECE_ROWS, LANES), BF16),
            jax.ShapeDtypeStruct((n_out, queries), F32),
        ],
        5,
        flops=4 * queries * channels,
        bytes_accessed=12 * queries * channels,
        transcendentals=0,
    )(ema_decay, *pairs[0], *pairs[1])
    return call(
        track_kernel,
        jax.ShapeDtypeStruct((1, n_out, queries), F32),
        6,
        flops=8 * queries * channels * channels,
        bytes_accessed=8 * queries * channels,
        transcendentals=2 * queries * channels,
    )(dw_kernel, pw_weight, out_weight, place, attended, core_swap(attended))


def local(feature_maps, query_frame, *rest):
    n_tm, n_space = lax.axis_size("tm"), lax.axis_size("space")
    paired = n_tm == 2 and n_space > 1 and n_space & (n_space - 1) == 0
    if paired and query_frame.shape[0] % (2 * LANES) == 0:
        return local_pair(feature_maps, query_frame, *rest)
    return local_general(feature_maps, query_frame, *rest)


def solution(mesh):
    placed = (
        P(("video", "tm"), "space", None, None),
        P("video"),
        P("video"),
        P("video"),
        P(("video", "tm"), None),
        P(),
        P(),
        P(),
    )
    return jax.shard_map(
        local, mesh=mesh, in_specs=placed, out_specs=P(("video", "tm"), None, None), check_vma=False
    )
```

```python
import functools
import math

import jax
import jax.numpy as jnp
from jax import lax
from jax.experimental import pallas as pl
from jax.experimental.pallas import tpu as pltpu
from jax.sharding import PartitionSpec as P

F32 = jnp.float32
BF16 = jnp.bfloat16
LANES = 128
AUX_ROWS = 8
PIECE_ROWS = 16
VMEM_LIMIT = 40 * 1024 * 1024
FIRST_LIMIT = 60 * 1024 * 1024
NT = (((1,), (1,)), ((), ()))


def pick_chunk(total, limit):
    best = None
    for size in range(LANES, limit + 1, LANES):
        if total % size == 0 and (best is None or size % 256 == 0 or best % 256):
            best = size
    return best if best is not None else total


def gather_kernel(rows_here, map_width, frame_ref, row_ref, col_ref, map_ref, *out_refs):
    positions = map_ref.shape[0]
    queries = frame_ref.shape[1]
    tm = lax.axis_index("tm")
    row = row_ref[...] - lax.axis_index("space") * rows_here
    here = (frame_ref[...] == tm) & (row >= 0) & (row < rows_here)
    target = jnp.where(here, row * map_width + col_ref[...], -1)
    target = jnp.transpose(jnp.broadcast_to(target, (LANES, queries)))
    chunk = pick_chunk(positions, 1536)
    picked = None
    for base in range(0, positions, chunk):
        parts = []
        for lane_base in range(base, base + chunk, LANES):
            lane = lax.broadcasted_iota(jnp.int32, (queries, LANES), 1) + lane_base
            parts.append(jnp.where(lane == target, 1.0, 0.0).astype(BF16))
        hot = jnp.concatenate(parts, axis=1)
        term = jnp.dot(hot, map_ref[base : base + chunk, :], preferred_element_type=F32)
        picked = term if picked is None else picked + term
    if len(out_refs) == 1:
        out_refs[0][...] = picked.astype(BF16)
        return
    half = queries // 2
    first, second = picked[:half].astype(F32), picked[half:].astype(F32)
    out_refs[0][...] = jnp.where(tm == 0, first, second).astype(BF16)
    out_refs[1][...] = jnp.where(tm == 0, second, first).astype(BF16)


def volume_kernel(n_groups, rows_here, height, width, *refs):
    *query_refs, map_ref, coord_ref, decay_ref, out_ref = refs
    positions, channels = map_ref.shape
    factor = math.log2(math.e) / math.sqrt(channels)
    part_queries = query_refs[0].shape[0]
    n_parts = len(query_refs)
    group = part_queries * n_parts // n_groups
    feat_rows = out_ref.shape[1] - AUX_ROWS
    first_row = (lax.axis_index("space") * rows_here).astype(F32)
    tm = lax.axis_index("tm")
    chunk = pick_chunk(positions, 1280)
    state = [None] * n_parts
    for base in range(0, positions, chunk):
        keys = map_ref[base : base + chunk, :]
        values = jnp.concatenate([keys, coord_ref[base : base + chunk, :]], axis=1)
        for part in range(n_parts):
            scores = lax.dot_general(
                query_refs[part][...], keys, NT, preferred_element_type=F32
            )
            top = jnp.max(scores, axis=1, keepdims=True) * factor
            if state[part] is not None:
                old_top, old_sum = state[part]
                top = jnp.maximum(top, old_top)
            weights = jnp.exp2(scores * factor - top).astype(BF16)
            sums = jnp.dot(weights, values, preferred_element_type=F32)
            if state[part] is not None:
                sums = sums + jnp.exp2(old_top - top) * old_sum
            state[part] = (top, sums)
    decay = [decay_ref[...]]
    sub = lax.broadcasted_iota(jnp.int32, (AUX_ROWS, LANES), 0)
    for part in range(n_parts):
        top, sums = state[part]
        feats = sums[:, :channels] / sums[:, channels + 2 : channels + 3]
        extra = sums[:, channels:]
        lane = lax.broadcasted_iota(jnp.int32, extra.shape, 1)
        extra = jnp.transpose(jnp.where(lane == 3, top, extra))
        total = extra[2:3]
        rows = [extra[3:4]]
        rows += [total, extra[0:1] / total / width, (extra[1:2] / total + first_row) / height]
        aux = jnp.zeros((AUX_ROWS, part_queries), F32)
        wide = lax.broadcasted_iota(jnp.int32, aux.shape, 0)
        for index, values in enumerate(rows):
            aux = jnp.where(wide == index, values, aux)
        where = part if n_parts == 1 else jnp.where(tm == 0, part, 1 - part)
        groups_here = n_groups // n_parts
        for index in range(groups_here):
            shift = (part_queries - index * group) % part_queries
            block = pltpu.roll(aux, shift, 1) if shift else aux
            block = block[:, :LANES]
            for offset, piece in enumerate(decay):
                block = jnp.where(sub == len(rows) + offset, piece, block)
            pieces = [feats[index * group : (index + 1) * group]]
            if feat_rows > group:
                pieces.append(jnp.zeros((feat_rows - group, LANES), F32))
            pieces.append(block)
            out_ref[where * groups_here + index] = jnp.concatenate(pieces, axis=0).astype(
                out_ref.dtype
            )


def tail_kernel(n_tm, n_space, group, dw_ref, pw_ref, ow_ref, in_ref, out_ref):
    feat_rows = in_ref.shape[1] - AUX_ROWS
    n_blocks = n_tm * n_space
    blocks = [in_ref[index].astype(F32) for index in range(n_blocks)]
    aux = [block[feat_rows:] for block in blocks]
    positions, shares, decays = [], [], []
    for frame in range(n_tm):
        mine = aux[frame * n_space : (frame + 1) * n_space]
        top = mine[0][0:1]
        for block in mine[1:]:
            top = jnp.maximum(top, block[0:1])
        weight = [jnp.exp2(b[0:1] - top) * b[1:2] for b in mine]
        total = sum(weight[1:], weight[0])
        share = [w / total for w in weight]
        shares += share
        across = [s * b[2:3] for s, b in zip(share, mine)]
        down = [s * b[3:4] for s, b in zip(share, mine)]
        positions.append((sum(across[1:], across[0]), sum(down[1:], down[0])))
        decays.append(mine[0][4:5])
    pad_blocks = -(-n_blocks // 8) * 8
    table = jnp.zeros((pad_blocks, LANES), F32)
    sub = lax.broadcasted_iota(jnp.int32, table.shape, 0)
    for index, share in enumerate(shares):
        table = jnp.where(sub == index, share, table)
    table = jnp.transpose(table)
    attended = []
    for frame in range(n_tm):
        value = None
        for index in range(frame * n_space, (frame + 1) * n_space):
            term = table[:group, index : index + 1] * blocks[index][:group]
            value = term if value is None else value + term
        attended.append(value.astype(BF16).astype(F32))
    taps = dw_ref.shape[0]
    hidden = []
    for frame in range(n_tm):
        depth = None
        for tap in range(taps):
            source = frame + tap - taps // 2
            if 0 <= source < n_tm:
                term = dw_ref[tap : tap + 1, :] * attended[source]
                depth = term if depth is None else depth + term
        hidden.append(jax.nn.gelu(depth).astype(BF16).astype(F32))
    hidden = jnp.concatenate(hidden, axis=0).astype(BF16)
    mixed = jnp.dot(hidden, pw_ref[...], preferred_element_type=F32)
    memory = None
    out = jnp.zeros(out_ref.shape, F32)
    out_sub = lax.broadcasted_iota(jnp.int32, out.shape, 0)
    n_out = ow_ref.shape[0]
    for frame in range(n_tm):
        refined = attended[frame] + mixed[frame * group : (frame + 1) * group]
        fresh = (1.0 - decays[frame]) * refined
        memory = fresh if memory is None else decays[frame] * memory + fresh
        padded = memory
        if group < LANES:
            padded = jnp.concatenate([memory, jnp.zeros((LANES - group, LANES), F32)], axis=0)
        delta = lax.dot_general(
            ow_ref[...], padded, NT, preferred_element_type=F32, precision=lax.Precision.HIGHEST
        )
        for axis in range(n_out):
            line = positions[frame][axis] + delta[axis : axis + 1]
            out = jnp.where(out_sub == frame * n_out + axis, line, out)
    out_ref[...] = out


def call(kernel, out_shape, n_in, **cost):
    vmem = pl.BlockSpec(memory_space=pltpu.VMEM)
    return pl.pallas_call(
        kernel,
        out_shape=out_shape,
        in_specs=[vmem] * n_in,
        out_specs=jax.tree.map(lambda _: vmem, out_shape),
        compiler_params=pltpu.CompilerParams(vmem_limit_bytes=VMEM_LIMIT),
        cost_estimate=pl.CostEstimate(**cost),
    )


def hot_rows(target, map_ref, base, chunk):
    rows = target.shape[0]
    lane = lax.broadcasted_iota(jnp.int32, (rows, LANES), 1)
    parts = []
    for lane_base in range(base, base + chunk, LANES):
        parts.append(jnp.where(lane + lane_base == target, 1.0, 0.0).astype(BF16))
    hot = jnp.concatenate(parts, axis=1)
    return jnp.dot(hot, map_ref[base : base + chunk, :], preferred_element_type=F32)


def pick_both_kernel(
    rows_here,
    map_width,
    frame_hbm,
    row_hbm,
    col_hbm,
    map_hbm,
    send_ref,
    keep_ref,
    index_ref,
    map_ref,
    index_sem,
    map_sem,
):
    index_copies = [
        pltpu.make_async_copy(ref, index_ref.at[i], index_sem.at[i])
        for i, ref in enumerate((frame_hbm, row_hbm, col_hbm))
    ]
    chunk = map_ref.shape[0] // map_sem.shape[0]
    map_copies = [
        pltpu.make_async_copy(
            map_hbm.at[pl.ds(i * chunk, chunk)], map_ref.at[pl.ds(i * chunk, chunk)], map_sem.at[i]
        )
        for i in range(map_sem.shape[0])
    ]
    for copy in index_copies + map_copies:
        copy.start()
    for copy in index_copies:
        copy.wait()
    tm = lax.axis_index("tm")
    row = index_ref[1] - lax.axis_index("space") * rows_here
    here = (index_ref[0] == tm) & (row >= 0) & (row < rows_here)
    target = jnp.where(here, row * map_width + index_ref[2], -1)
    queries = target.shape[1]
    target = jnp.transpose(jnp.broadcast_to(target, (LANES, queries)))
    tile = jnp.right_shift(target, 7).astype(F32).astype(BF16)
    lane = lax.broadcasted_iota(jnp.int32, (queries, LANES), 1)
    hot_lane = jnp.where(lane == jnp.bitwise_and(target, LANES - 1), 1.0, 0.0).astype(BF16)
    picked = None
    for index, copy in enumerate(map_copies):
        tiles = range(index * chunk // LANES, (index + 1) * chunk // LANES)
        hot = jnp.concatenate(
            [jnp.where(tile == jnp.asarray(j, BF16), hot_lane, jnp.zeros_like(hot_lane)) for j in tiles],
            axis=1,
        )
        copy.wait()
        window = slice(index * chunk, (index + 1) * chunk)
        term = jnp.dot(hot, map_ref[window, :], preferred_element_type=F32)
        picked = term if picked is None else picked + term
    half = queries // 2
    first, second = picked[:half], picked[half:]
    send_ref[...] = jnp.where(tm == 0, second, first).astype(BF16)
    keep_ref[...] = jnp.where(tm == 0, first, second).astype(BF16)


def coord_kernel(map_width, after_ref, out_ref):
    positions = out_ref.shape[0]
    chunk = pick_chunk(positions, 512)
    lane = lax.broadcasted_iota(jnp.int32, (chunk, LANES), 1)
    local_place = lax.broadcasted_iota(jnp.int32, (chunk, LANES), 0).astype(F32)

    @pl.loop(0, positions // chunk)
    def _(step):
        place = local_place + (step * chunk).astype(F32)
        row = jnp.floor((place + 0.5) * (1.0 / map_width))
        rest = jnp.where(lane == 2, 1.0, 0.0)
        value = jnp.where(lane == 0, place - row * map_width, jnp.where(lane == 1, row, rest))
        out_ref[pl.ds(pl.multiple_of(step * chunk, chunk), chunk), :] = value.astype(BF16)


def split(value):
    pieces = []
    for _ in range(3):
        piece = value.astype(BF16).astype(F32)
        pieces.append(piece)
        value = value - piece
    return pieces


def half_kernel(rows_here, height, width, query_ref, map_ref, coord_ref, out_ref):
    positions, channels = map_ref.shape
    factor = math.log2(math.e) / math.sqrt(channels)
    query = query_ref[...]
    first_row = (lax.axis_index("space") * rows_here).astype(F32)
    chunk = pick_chunk(positions, 1280)

    def score(base):
        keys = map_ref[base : base + chunk, :]
        return lax.dot_general(query, keys, NT, preferred_element_type=F32)

    top = sums = None
    ahead = score(0)
    for base in range(0, positions, chunk):
        scores = ahead
        if base + chunk < positions:
            ahead = score(base + chunk)
        window = slice(base, base + chunk)
        values = jnp.concatenate([map_ref[window, :], coord_ref[window, :]], axis=1)
        new_top = jnp.max(scores, axis=1, keepdims=True) * factor
        if top is not None:
            new_top = jnp.maximum(new_top, top)
        weights = jnp.exp2(scores * factor - new_top).astype(BF16)
        terms = jnp.dot(weights, values, preferred_element_type=F32)
        sums = terms if sums is None else terms + jnp.exp2(top - new_top) * sums
        top = new_top
    feats = sums[:, :channels] / sums[:, channels + 2 : channels + 3]
    extra = sums[:, channels:]
    lane = lax.broadcasted_iota(jnp.int32, extra.shape, 1)
    extra = jnp.transpose(jnp.where(lane == 3, top, extra))
    total = extra[2:3]
    across = extra[0:1] / total / width
    down = (extra[1:2] / total + first_row) / height
    store_block(out_ref, feats, [extra[3:4], total, across, down])


def store_block(out_ref, feats, lines):
    queries = feats.shape[0]
    out_ref[:queries, :] = feats
    rows = [piece for line in lines for piece in split(line)]
    sub = lax.broadcasted_iota(jnp.int32, (PIECE_ROWS, queries), 0)
    aux = jnp.zeros((PIECE_ROWS, queries), F32)
    for index, row in enumerate(rows):
        aux = jnp.where(sub == index, row, aux)
    for tile in range(queries // LANES):
        base = queries + tile * PIECE_ROWS
        out_ref[base : base + PIECE_ROWS, :] = aux[:, tile * LANES : (tile + 1) * LANES]


def merged(bit, own_ref, came_ref):
    queries = own_ref.shape[0] * LANES // (LANES + PIECE_ROWS)
    high = (lax.axis_index("space") & bit) != 0
    own, came = own_ref[...].astype(F32), came_ref[...].astype(F32)
    pair = [jnp.where(high, came, own), jnp.where(high, own, came)]
    feats, lines = [], []
    for tile in range(queries // LANES):
        base = queries + tile * PIECE_ROWS
        parts = []
        for block in pair:
            aux = block[base : base + PIECE_ROWS]
            parts.append(
                [aux[i : i + 1] + aux[i + 1 : i + 2] + aux[i + 2 : i + 3] for i in (0, 3, 6, 9)]
            )
        (top_a, total_a, *place_a), (top_b, total_b, *place_b) = parts
        top = jnp.maximum(top_a, top_b)
        weight_a, weight_b = jnp.exp2(top_a - top) * total_a, jnp.exp2(top_b - top) * total_b
        total = weight_a + weight_b
        share_a, share_b = weight_a / total, weight_b / total
        places = [share_a * a + share_b * b for a, b in zip(place_a, place_b)]
        lines.append([top, total, *places])
        sub = lax.broadcasted_iota(jnp.int32, (8, LANES), 0)
        table = jnp.transpose(jnp.where(sub == 0, share_a, jnp.where(sub == 1, share_b, 0.0)))
        window = slice(tile * LANES, (tile + 1) * LANES)
        feats.append(table[:, 0:1] * pair[0][window] + table[:, 1:2] * pair[1][window])
    return jnp.concatenate(feats, axis=0), [jnp.concatenate(v, axis=1) for v in zip(*lines)]


def my_bit(step, n_space):
    bits = n_space.bit_length() - 1
    return jnp.left_shift(1, lax.rem(lax.axis_index("tm") + step, bits))


def merge_kernel(n_space, step, own_ref, came_ref, out_ref):
    store_block(out_ref, *merged(my_bit(step, n_space), own_ref, came_ref))


def last_merge_kernel(n_space, step, decay_ref, near_own, near_came, far_own, far_came, *outs):
    out_ref, place_ref = outs
    bit = my_bit(step, n_space)
    base = 0
    for own_ref, came_ref in ((near_own, near_came), (far_own, far_came)):
        feats, lines = merged(bit, own_ref, came_ref)
        window = slice(base, base + feats.shape[0])
        out_ref[window, :] = feats.astype(BF16)
        place_ref[0:1, window] = lines[2]
        place_ref[1:2, window] = lines[3]
        base += feats.shape[0]
    sub = lax.broadcasted_iota(jnp.int32, (PIECE_ROWS, LANES), 0)
    rows = jnp.zeros((PIECE_ROWS, LANES), F32)
    for index, piece in enumerate(split(decay_ref[...])):
        rows = jnp.where(sub == index, piece, rows)
    out_ref[base:, :] = rows.astype(BF16)


def track_kernel(dw_ref, pw_ref, ow_ref, place_ref, mine_ref, theirs_ref, out_ref):
    early = lax.axis_index("tm") == 0
    queries = place_ref.shape[1]
    half = queries // 2
    mine, theirs = mine_ref[...].astype(F32), theirs_ref[...].astype(F32)

    def retention(rows):
        return rows[queries : queries + 1] + rows[queries + 1 : queries + 2] + rows[queries + 2 : queries + 3]

    decay_mine, decay_theirs = retention(mine), retention(theirs)
    mine = mine[:queries]
    theirs = jnp.concatenate([theirs[half:queries], theirs[:half]], axis=0)
    attended = [jnp.where(early, mine, theirs), jnp.where(early, theirs, mine)]
    decay = [
        jnp.where(early, decay_mine, decay_theirs),
        jnp.where(early, decay_theirs, decay_mine),
    ]
    taps = dw_ref.shape[0]
    refined = []
    for frame in range(2):
        depth = None
        for tap in range(taps):
            source = frame + tap - taps // 2
            if 0 <= source < 2:
                term = dw_ref[tap : tap + 1, :] * attended[source]
                depth = term if depth is None else depth + term
        hidden = jax.nn.gelu(depth).astype(BF16)
        mixed = jnp.dot(hidden, pw_ref[...], preferred_element_type=F32)
        refined.append(attended[frame] + mixed)
    first = (1.0 - decay[0]) * refined[0]
    second = decay[1] * first + (1.0 - decay[1]) * refined[1]
    memory = jnp.where(early, first, second)
    delta = lax.dot_general(
        ow_ref[...], memory, NT, preferred_element_type=F32, precision=lax.Precision.HIGHEST
    )
    line = place_ref[...] + delta
    low, high = line[:, :half], line[:, half:]
    out_ref[0, :, :half] = jnp.where(early, low, high)
    out_ref[0, :, half:] = jnp.where(early, high, low)


def swap(value, axis, bit):
    return lax.ppermute(value, axis, [(i, i ^ bit) for i in range(lax.axis_size(axis))])


def all_sum(value, axis):
    count = lax.axis_size(axis)
    if count & (count - 1):
        return lax.psum(value, axis)
    bit = 1
    while bit < count:
        value = value + swap(value, axis, bit)
        bit *= 2
    return value


def local_general(
    feature_maps, query_frame, query_row, query_col, ema_decay, dw_kernel, pw_weight, out_weight
):
    frames_here, rows_here, map_width, channels = feature_maps.shape
    assert frames_here == 1 and channels == LANES
    queries = query_frame.shape[0]
    n_tm, n_space = lax.axis_size("tm"), lax.axis_size("space")
    n_groups = n_tm * n_space
    group = queries // n_groups
    height = rows_here * n_space
    positions = rows_here * map_width
    maps = feature_maps.reshape(positions, channels)
    halves = 2 if n_tm == 2 else 1
    part = jax.ShapeDtypeStruct((queries // halves, channels), BF16)

    picked = call(
        functools.partial(gather_kernel, rows_here, map_width),
        [part] * halves,
        4,
        flops=2 * queries * positions * channels,
        bytes_accessed=2 * positions * channels,
        transcendentals=0,
    )(query_frame[None], query_row[None], query_col[None], maps)

    place = jnp.arange(positions, dtype=jnp.int32)[:, None]
    lane = jnp.arange(LANES, dtype=jnp.int32)[None, :]
    coords = jnp.where(
        lane == 0,
        place % map_width,
        jnp.where(lane == 1, place // map_width, jnp.where(lane == 2, 1, 0)),
    ).astype(BF16)

    if halves == 2:
        mine = picked[0] + swap(picked[1], "tm", 1)
        mine = all_sum(mine, "space")
        feats = [mine, swap(mine, "tm", 1)]
    else:
        feats = [all_sum(all_sum(picked[0], "tm"), "space")]

    feat_rows = -(-group // 8) * 8
    blocks = call(
        functools.partial(volume_kernel, n_groups, rows_here, height, map_width),
        jax.ShapeDtypeStruct((n_groups, feat_rows + AUX_ROWS, LANES), F32),
        halves + 3,
        flops=6 * queries * positions * channels,
        bytes_accessed=4 * positions * channels,
        transcendentals=queries * positions,
    )(*feats, maps, coords, ema_decay)

    blocks = lax.all_to_all(blocks, ("tm", "space"), 0, 0, tiled=True)

    n_out = out_weight.shape[0]
    out_rows = -(-n_tm * n_out // 8) * 8
    lines = call(
        functools.partial(tail_kernel, n_tm, n_space, group),
        jax.ShapeDtypeStruct((out_rows, LANES), F32),
        4,
        flops=2 * n_tm * group * channels * channels,
        bytes_accessed=4 * n_groups * (feat_rows + AUX_ROWS) * LANES,
        transcendentals=n_tm * group * channels,
    )(dw_kernel, pw_weight, out_weight, blocks)

    lines = lax.all_gather(lines, ("tm", "space"), axis=0)
    own = lax.dynamic_slice_in_dim(lines, lax.axis_index("tm") * n_out, n_out, axis=1)
    own = own[:, :, :group]
    return jnp.transpose(own, (1, 0, 2)).reshape(1, n_out, queries)


def core_swap(value):
    return lax.ppermute(value, "tm", [(0, 1), (1, 0)])


def space_swap(value, step):
    n_space = lax.axis_size("space")
    bits = n_space.bit_length() - 1
    pairs = []
    for tm in range(2):
        for space in range(n_space):
            to = space ^ (1 << (tm + step) % bits)
            pairs.append((tm * n_space + space, tm * n_space + to))
    return lax.ppermute(value, ("tm", "space"), pairs)


def local_pair(
    feature_maps, query_frame, query_row, query_col, ema_decay, dw_kernel, pw_weight, out_weight
):
    _, rows_here, map_width, channels = feature_maps.shape
    queries = query_frame.shape[0]
    n_space = lax.axis_size("space")
    half = queries // 2
    height = rows_here * n_space
    positions = rows_here * map_width
    maps = feature_maps.reshape(positions, channels)

    half_shape = jax.ShapeDtypeStruct((half, channels), BF16)
    vmem, hbm = pl.BlockSpec(memory_space=pltpu.VMEM), pl.BlockSpec(memory_space=pl.ANY)
    n_chunks = positions // pick_chunk(positions, 1536)
    send, keep = pl.pallas_call(
        functools.partial(pick_both_kernel, rows_here, map_width),
        out_shape=[half_shape] * 2,
        in_specs=[hbm] * 4,
        out_specs=[vmem] * 2,
        scratch_shapes=[
            pltpu.VMEM((3, 1, queries), jnp.int32),
            pltpu.VMEM((positions, channels), BF16),
            pltpu.SemaphoreType.DMA((3,)),
            pltpu.SemaphoreType.DMA((n_chunks,)),
        ],
        compiler_params=pltpu.CompilerParams(vmem_limit_bytes=FIRST_LIMIT),
        cost_estimate=pl.CostEstimate(
            flops=2 * queries * positions * channels,
            bytes_accessed=2 * positions * channels,
            transcendentals=0,
        ),
    )(query_frame[None], query_row[None], query_col[None], maps)
    arrived = core_swap(send)
    coords = call(
        functools.partial(coord_kernel, map_width),
        jax.ShapeDtypeStruct((positions, LANES), BF16),
        1,
        flops=8 * positions * LANES,
        bytes_accessed=2 * positions * LANES,
        transcendentals=0,
    )(keep)
    mine = keep + arrived
    steps = n_space.bit_length() - 1
    for step in range(steps):
        mine = mine + space_swap(mine, step)
    theirs = core_swap(mine)

    block = jax.ShapeDtypeStruct((half + half // LANES * PIECE_ROWS, LANES), F32)

    def blocks_of(feats):
        return call(
            functools.partial(half_kernel, rows_here, height, map_width),
            block,
            3,
            flops=3 * queries * positions * channels,
            bytes_accessed=4 * positions * channels,
            transcendentals=half * positions,
        )(feats, maps, coords)

    def sent(value, step):
        value = lax.optimization_barrier(value.astype(jnp.float16))
        return value.astype(F32), space_swap(value, step).astype(F32)

    def merge(pair, step):
        return call(
            functools.partial(merge_kernel, n_space, step),
            block,
            2,
            flops=0,
            bytes_accessed=0,
            transcendentals=0,
        )(*pair)

    pairs = [sent(blocks_of(mine), 0), sent(blocks_of(theirs), 0)]
    for step in range(1, steps):
        pairs = [sent(merge(pair, step - 1), step) for pair in pairs]

    n_out = out_weight.shape[0]
    attended, place = call(
        functools.partial(last_merge_kernel, n_space, steps - 1),
        [
            jax.ShapeDtypeStruct((queries + PIECE_ROWS, LANES), BF16),
            jax.ShapeDtypeStruct((n_out, queries), F32),
        ],
        5,
        flops=4 * queries * channels,
        bytes_accessed=12 * queries * channels,
        transcendentals=0,
    )(ema_decay, *pairs[0], *pairs[1])
    return call(
        track_kernel,
        jax.ShapeDtypeStruct((1, n_out, queries), F32),
        6,
        flops=8 * queries * channels * channels,
        bytes_accessed=8 * queries * channels,
        transcendentals=2 * queries * channels,
    )(dw_kernel, pw_weight, out_weight, place, attended, core_swap(attended))


def local(feature_maps, query_frame, *rest):
    n_tm, n_space = lax.axis_size("tm"), lax.axis_size("space")
    paired = n_tm == 2 and n_space > 1 and n_space & (n_space - 1) == 0
    if paired and query_frame.shape[0] % (2 * LANES) == 0:
        return local_pair(feature_maps, query_frame, *rest)
    return local_general(feature_maps, query_frame, *rest)


def solution(mesh):
    placed = (
        P(("video", "tm"), "space", None, None),
        P("video"),
        P("video"),
        P("video"),
        P(("video", "tm"), None),
        P(),
        P(),
        P(),
    )
    return jax.shard_map(
        local, mesh=mesh, in_specs=placed, out_specs=P(("video", "tm"), None, None), check_vma=False
    )
```

```python
import functools
import math

import jax
import jax.numpy as jnp
from jax import lax
from jax.experimental import pallas as pl
from jax.experimental.pallas import tpu as pltpu
from jax.sharding import PartitionSpec as P

F32 = jnp.float32
BF16 = jnp.bfloat16
LANES = 128
AUX_ROWS = 8
PIECE_ROWS = 16
VMEM_LIMIT = 40 * 1024 * 1024
NT = (((1,), (1,)), ((), ()))


def pick_chunk(total, limit):
    best = None
    for size in range(LANES, limit + 1, LANES):
        if total % size == 0 and (best is None or size % 256 == 0 or best % 256):
            best = size
    return best if best is not None else total


def gather_kernel(rows_here, map_width, frame_ref, row_ref, col_ref, map_ref, *out_refs):
    positions = map_ref.shape[0]
    queries = frame_ref.shape[1]
    tm = lax.axis_index("tm")
    row = row_ref[...] - lax.axis_index("space") * rows_here
    here = (frame_ref[...] == tm) & (row >= 0) & (row < rows_here)
    target = jnp.where(here, row * map_width + col_ref[...], -1)
    target = jnp.transpose(jnp.broadcast_to(target, (LANES, queries)))
    chunk = pick_chunk(positions, 1536)
    picked = None
    for base in range(0, positions, chunk):
        parts = []
        for lane_base in range(base, base + chunk, LANES):
            lane = lax.broadcasted_iota(jnp.int32, (queries, LANES), 1) + lane_base
            parts.append(jnp.where(lane == target, 1.0, 0.0).astype(BF16))
        hot = jnp.concatenate(parts, axis=1)
        term = jnp.dot(hot, map_ref[base : base + chunk, :], preferred_element_type=F32)
        picked = term if picked is None else picked + term
    if len(out_refs) == 1:
        out_refs[0][...] = picked.astype(BF16)
        return
    half = queries // 2
    first, second = picked[:half].astype(F32), picked[half:].astype(F32)
    out_refs[0][...] = jnp.where(tm == 0, first, second).astype(BF16)
    out_refs[1][...] = jnp.where(tm == 0, second, first).astype(BF16)


def volume_kernel(n_groups, rows_here, height, width, *refs):
    *query_refs, map_ref, coord_ref, decay_ref, out_ref = refs
    positions, channels = map_ref.shape
    factor = math.log2(math.e) / math.sqrt(channels)
    part_queries = query_refs[0].shape[0]
    n_parts = len(query_refs)
    group = part_queries * n_parts // n_groups
    feat_rows = out_ref.shape[1] - AUX_ROWS
    first_row = (lax.axis_index("space") * rows_here).astype(F32)
    tm = lax.axis_index("tm")
    chunk = pick_chunk(positions, 1280)
    state = [None] * n_parts
    for base in range(0, positions, chunk):
        keys = map_ref[base : base + chunk, :]
        values = jnp.concatenate([keys, coord_ref[base : base + chunk, :]], axis=1)
        for part in range(n_parts):
            scores = lax.dot_general(
                query_refs[part][...], keys, NT, preferred_element_type=F32
            )
            top = jnp.max(scores, axis=1, keepdims=True) * factor
            if state[part] is not None:
                old_top, old_sum = state[part]
                top = jnp.maximum(top, old_top)
            weights = jnp.exp2(scores * factor - top).astype(BF16)
            sums = jnp.dot(weights, values, preferred_element_type=F32)
            if state[part] is not None:
                sums = sums + jnp.exp2(old_top - top) * old_sum
            state[part] = (top, sums)
    decay = [decay_ref[...]]
    sub = lax.broadcasted_iota(jnp.int32, (AUX_ROWS, LANES), 0)
    for part in range(n_parts):
        top, sums = state[part]
        feats = sums[:, :channels] / sums[:, channels + 2 : channels + 3]
        extra = sums[:, channels:]
        lane = lax.broadcasted_iota(jnp.int32, extra.shape, 1)
        extra = jnp.transpose(jnp.where(lane == 3, top, extra))
        total = extra[2:3]
        rows = [extra[3:4]]
        rows += [total, extra[0:1] / total / width, (extra[1:2] / total + first_row) / height]
        aux = jnp.zeros((AUX_ROWS, part_queries), F32)
        wide = lax.broadcasted_iota(jnp.int32, aux.shape, 0)
        for index, values in enumerate(rows):
            aux = jnp.where(wide == index, values, aux)
        where = part if n_parts == 1 else jnp.where(tm == 0, part, 1 - part)
        groups_here = n_groups // n_parts
        for index in range(groups_here):
            shift = (part_queries - index * group) % part_queries
            block = pltpu.roll(aux, shift, 1) if shift else aux
            block = block[:, :LANES]
            for offset, piece in enumerate(decay):
                block = jnp.where(sub == len(rows) + offset, piece, block)
            pieces = [feats[index * group : (index + 1) * group]]
            if feat_rows > group:
                pieces.append(jnp.zeros((feat_rows - group, LANES), F32))
            pieces.append(block)
            out_ref[where * groups_here + index] = jnp.concatenate(pieces, axis=0).astype(
                out_ref.dtype
            )


def tail_kernel(n_tm, n_space, group, dw_ref, pw_ref, ow_ref, in_ref, out_ref):
    feat_rows = in_ref.shape[1] - AUX_ROWS
    n_blocks = n_tm * n_space
    blocks = [in_ref[index].astype(F32) for index in range(n_blocks)]
    aux = [block[feat_rows:] for block in blocks]
    positions, shares, decays = [], [], []
    for frame in range(n_tm):
        mine = aux[frame * n_space : (frame + 1) * n_space]
        top = mine[0][0:1]
        for block in mine[1:]:
            top = jnp.maximum(top, block[0:1])
        weight = [jnp.exp2(b[0:1] - top) * b[1:2] for b in mine]
        total = sum(weight[1:], weight[0])
        share = [w / total for w in weight]
        shares += share
        across = [s * b[2:3] for s, b in zip(share, mine)]
        down = [s * b[3:4] for s, b in zip(share, mine)]
        positions.append((sum(across[1:], across[0]), sum(down[1:], down[0])))
        decays.append(mine[0][4:5])
    pad_blocks = -(-n_blocks // 8) * 8
    table = jnp.zeros((pad_blocks, LANES), F32)
    sub = lax.broadcasted_iota(jnp.int32, table.shape, 0)
    for index, share in enumerate(shares):
        table = jnp.where(sub == index, share, table)
    table = jnp.transpose(table)
    attended = []
    for frame in range(n_tm):
        value = None
        for index in range(frame * n_space, (frame + 1) * n_space):
            term = table[:group, index : index + 1] * blocks[index][:group]
            value = term if value is None else value + term
        attended.append(value.astype(BF16).astype(F32))
    taps = dw_ref.shape[0]
    hidden = []
    for frame in range(n_tm):
        depth = None
        for tap in range(taps):
            source = frame + tap - taps // 2
            if 0 <= source < n_tm:
                term = dw_ref[tap : tap + 1, :] * attended[source]
                depth = term if depth is None else depth + term
        hidden.append(jax.nn.gelu(depth).astype(BF16).astype(F32))
    hidden = jnp.concatenate(hidden, axis=0).astype(BF16)
    mixed = jnp.dot(hidden, pw_ref[...], preferred_element_type=F32)
    memory = None
    out = jnp.zeros(out_ref.shape, F32)
    out_sub = lax.broadcasted_iota(jnp.int32, out.shape, 0)
    n_out = ow_ref.shape[0]
    for frame in range(n_tm):
        refined = attended[frame] + mixed[frame * group : (frame + 1) * group]
        fresh = (1.0 - decays[frame]) * refined
        memory = fresh if memory is None else decays[frame] * memory + fresh
        padded = memory
        if group < LANES:
            padded = jnp.concatenate([memory, jnp.zeros((LANES - group, LANES), F32)], axis=0)
        delta = lax.dot_general(
            ow_ref[...], padded, NT, preferred_element_type=F32, precision=lax.Precision.HIGHEST
        )
        for axis in range(n_out):
            line = positions[frame][axis] + delta[axis : axis + 1]
            out = jnp.where(out_sub == frame * n_out + axis, line, out)
    out_ref[...] = out


def call(kernel, out_shape, n_in, **cost):
    vmem = pl.BlockSpec(memory_space=pltpu.VMEM)
    return pl.pallas_call(
        kernel,
        out_shape=out_shape,
        in_specs=[vmem] * n_in,
        out_specs=jax.tree.map(lambda _: vmem, out_shape),
        compiler_params=pltpu.CompilerParams(vmem_limit_bytes=VMEM_LIMIT),
        cost_estimate=pl.CostEstimate(**cost),
    )


def hot_rows(target, map_ref, base, chunk):
    rows = target.shape[0]
    lane = lax.broadcasted_iota(jnp.int32, (rows, LANES), 1)
    parts = []
    for lane_base in range(base, base + chunk, LANES):
        parts.append(jnp.where(lane + lane_base == target, 1.0, 0.0).astype(BF16))
    hot = jnp.concatenate(parts, axis=1)
    return jnp.dot(hot, map_ref[base : base + chunk, :], preferred_element_type=F32)


def pick_kernel(core_flip, target_ref, map_ref, out_ref):
    half = target_ref.shape[1] // 2
    positions = map_ref.shape[0]
    chunk = pick_chunk(positions, 1536)
    second = lax.axis_index("tm") != core_flip
    target = jnp.where(second, target_ref[:, half:], target_ref[:, :half])
    target = jnp.transpose(jnp.broadcast_to(target, (LANES, half)))
    picked = None
    for base in range(0, positions, chunk):
        term = hot_rows(target, map_ref, base, chunk)
        picked = term if picked is None else picked + term
    out_ref[...] = picked.astype(BF16)


def coord_kernel(map_width, after_ref, out_ref):
    positions = out_ref.shape[0]
    chunk = pick_chunk(positions, 512)
    lane = lax.broadcasted_iota(jnp.int32, (chunk, LANES), 1)
    local_place = lax.broadcasted_iota(jnp.int32, (chunk, LANES), 0).astype(F32)

    @pl.loop(0, positions // chunk)
    def _(step):
        place = local_place + (step * chunk).astype(F32)
        row = jnp.floor((place + 0.5) * (1.0 / map_width))
        rest = jnp.where(lane == 2, 1.0, 0.0)
        value = jnp.where(lane == 0, place - row * map_width, jnp.where(lane == 1, row, rest))
        out_ref[pl.ds(pl.multiple_of(step * chunk, chunk), chunk), :] = value.astype(BF16)


def turn_kernel(map_ref, after_ref, out_ref):
    positions = map_ref.shape[0]
    chunk = pick_chunk(positions, 768)
    for base in range(0, positions, chunk):
        rows = map_ref[base : base + chunk, :].astype(F32)
        out_ref[:, base : base + chunk] = jnp.transpose(rows).astype(BF16)


def split(value):
    pieces = []
    for _ in range(3):
        piece = value.astype(BF16).astype(F32)
        pieces.append(piece)
        value = value - piece
    return pieces


def half_kernel(rows_here, height, width, query_ref, map_ref, turned_ref, coord_ref, out_ref):
    positions, channels = map_ref.shape
    factor = math.log2(math.e) / math.sqrt(channels)
    query = query_ref[...]
    first_row = (lax.axis_index("space") * rows_here).astype(F32)
    chunk = pick_chunk(positions, 1280)

    def score(base):
        keys = turned_ref[:, base : base + chunk]
        return jnp.dot(query, keys, preferred_element_type=F32)

    top = sums = None
    ahead = score(0)
    for base in range(0, positions, chunk):
        scores = ahead
        if base + chunk < positions:
            ahead = score(base + chunk)
        window = slice(base, base + chunk)
        values = jnp.concatenate([map_ref[window, :], coord_ref[window, :]], axis=1)
        new_top = jnp.max(scores, axis=1, keepdims=True) * factor
        if top is not None:
            new_top = jnp.maximum(new_top, top)
        weights = jnp.exp2(scores * factor - new_top).astype(BF16)
        terms = jnp.dot(weights, values, preferred_element_type=F32)
        sums = terms if sums is None else terms + jnp.exp2(top - new_top) * sums
        top = new_top
    feats = sums[:, :channels] / sums[:, channels + 2 : channels + 3]
    extra = sums[:, channels:]
    lane = lax.broadcasted_iota(jnp.int32, extra.shape, 1)
    extra = jnp.transpose(jnp.where(lane == 3, top, extra))
    total = extra[2:3]
    across = extra[0:1] / total / width
    down = (extra[1:2] / total + first_row) / height
    store_block(out_ref, feats, [extra[3:4], total, across, down])


def store_block(out_ref, feats, lines):
    queries = feats.shape[0]
    out_ref[:queries, :] = feats
    rows = [piece for line in lines for piece in split(line)]
    sub = lax.broadcasted_iota(jnp.int32, (PIECE_ROWS, queries), 0)
    aux = jnp.zeros((PIECE_ROWS, queries), F32)
    for index, row in enumerate(rows):
        aux = jnp.where(sub == index, row, aux)
    for tile in range(queries // LANES):
        base = queries + tile * PIECE_ROWS
        out_ref[base : base + PIECE_ROWS, :] = aux[:, tile * LANES : (tile + 1) * LANES]


def merged(bit, own_ref, came_ref):
    queries = own_ref.shape[0] * LANES // (LANES + PIECE_ROWS)
    high = (lax.axis_index("space") & bit) != 0
    own, came = own_ref[...].astype(F32), came_ref[...].astype(F32)
    pair = [jnp.where(high, came, own), jnp.where(high, own, came)]
    feats, lines = [], []
    for tile in range(queries // LANES):
        base = queries + tile * PIECE_ROWS
        parts = []
        for block in pair:
            aux = block[base : base + PIECE_ROWS]
            parts.append(
                [aux[i : i + 1] + aux[i + 1 : i + 2] + aux[i + 2 : i + 3] for i in (0, 3, 6, 9)]
            )
        (top_a, total_a, *place_a), (top_b, total_b, *place_b) = parts
        top = jnp.maximum(top_a, top_b)
        weight_a, weight_b = jnp.exp2(top_a - top) * total_a, jnp.exp2(top_b - top) * total_b
        total = weight_a + weight_b
        share_a, share_b = weight_a / total, weight_b / total
        places = [share_a * a + share_b * b for a, b in zip(place_a, place_b)]
        lines.append([top, total, *places])
        sub = lax.broadcasted_iota(jnp.int32, (8, LANES), 0)
        table = jnp.transpose(jnp.where(sub == 0, share_a, jnp.where(sub == 1, share_b, 0.0)))
        window = slice(tile * LANES, (tile + 1) * LANES)
        feats.append(table[:, 0:1] * pair[0][window] + table[:, 1:2] * pair[1][window])
    return jnp.concatenate(feats, axis=0), [jnp.concatenate(v, axis=1) for v in zip(*lines)]


def my_bit(step, n_space):
    bits = n_space.bit_length() - 1
    return jnp.left_shift(1, lax.rem(lax.axis_index("tm") + step, bits))


def merge_kernel(n_space, step, own_ref, came_ref, out_ref):
    store_block(out_ref, *merged(my_bit(step, n_space), own_ref, came_ref))


def last_merge_kernel(n_space, step, decay_ref, near_own, near_came, far_own, far_came, *outs):
    out_ref, place_ref = outs
    bit = my_bit(step, n_space)
    base = 0
    for own_ref, came_ref in ((near_own, near_came), (far_own, far_came)):
        feats, lines = merged(bit, own_ref, came_ref)
        window = slice(base, base + feats.shape[0])
        out_ref[window, :] = feats.astype(BF16)
        place_ref[0:1, window] = lines[2]
        place_ref[1:2, window] = lines[3]
        base += feats.shape[0]
    sub = lax.broadcasted_iota(jnp.int32, (PIECE_ROWS, LANES), 0)
    rows = jnp.zeros((PIECE_ROWS, LANES), F32)
    for index, piece in enumerate(split(decay_ref[...])):
        rows = jnp.where(sub == index, piece, rows)
    out_ref[base:, :] = rows.astype(BF16)


def track_kernel(dw_ref, pw_ref, ow_ref, place_ref, mine_ref, theirs_ref, out_ref):
    early = lax.axis_index("tm") == 0
    queries = place_ref.shape[1]
    half = queries // 2
    mine, theirs = mine_ref[...].astype(F32), theirs_ref[...].astype(F32)

    def retention(rows):
        return rows[queries : queries + 1] + rows[queries + 1 : queries + 2] + rows[queries + 2 : queries + 3]

    decay_mine, decay_theirs = retention(mine), retention(theirs)
    mine = mine[:queries]
    theirs = jnp.concatenate([theirs[half:queries], theirs[:half]], axis=0)
    attended = [jnp.where(early, mine, theirs), jnp.where(early, theirs, mine)]
    decay = [
        jnp.where(early, decay_mine, decay_theirs),
        jnp.where(early, decay_theirs, decay_mine),
    ]
    taps = dw_ref.shape[0]
    refined = []
    for frame in range(2):
        depth = None
        for tap in range(taps):
            source = frame + tap - taps // 2
            if 0 <= source < 2:
                term = dw_ref[tap : tap + 1, :] * attended[source]
                depth = term if depth is None else depth + term
        hidden = jax.nn.gelu(depth).astype(BF16)
        mixed = jnp.dot(hidden, pw_ref[...], preferred_element_type=F32)
        refined.append(attended[frame] + mixed)
    first = (1.0 - decay[0]) * refined[0]
    second = decay[1] * first + (1.0 - decay[1]) * refined[1]
    memory = jnp.where(early, first, second)
    delta = lax.dot_general(
        ow_ref[...], memory, NT, preferred_element_type=F32, precision=lax.Precision.HIGHEST
    )
    line = place_ref[...] + delta
    low, high = line[:, :half], line[:, half:]
    out_ref[0, :, :half] = jnp.where(early, low, high)
    out_ref[0, :, half:] = jnp.where(early, high, low)


def swap(value, axis, bit):
    return lax.ppermute(value, axis, [(i, i ^ bit) for i in range(lax.axis_size(axis))])


def all_sum(value, axis):
    count = lax.axis_size(axis)
    if count & (count - 1):
        return lax.psum(value, axis)
    bit = 1
    while bit < count:
        value = value + swap(value, axis, bit)
        bit *= 2
    return value


def local_general(
    feature_maps, query_frame, query_row, query_col, ema_decay, dw_kernel, pw_weight, out_weight
):
    frames_here, rows_here, map_width, channels = feature_maps.shape
    assert frames_here == 1 and channels == LANES
    queries = query_frame.shape[0]
    n_tm, n_space = lax.axis_size("tm"), lax.axis_size("space")
    n_groups = n_tm * n_space
    group = queries // n_groups
    height = rows_here * n_space
    positions = rows_here * map_width
    maps = feature_maps.reshape(positions, channels)
    halves = 2 if n_tm == 2 else 1
    part = jax.ShapeDtypeStruct((queries // halves, channels), BF16)

    picked = call(
        functools.partial(gather_kernel, rows_here, map_width),
        [part] * halves,
        4,
        flops=2 * queries * positions * channels,
        bytes_accessed=2 * positions * channels,
        transcendentals=0,
    )(query_frame[None], query_row[None], query_col[None], maps)

    place = jnp.arange(positions, dtype=jnp.int32)[:, None]
    lane = jnp.arange(LANES, dtype=jnp.int32)[None, :]
    coords = jnp.where(
        lane == 0,
        place % map_width,
        jnp.where(lane == 1, place // map_width, jnp.where(lane == 2, 1, 0)),
    ).astype(BF16)

    if halves == 2:
        mine = picked[0] + swap(picked[1], "tm", 1)
        mine = all_sum(mine, "space")
        feats = [mine, swap(mine, "tm", 1)]
    else:
        feats = [all_sum(all_sum(picked[0], "tm"), "space")]

    feat_rows = -(-group // 8) * 8
    blocks = call(
        functools.partial(volume_kernel, n_groups, rows_here, height, map_width),
        jax.ShapeDtypeStruct((n_groups, feat_rows + AUX_ROWS, LANES), F32),
        halves + 3,
        flops=6 * queries * positions * channels,
        bytes_accessed=4 * positions * channels,
        transcendentals=queries * positions,
    )(*feats, maps, coords, ema_decay)

    blocks = lax.all_to_all(blocks, ("tm", "space"), 0, 0, tiled=True)

    n_out = out_weight.shape[0]
    out_rows = -(-n_tm * n_out // 8) * 8
    lines = call(
        functools.partial(tail_kernel, n_tm, n_space, group),
        jax.ShapeDtypeStruct((out_rows, LANES), F32),
        4,
        flops=2 * n_tm * group * channels * channels,
        bytes_accessed=4 * n_groups * (feat_rows + AUX_ROWS) * LANES,
        transcendentals=n_tm * group * channels,
    )(dw_kernel, pw_weight, out_weight, blocks)

    lines = lax.all_gather(lines, ("tm", "space"), axis=0)
    own = lax.dynamic_slice_in_dim(lines, lax.axis_index("tm") * n_out, n_out, axis=1)
    own = own[:, :, :group]
    return jnp.transpose(own, (1, 0, 2)).reshape(1, n_out, queries)


def core_swap(value):
    return lax.ppermute(value, "tm", [(0, 1), (1, 0)])


def space_swap(value, step):
    n_space = lax.axis_size("space")
    bits = n_space.bit_length() - 1
    pairs = []
    for tm in range(2):
        for space in range(n_space):
            to = space ^ (1 << (tm + step) % bits)
            pairs.append((tm * n_space + space, tm * n_space + to))
    return lax.ppermute(value, ("tm", "space"), pairs)


def local_pair(
    feature_maps, query_frame, query_row, query_col, ema_decay, dw_kernel, pw_weight, out_weight
):
    _, rows_here, map_width, channels = feature_maps.shape
    queries = query_frame.shape[0]
    n_space = lax.axis_size("space")
    half = queries // 2
    height = rows_here * n_space
    positions = rows_here * map_width
    maps = feature_maps.reshape(positions, channels)

    row = query_row - lax.axis_index("space") * rows_here
    here = (query_frame == lax.axis_index("tm")) & (row >= 0) & (row < rows_here)
    target = jnp.where(here, row * map_width + query_col, -1)[None]

    def pick(core_flip):
        return call(
            functools.partial(pick_kernel, core_flip),
            jax.ShapeDtypeStruct((half, channels), BF16),
            2,
            flops=queries * positions * channels,
            bytes_accessed=2 * positions * channels,
            transcendentals=0,
        )(target, maps)

    arrived = core_swap(pick(1))
    coords = call(
        functools.partial(coord_kernel, map_width),
        jax.ShapeDtypeStruct((positions, LANES), BF16),
        1,
        flops=8 * positions * LANES,
        bytes_accessed=2 * positions * LANES,
        transcendentals=0,
    )(target)
    keep = pick(0)
    turned = call(
        turn_kernel,
        jax.ShapeDtypeStruct((channels, positions), BF16),
        2,
        flops=8 * positions * LANES,
        bytes_accessed=4 * positions * LANES,
        transcendentals=0,
    )(maps, keep)
    mine = keep + arrived
    steps = n_space.bit_length() - 1
    for step in range(steps):
        mine = mine + space_swap(mine, step)
        mine, turned = lax.optimization_barrier((mine, turned))
    theirs = core_swap(mine)

    block = jax.ShapeDtypeStruct((half + half // LANES * PIECE_ROWS, LANES), F32)

    def blocks_of(feats):
        return call(
            functools.partial(half_kernel, rows_here, height, map_width),
            block,
            4,
            flops=3 * queries * positions * channels,
            bytes_accessed=4 * positions * channels,
            transcendentals=half * positions,
        )(feats, maps, turned, coords)

    def sent(value, step):
        value = lax.optimization_barrier(value.astype(jnp.float16))
        return value.astype(F32), space_swap(value, step).astype(F32)

    def merge(pair, step):
        return call(
            functools.partial(merge_kernel, n_space, step),
            block,
            2,
            flops=0,
            bytes_accessed=0,
            transcendentals=0,
        )(*pair)

    pairs = [sent(blocks_of(mine), 0), sent(blocks_of(theirs), 0)]
    for step in range(1, steps):
        pairs = [sent(merge(pair, step - 1), step) for pair in pairs]

    n_out = out_weight.shape[0]
    attended, place = call(
        functools.partial(last_merge_kernel, n_space, steps - 1),
        [
            jax.ShapeDtypeStruct((queries + PIECE_ROWS, LANES), BF16),
            jax.ShapeDtypeStruct((n_out, queries), F32),
        ],
        5,
        flops=4 * queries * channels,
        bytes_accessed=12 * queries * channels,
        transcendentals=0,
    )(ema_decay, *pairs[0], *pairs[1])
    return call(
        track_kernel,
        jax.ShapeDtypeStruct((1, n_out, queries), F32),
        6,
        flops=8 * queries * channels * channels,
        bytes_accessed=8 * queries * channels,
        transcendentals=2 * queries * channels,
    )(dw_kernel, pw_weight, out_weight, place, attended, core_swap(attended))


def local(feature_maps, query_frame, *rest):
    n_tm, n_space = lax.axis_size("tm"), lax.axis_size("space")
    paired = n_tm == 2 and n_space > 1 and n_space & (n_space - 1) == 0
    if paired and query_frame.shape[0] % (2 * LANES) == 0:
        return local_pair(feature_maps, query_frame, *rest)
    return local_general(feature_maps, query_frame, *rest)


def solution(mesh):
    placed = (
        P(("video", "tm"), "space", None, None),
        P("video"),
        P("video"),
        P("video"),
        P(("video", "tm"), None),
        P(),
        P(),
        P(),
    )
    return jax.shard_map(
        local, mesh=mesh, in_specs=placed, out_specs=P(("video", "tm"), None, None), check_vma=False
    )
```

```python
import functools
import math

import jax
import jax.numpy as jnp
from jax import lax
from jax.experimental import pallas as pl
from jax.experimental.pallas import tpu as pltpu
from jax.sharding import PartitionSpec as P

F32 = jnp.float32
BF16 = jnp.bfloat16
LANES = 128
AUX_ROWS = 8
PIECE_ROWS = 16
VMEM_LIMIT = 40 * 1024 * 1024
NT = (((1,), (1,)), ((), ()))


def pick_chunk(total, limit):
    best = None
    for size in range(LANES, limit + 1, LANES):
        if total % size == 0 and (best is None or size % 256 == 0 or best % 256):
            best = size
    return best if best is not None else total


def gather_kernel(rows_here, map_width, frame_ref, row_ref, col_ref, map_ref, *out_refs):
    positions = map_ref.shape[0]
    queries = frame_ref.shape[1]
    tm = lax.axis_index("tm")
    row = row_ref[...] - lax.axis_index("space") * rows_here
    here = (frame_ref[...] == tm) & (row >= 0) & (row < rows_here)
    target = jnp.where(here, row * map_width + col_ref[...], -1)
    target = jnp.transpose(jnp.broadcast_to(target, (LANES, queries)))
    chunk = pick_chunk(positions, 1536)
    picked = None
    for base in range(0, positions, chunk):
        parts = []
        for lane_base in range(base, base + chunk, LANES):
            lane = lax.broadcasted_iota(jnp.int32, (queries, LANES), 1) + lane_base
            parts.append(jnp.where(lane == target, 1.0, 0.0).astype(BF16))
        hot = jnp.concatenate(parts, axis=1)
        term = jnp.dot(hot, map_ref[base : base + chunk, :], preferred_element_type=F32)
        picked = term if picked is None else picked + term
    if len(out_refs) == 1:
        out_refs[0][...] = picked.astype(BF16)
        return
    half = queries // 2
    first, second = picked[:half].astype(F32), picked[half:].astype(F32)
    out_refs[0][...] = jnp.where(tm == 0, first, second).astype(BF16)
    out_refs[1][...] = jnp.where(tm == 0, second, first).astype(BF16)


def volume_kernel(n_groups, rows_here, height, width, *refs):
    *query_refs, map_ref, coord_ref, decay_ref, out_ref = refs
    positions, channels = map_ref.shape
    factor = math.log2(math.e) / math.sqrt(channels)
    part_queries = query_refs[0].shape[0]
    n_parts = len(query_refs)
    group = part_queries * n_parts // n_groups
    feat_rows = out_ref.shape[1] - AUX_ROWS
    first_row = (lax.axis_index("space") * rows_here).astype(F32)
    tm = lax.axis_index("tm")
    chunk = pick_chunk(positions, 1280)
    state = [None] * n_parts
    for base in range(0, positions, chunk):
        keys = map_ref[base : base + chunk, :]
        values = jnp.concatenate([keys, coord_ref[base : base + chunk, :]], axis=1)
        for part in range(n_parts):
            scores = lax.dot_general(
                query_refs[part][...], keys, NT, preferred_element_type=F32
            )
            top = jnp.max(scores, axis=1, keepdims=True) * factor
            if state[part] is not None:
                old_top, old_sum = state[part]
                top = jnp.maximum(top, old_top)
            weights = jnp.exp2(scores * factor - top).astype(BF16)
            sums = jnp.dot(weights, values, preferred_element_type=F32)
            if state[part] is not None:
                sums = sums + jnp.exp2(old_top - top) * old_sum
            state[part] = (top, sums)
    decay = [decay_ref[...]]
    sub = lax.broadcasted_iota(jnp.int32, (AUX_ROWS, LANES), 0)
    for part in range(n_parts):
        top, sums = state[part]
        feats = sums[:, :channels] / sums[:, channels + 2 : channels + 3]
        extra = sums[:, channels:]
        lane = lax.broadcasted_iota(jnp.int32, extra.shape, 1)
        extra = jnp.transpose(jnp.where(lane == 3, top, extra))
        total = extra[2:3]
        rows = [extra[3:4]]
        rows += [total, extra[0:1] / total / width, (extra[1:2] / total + first_row) / height]
        aux = jnp.zeros((AUX_ROWS, part_queries), F32)
        wide = lax.broadcasted_iota(jnp.int32, aux.shape, 0)
        for index, values in enumerate(rows):
            aux = jnp.where(wide == index, values, aux)
        where = part if n_parts == 1 else jnp.where(tm == 0, part, 1 - part)
        groups_here = n_groups // n_parts
        for index in range(groups_here):
            shift = (part_queries - index * group) % part_queries
            block = pltpu.roll(aux, shift, 1) if shift else aux
            block = block[:, :LANES]
            for offset, piece in enumerate(decay):
                block = jnp.where(sub == len(rows) + offset, piece, block)
            pieces = [feats[index * group : (index + 1) * group]]
            if feat_rows > group:
                pieces.append(jnp.zeros((feat_rows - group, LANES), F32))
            pieces.append(block)
            out_ref[where * groups_here + index] = jnp.concatenate(pieces, axis=0).astype(
                out_ref.dtype
            )


def tail_kernel(n_tm, n_space, group, dw_ref, pw_ref, ow_ref, in_ref, out_ref):
    feat_rows = in_ref.shape[1] - AUX_ROWS
    n_blocks = n_tm * n_space
    blocks = [in_ref[index].astype(F32) for index in range(n_blocks)]
    aux = [block[feat_rows:] for block in blocks]
    positions, shares, decays = [], [], []
    for frame in range(n_tm):
        mine = aux[frame * n_space : (frame + 1) * n_space]
        top = mine[0][0:1]
        for block in mine[1:]:
            top = jnp.maximum(top, block[0:1])
        weight = [jnp.exp2(b[0:1] - top) * b[1:2] for b in mine]
        total = sum(weight[1:], weight[0])
        share = [w / total for w in weight]
        shares += share
        across = [s * b[2:3] for s, b in zip(share, mine)]
        down = [s * b[3:4] for s, b in zip(share, mine)]
        positions.append((sum(across[1:], across[0]), sum(down[1:], down[0])))
        decays.append(mine[0][4:5])
    pad_blocks = -(-n_blocks // 8) * 8
    table = jnp.zeros((pad_blocks, LANES), F32)
    sub = lax.broadcasted_iota(jnp.int32, table.shape, 0)
    for index, share in enumerate(shares):
        table = jnp.where(sub == index, share, table)
    table = jnp.transpose(table)
    attended = []
    for frame in range(n_tm):
        value = None
        for index in range(frame * n_space, (frame + 1) * n_space):
            term = table[:group, index : index + 1] * blocks[index][:group]
            value = term if value is None else value + term
        attended.append(value.astype(BF16).astype(F32))
    taps = dw_ref.shape[0]
    hidden = []
    for frame in range(n_tm):
        depth = None
        for tap in range(taps):
            source = frame + tap - taps // 2
            if 0 <= source < n_tm:
                term = dw_ref[tap : tap + 1, :] * attended[source]
                depth = term if depth is None else depth + term
        hidden.append(jax.nn.gelu(depth).astype(BF16).astype(F32))
    hidden = jnp.concatenate(hidden, axis=0).astype(BF16)
    mixed = jnp.dot(hidden, pw_ref[...], preferred_element_type=F32)
    memory = None
    out = jnp.zeros(out_ref.shape, F32)
    out_sub = lax.broadcasted_iota(jnp.int32, out.shape, 0)
    n_out = ow_ref.shape[0]
    for frame in range(n_tm):
        refined = attended[frame] + mixed[frame * group : (frame + 1) * group]
        fresh = (1.0 - decays[frame]) * refined
        memory = fresh if memory is None else decays[frame] * memory + fresh
        padded = memory
        if group < LANES:
            padded = jnp.concatenate([memory, jnp.zeros((LANES - group, LANES), F32)], axis=0)
        delta = lax.dot_general(
            ow_ref[...], padded, NT, preferred_element_type=F32, precision=lax.Precision.HIGHEST
        )
        for axis in range(n_out):
            line = positions[frame][axis] + delta[axis : axis + 1]
            out = jnp.where(out_sub == frame * n_out + axis, line, out)
    out_ref[...] = out


def call(kernel, out_shape, n_in, **cost):
    vmem = pl.BlockSpec(memory_space=pltpu.VMEM)
    return pl.pallas_call(
        kernel,
        out_shape=out_shape,
        in_specs=[vmem] * n_in,
        out_specs=jax.tree.map(lambda _: vmem, out_shape),
        compiler_params=pltpu.CompilerParams(vmem_limit_bytes=VMEM_LIMIT),
        cost_estimate=pl.CostEstimate(**cost),
    )


def hot_rows(target, map_ref, base, chunk):
    rows = target.shape[0]
    lane = lax.broadcasted_iota(jnp.int32, (rows, LANES), 1)
    parts = []
    for lane_base in range(base, base + chunk, LANES):
        parts.append(jnp.where(lane + lane_base == target, 1.0, 0.0).astype(BF16))
    hot = jnp.concatenate(parts, axis=1)
    return jnp.dot(hot, map_ref[base : base + chunk, :], preferred_element_type=F32)


def pick_kernel(core_flip, target_ref, map_ref, out_ref):
    half = target_ref.shape[1] // 2
    positions = map_ref.shape[0]
    chunk = pick_chunk(positions, 1536)
    second = lax.axis_index("tm") != core_flip
    target = jnp.where(second, target_ref[:, half:], target_ref[:, :half])
    target = jnp.transpose(jnp.broadcast_to(target, (LANES, half)))
    picked = None
    for base in range(0, positions, chunk):
        term = hot_rows(target, map_ref, base, chunk)
        picked = term if picked is None else picked + term
    out_ref[...] = picked.astype(BF16)


def coord_kernel(map_width, out_ref):
    positions = out_ref.shape[0]
    chunk = pick_chunk(positions, 512)
    lane = lax.broadcasted_iota(jnp.int32, (chunk, LANES), 1)
    local_place = lax.broadcasted_iota(jnp.int32, (chunk, LANES), 0).astype(F32)

    @pl.loop(0, positions // chunk)
    def _(step):
        place = local_place + (step * chunk).astype(F32)
        row = jnp.floor((place + 0.5) * (1.0 / map_width))
        rest = jnp.where(lane == 2, 1.0, 0.0)
        value = jnp.where(lane == 0, place - row * map_width, jnp.where(lane == 1, row, rest))
        out_ref[pl.ds(pl.multiple_of(step * chunk, chunk), chunk), :] = value.astype(BF16)


def split(value):
    pieces = []
    for _ in range(3):
        piece = value.astype(BF16).astype(F32)
        pieces.append(piece)
        value = value - piece
    return pieces


def half_kernel(rows_here, height, width, query_ref, map_ref, coord_ref, out_ref):
    positions, channels = map_ref.shape
    factor = math.log2(math.e) / math.sqrt(channels)
    query = query_ref[...]
    first_row = (lax.axis_index("space") * rows_here).astype(F32)
    chunk = pick_chunk(positions, 2560)

    def score(base):
        keys = map_ref[base : base + chunk, :]
        return lax.dot_general(query, keys, NT, preferred_element_type=F32)

    top = sums = None
    ahead = score(0)
    for base in range(0, positions, chunk):
        scores = ahead
        if base + chunk < positions:
            ahead = score(base + chunk)
        window = slice(base, base + chunk)
        values = jnp.concatenate([map_ref[window, :], coord_ref[window, :]], axis=1)
        new_top = jnp.max(scores, axis=1, keepdims=True) * factor
        if top is not None:
            new_top = jnp.maximum(new_top, top)
        weights = jnp.exp2(scores * factor - new_top).astype(BF16)
        terms = jnp.dot(weights, values, preferred_element_type=F32)
        sums = terms if sums is None else terms + jnp.exp2(top - new_top) * sums
        top = new_top
    feats = sums[:, :channels] / sums[:, channels + 2 : channels + 3]
    extra = sums[:, channels:]
    lane = lax.broadcasted_iota(jnp.int32, extra.shape, 1)
    extra = jnp.transpose(jnp.where(lane == 3, top, extra))
    total = extra[2:3]
    across = extra[0:1] / total / width
    down = (extra[1:2] / total + first_row) / height
    store_block(out_ref, feats, [extra[3:4], total, across, down])


def store_block(out_ref, feats, lines):
    queries = feats.shape[0]
    out_ref[:queries, :] = feats
    rows = [piece for line in lines for piece in split(line)]
    sub = lax.broadcasted_iota(jnp.int32, (PIECE_ROWS, queries), 0)
    aux = jnp.zeros((PIECE_ROWS, queries), F32)
    for index, row in enumerate(rows):
        aux = jnp.where(sub == index, row, aux)
    for tile in range(queries // LANES):
        base = queries + tile * PIECE_ROWS
        out_ref[base : base + PIECE_ROWS, :] = aux[:, tile * LANES : (tile + 1) * LANES]


def merged(bit, own_ref, came_ref):
    queries = own_ref.shape[0] * LANES // (LANES + PIECE_ROWS)
    high = (lax.axis_index("space") & bit) != 0
    own, came = own_ref[...].astype(F32), came_ref[...].astype(F32)
    pair = [jnp.where(high, came, own), jnp.where(high, own, came)]
    feats, lines = [], []
    for tile in range(queries // LANES):
        base = queries + tile * PIECE_ROWS
        parts = []
        for block in pair:
            aux = block[base : base + PIECE_ROWS]
            parts.append(
                [aux[i : i + 1] + aux[i + 1 : i + 2] + aux[i + 2 : i + 3] for i in (0, 3, 6, 9)]
            )
        (top_a, total_a, *place_a), (top_b, total_b, *place_b) = parts
        top = jnp.maximum(top_a, top_b)
        weight_a, weight_b = jnp.exp2(top_a - top) * total_a, jnp.exp2(top_b - top) * total_b
        total = weight_a + weight_b
        share_a, share_b = weight_a / total, weight_b / total
        places = [share_a * a + share_b * b for a, b in zip(place_a, place_b)]
        lines.append([top, total, *places])
        sub = lax.broadcasted_iota(jnp.int32, (8, LANES), 0)
        table = jnp.transpose(jnp.where(sub == 0, share_a, jnp.where(sub == 1, share_b, 0.0)))
        window = slice(tile * LANES, (tile + 1) * LANES)
        feats.append(table[:, 0:1] * pair[0][window] + table[:, 1:2] * pair[1][window])
    return jnp.concatenate(feats, axis=0), [jnp.concatenate(v, axis=1) for v in zip(*lines)]


def my_bit(step, n_space):
    bits = n_space.bit_length() - 1
    return jnp.left_shift(1, lax.rem(lax.axis_index("tm") + step, bits))


def merge_kernel(n_space, step, own_ref, came_ref, out_ref):
    store_block(out_ref, *merged(my_bit(step, n_space), own_ref, came_ref))


def last_merge_kernel(n_space, step, decay_ref, near_own, near_came, far_own, far_came, *outs):
    out_ref, place_ref = outs
    bit = my_bit(step, n_space)
    base = 0
    for own_ref, came_ref in ((near_own, near_came), (far_own, far_came)):
        feats, lines = merged(bit, own_ref, came_ref)
        window = slice(base, base + feats.shape[0])
        out_ref[window, :] = feats.astype(BF16)
        place_ref[0:1, window] = lines[2]
        place_ref[1:2, window] = lines[3]
        base += feats.shape[0]
    sub = lax.broadcasted_iota(jnp.int32, (PIECE_ROWS, LANES), 0)
    rows = jnp.zeros((PIECE_ROWS, LANES), F32)
    for index, piece in enumerate(split(decay_ref[...])):
        rows = jnp.where(sub == index, piece, rows)
    out_ref[base:, :] = rows.astype(BF16)


def track_kernel(dw_ref, pw_ref, ow_ref, place_ref, mine_ref, theirs_ref, out_ref):
    early = lax.axis_index("tm") == 0
    queries = place_ref.shape[1]
    half = queries // 2
    mine, theirs = mine_ref[...].astype(F32), theirs_ref[...].astype(F32)

    def retention(rows):
        return rows[queries : queries + 1] + rows[queries + 1 : queries + 2] + rows[queries + 2 : queries + 3]

    decay_mine, decay_theirs = retention(mine), retention(theirs)
    mine = mine[:queries]
    theirs = jnp.concatenate([theirs[half:queries], theirs[:half]], axis=0)
    attended = [jnp.where(early, mine, theirs), jnp.where(early, theirs, mine)]
    decay = [
        jnp.where(early, decay_mine, decay_theirs),
        jnp.where(early, decay_theirs, decay_mine),
    ]
    taps = dw_ref.shape[0]
    refined = []
    for frame in range(2):
        depth = None
        for tap in range(taps):
            source = frame + tap - taps // 2
            if 0 <= source < 2:
                term = dw_ref[tap : tap + 1, :] * attended[source]
                depth = term if depth is None else depth + term
        hidden = jax.nn.gelu(depth).astype(BF16)
        mixed = jnp.dot(hidden, pw_ref[...], preferred_element_type=F32)
        refined.append(attended[frame] + mixed)
    first = (1.0 - decay[0]) * refined[0]
    second = decay[1] * first + (1.0 - decay[1]) * refined[1]
    memory = jnp.where(early, first, second)
    n_out = ow_ref.shape[0]
    weights = jnp.concatenate(split(ow_ref[...]), axis=0).astype(BF16)
    line = place_ref[...]
    for piece in split(memory)[:2]:
        terms = lax.dot_general(weights, piece.astype(BF16), NT, preferred_element_type=F32)
        line = line + terms[:n_out] + terms[n_out : 2 * n_out] + terms[2 * n_out :]
    low, high = line[:, :half], line[:, half:]
    out_ref[0, :, :half] = jnp.where(early, low, high)
    out_ref[0, :, half:] = jnp.where(early, high, low)


def swap(value, axis, bit):
    return lax.ppermute(value, axis, [(i, i ^ bit) for i in range(lax.axis_size(axis))])


def all_sum(value, axis):
    count = lax.axis_size(axis)
    if count & (count - 1):
        return lax.psum(value, axis)
    bit = 1
    while bit < count:
        value = value + swap(value, axis, bit)
        bit *= 2
    return value


def local_general(
    feature_maps, query_frame, query_row, query_col, ema_decay, dw_kernel, pw_weight, out_weight
):
    frames_here, rows_here, map_width, channels = feature_maps.shape
    assert frames_here == 1 and channels == LANES
    queries = query_frame.shape[0]
    n_tm, n_space = lax.axis_size("tm"), lax.axis_size("space")
    n_groups = n_tm * n_space
    group = queries // n_groups
    height = rows_here * n_space
    positions = rows_here * map_width
    maps = feature_maps.reshape(positions, channels)
    halves = 2 if n_tm == 2 else 1
    part = jax.ShapeDtypeStruct((queries // halves, channels), BF16)

    picked = call(
        functools.partial(gather_kernel, rows_here, map_width),
        [part] * halves,
        4,
        flops=2 * queries * positions * channels,
        bytes_accessed=2 * positions * channels,
        transcendentals=0,
    )(query_frame[None], query_row[None], query_col[None], maps)

    place = jnp.arange(positions, dtype=jnp.int32)[:, None]
    lane = jnp.arange(LANES, dtype=jnp.int32)[None, :]
    coords = jnp.where(
        lane == 0,
        place % map_width,
        jnp.where(lane == 1, place // map_width, jnp.where(lane == 2, 1, 0)),
    ).astype(BF16)

    if halves == 2:
        mine = picked[0] + swap(picked[1], "tm", 1)
        mine = all_sum(mine, "space")
        feats = [mine, swap(mine, "tm", 1)]
    else:
        feats = [all_sum(all_sum(picked[0], "tm"), "space")]

    feat_rows = -(-group // 8) * 8
    blocks = call(
        functools.partial(volume_kernel, n_groups, rows_here, height, map_width),
        jax.ShapeDtypeStruct((n_groups, feat_rows + AUX_ROWS, LANES), F32),
        halves + 3,
        flops=6 * queries * positions * channels,
        bytes_accessed=4 * positions * channels,
        transcendentals=queries * positions,
    )(*feats, maps, coords, ema_decay)

    blocks = lax.all_to_all(blocks, ("tm", "space"), 0, 0, tiled=True)

    n_out = out_weight.shape[0]
    out_rows = -(-n_tm * n_out // 8) * 8
    lines = call(
        functools.partial(tail_kernel, n_tm, n_space, group),
        jax.ShapeDtypeStruct((out_rows, LANES), F32),
        4,
        flops=2 * n_tm * group * channels * channels,
        bytes_accessed=4 * n_groups * (feat_rows + AUX_ROWS) * LANES,
        transcendentals=n_tm * group * channels,
    )(dw_kernel, pw_weight, out_weight, blocks)

    lines = lax.all_gather(lines, ("tm", "space"), axis=0)
    own = lax.dynamic_slice_in_dim(lines, lax.axis_index("tm") * n_out, n_out, axis=1)
    own = own[:, :, :group]
    return jnp.transpose(own, (1, 0, 2)).reshape(1, n_out, queries)


def core_swap(value):
    return lax.ppermute(value, "tm", [(0, 1), (1, 0)])


def space_swap(value, step):
    n_space = lax.axis_size("space")
    bits = n_space.bit_length() - 1
    pairs = []
    for tm in range(2):
        for space in range(n_space):
            to = space ^ (1 << (tm + step) % bits)
            pairs.append((tm * n_space + space, tm * n_space + to))
    return lax.ppermute(value, ("tm", "space"), pairs)


def local_pair(
    feature_maps, query_frame, query_row, query_col, ema_decay, dw_kernel, pw_weight, out_weight
):
    _, rows_here, map_width, channels = feature_maps.shape
    queries = query_frame.shape[0]
    n_space = lax.axis_size("space")
    half = queries // 2
    height = rows_here * n_space
    positions = rows_here * map_width
    maps = feature_maps.reshape(positions, channels)

    row = query_row - lax.axis_index("space") * rows_here
    here = (query_frame == lax.axis_index("tm")) & (row >= 0) & (row < rows_here)
    target = jnp.where(here, row * map_width + query_col, -1)[None]

    coords = call(
        functools.partial(coord_kernel, map_width),
        jax.ShapeDtypeStruct((positions, LANES), BF16),
        0,
        flops=2048 * positions * LANES,
        bytes_accessed=2 * positions * LANES,
        transcendentals=0,
    )()
    target, coords = lax.optimization_barrier((target, coords))

    def pick(core_flip):
        return call(
            functools.partial(pick_kernel, core_flip),
            jax.ShapeDtypeStruct((half, channels), BF16),
            2,
            flops=queries * positions * channels,
            bytes_accessed=2 * positions * channels,
            transcendentals=0,
        )(target, maps)

    arrived = core_swap(pick(1))
    mine = pick(0) + arrived
    steps = n_space.bit_length() - 1
    for step in range(steps):
        mine = mine + space_swap(mine, step)
    theirs = core_swap(mine)

    block = jax.ShapeDtypeStruct((half + half // LANES * PIECE_ROWS, LANES), F32)

    def blocks_of(feats):
        return call(
            functools.partial(half_kernel, rows_here, height, map_width),
            block,
            3,
            flops=3 * queries * positions * channels,
            bytes_accessed=4 * positions * channels,
            transcendentals=half * positions,
        )(feats, maps, coords)

    def sent(value, step):
        value = lax.optimization_barrier(value.astype(jnp.float16))
        return value.astype(F32), space_swap(value, step).astype(F32)

    def merge(pair, step):
        return call(
            functools.partial(merge_kernel, n_space, step),
            block,
            2,
            flops=0,
            bytes_accessed=0,
            transcendentals=0,
        )(*pair)

    pairs = [sent(blocks_of(mine), 0), sent(blocks_of(theirs), 0)]
    for step in range(1, steps):
        pairs = [sent(merge(pair, step - 1), step) for pair in pairs]

    n_out = out_weight.shape[0]
    attended, place = call(
        functools.partial(last_merge_kernel, n_space, steps - 1),
        [
            jax.ShapeDtypeStruct((queries + PIECE_ROWS, LANES), BF16),
            jax.ShapeDtypeStruct((n_out, queries), F32),
        ],
        5,
        flops=4 * queries * channels,
        bytes_accessed=12 * queries * channels,
        transcendentals=0,
    )(ema_decay, *pairs[0], *pairs[1])
    return call(
        track_kernel,
        jax.ShapeDtypeStruct((1, n_out, queries), F32),
        6,
        flops=8 * queries * channels * channels,
        bytes_accessed=8 * queries * channels,
        transcendentals=2 * queries * channels,
    )(dw_kernel, pw_weight, out_weight, place, attended, core_swap(attended))


def local(feature_maps, query_frame, *rest):
    n_tm, n_space = lax.axis_size("tm"), lax.axis_size("space")
    paired = n_tm == 2 and n_space > 1 and n_space & (n_space - 1) == 0
    if paired and query_frame.shape[0] % (2 * LANES) == 0:
        return local_pair(feature_maps, query_frame, *rest)
    return local_general(feature_maps, query_frame, *rest)


def solution(mesh):
    placed = (
        P(("video", "tm"), "space", None, None),
        P("video"),
        P("video"),
        P("video"),
        P(("video", "tm"), None),
        P(),
        P(),
        P(),
    )
    return jax.shard_map(
        local, mesh=mesh, in_specs=placed, out_specs=P(("video", "tm"), None, None), check_vma=False
    )
```

```python
import functools
import math

import jax
import jax.numpy as jnp
from jax import lax
from jax.experimental import pallas as pl
from jax.experimental.pallas import tpu as pltpu
from jax.sharding import PartitionSpec as P

F32 = jnp.float32
BF16 = jnp.bfloat16
LANES = 128
AUX_ROWS = 8
PIECE_ROWS = 16
VMEM_LIMIT = 40 * 1024 * 1024
NT = (((1,), (1,)), ((), ()))


def pick_chunk(total, limit):
    best = None
    for size in range(LANES, limit + 1, LANES):
        if total % size == 0 and (best is None or size % 256 == 0 or best % 256):
            best = size
    return best if best is not None else total


def gather_kernel(rows_here, map_width, frame_ref, row_ref, col_ref, map_ref, *out_refs):
    positions = map_ref.shape[0]
    queries = frame_ref.shape[1]
    tm = lax.axis_index("tm")
    row = row_ref[...] - lax.axis_index("space") * rows_here
    here = (frame_ref[...] == tm) & (row >= 0) & (row < rows_here)
    target = jnp.where(here, row * map_width + col_ref[...], -1)
    target = jnp.transpose(jnp.broadcast_to(target, (LANES, queries)))
    chunk = pick_chunk(positions, 1536)
    picked = None
    for base in range(0, positions, chunk):
        parts = []
        for lane_base in range(base, base + chunk, LANES):
            lane = lax.broadcasted_iota(jnp.int32, (queries, LANES), 1) + lane_base
            parts.append(jnp.where(lane == target, 1.0, 0.0).astype(BF16))
        hot = jnp.concatenate(parts, axis=1)
        term = jnp.dot(hot, map_ref[base : base + chunk, :], preferred_element_type=F32)
        picked = term if picked is None else picked + term
    if len(out_refs) == 1:
        out_refs[0][...] = picked.astype(BF16)
        return
    half = queries // 2
    first, second = picked[:half].astype(F32), picked[half:].astype(F32)
    out_refs[0][...] = jnp.where(tm == 0, first, second).astype(BF16)
    out_refs[1][...] = jnp.where(tm == 0, second, first).astype(BF16)


def volume_kernel(n_groups, rows_here, height, width, *refs):
    *query_refs, map_ref, coord_ref, decay_ref, out_ref = refs
    positions, channels = map_ref.shape
    factor = math.log2(math.e) / math.sqrt(channels)
    part_queries = query_refs[0].shape[0]
    n_parts = len(query_refs)
    group = part_queries * n_parts // n_groups
    feat_rows = out_ref.shape[1] - AUX_ROWS
    first_row = (lax.axis_index("space") * rows_here).astype(F32)
    tm = lax.axis_index("tm")
    chunk = pick_chunk(positions, 1280)
    state = [None] * n_parts
    for base in range(0, positions, chunk):
        keys = map_ref[base : base + chunk, :]
        values = jnp.concatenate([keys, coord_ref[base : base + chunk, :]], axis=1)
        for part in range(n_parts):
            scores = lax.dot_general(
                query_refs[part][...], keys, NT, preferred_element_type=F32
            )
            top = jnp.max(scores, axis=1, keepdims=True) * factor
            if state[part] is not None:
                old_top, old_sum = state[part]
                top = jnp.maximum(top, old_top)
            weights = jnp.exp2(scores * factor - top).astype(BF16)
            sums = jnp.dot(weights, values, preferred_element_type=F32)
            if state[part] is not None:
                sums = sums + jnp.exp2(old_top - top) * old_sum
            state[part] = (top, sums)
    decay = [decay_ref[...]]
    sub = lax.broadcasted_iota(jnp.int32, (AUX_ROWS, LANES), 0)
    for part in range(n_parts):
        top, sums = state[part]
        feats = sums[:, :channels] / sums[:, channels + 2 : channels + 3]
        extra = sums[:, channels:]
        lane = lax.broadcasted_iota(jnp.int32, extra.shape, 1)
        extra = jnp.transpose(jnp.where(lane == 3, top, extra))
        total = extra[2:3]
        rows = [extra[3:4]]
        rows += [total, extra[0:1] / total / width, (extra[1:2] / total + first_row) / height]
        aux = jnp.zeros((AUX_ROWS, part_queries), F32)
        wide = lax.broadcasted_iota(jnp.int32, aux.shape, 0)
        for index, values in enumerate(rows):
            aux = jnp.where(wide == index, values, aux)
        where = part if n_parts == 1 else jnp.where(tm == 0, part, 1 - part)
        groups_here = n_groups // n_parts
        for index in range(groups_here):
            shift = (part_queries - index * group) % part_queries
            block = pltpu.roll(aux, shift, 1) if shift else aux
            block = block[:, :LANES]
            for offset, piece in enumerate(decay):
                block = jnp.where(sub == len(rows) + offset, piece, block)
            pieces = [feats[index * group : (index + 1) * group]]
            if feat_rows > group:
                pieces.append(jnp.zeros((feat_rows - group, LANES), F32))
            pieces.append(block)
            out_ref[where * groups_here + index] = jnp.concatenate(pieces, axis=0).astype(
                out_ref.dtype
            )


def tail_kernel(n_tm, n_space, group, dw_ref, pw_ref, ow_ref, in_ref, out_ref):
    feat_rows = in_ref.shape[1] - AUX_ROWS
    n_blocks = n_tm * n_space
    blocks = [in_ref[index].astype(F32) for index in range(n_blocks)]
    aux = [block[feat_rows:] for block in blocks]
    positions, shares, decays = [], [], []
    for frame in range(n_tm):
        mine = aux[frame * n_space : (frame + 1) * n_space]
        top = mine[0][0:1]
        for block in mine[1:]:
            top = jnp.maximum(top, block[0:1])
        weight = [jnp.exp2(b[0:1] - top) * b[1:2] for b in mine]
        total = sum(weight[1:], weight[0])
        share = [w / total for w in weight]
        shares += share
        across = [s * b[2:3] for s, b in zip(share, mine)]
        down = [s * b[3:4] for s, b in zip(share, mine)]
        positions.append((sum(across[1:], across[0]), sum(down[1:], down[0])))
        decays.append(mine[0][4:5])
    pad_blocks = -(-n_blocks // 8) * 8
    table = jnp.zeros((pad_blocks, LANES), F32)
    sub = lax.broadcasted_iota(jnp.int32, table.shape, 0)
    for index, share in enumerate(shares):
        table = jnp.where(sub == index, share, table)
    table = jnp.transpose(table)
    attended = []
    for frame in range(n_tm):
        value = None
        for index in range(frame * n_space, (frame + 1) * n_space):
            term = table[:group, index : index + 1] * blocks[index][:group]
            value = term if value is None else value + term
        attended.append(value.astype(BF16).astype(F32))
    taps = dw_ref.shape[0]
    hidden = []
    for frame in range(n_tm):
        depth = None
        for tap in range(taps):
            source = frame + tap - taps // 2
            if 0 <= source < n_tm:
                term = dw_ref[tap : tap + 1, :] * attended[source]
                depth = term if depth is None else depth + term
        hidden.append(jax.nn.gelu(depth).astype(BF16).astype(F32))
    hidden = jnp.concatenate(hidden, axis=0).astype(BF16)
    mixed = jnp.dot(hidden, pw_ref[...], preferred_element_type=F32)
    memory = None
    out = jnp.zeros(out_ref.shape, F32)
    out_sub = lax.broadcasted_iota(jnp.int32, out.shape, 0)
    n_out = ow_ref.shape[0]
    for frame in range(n_tm):
        refined = attended[frame] + mixed[frame * group : (frame + 1) * group]
        fresh = (1.0 - decays[frame]) * refined
        memory = fresh if memory is None else decays[frame] * memory + fresh
        padded = memory
        if group < LANES:
            padded = jnp.concatenate([memory, jnp.zeros((LANES - group, LANES), F32)], axis=0)
        delta = lax.dot_general(
            ow_ref[...], padded, NT, preferred_element_type=F32, precision=lax.Precision.HIGHEST
        )
        for axis in range(n_out):
            line = positions[frame][axis] + delta[axis : axis + 1]
            out = jnp.where(out_sub == frame * n_out + axis, line, out)
    out_ref[...] = out


def call(kernel, out_shape, n_in, **cost):
    vmem = pl.BlockSpec(memory_space=pltpu.VMEM)
    return pl.pallas_call(
        kernel,
        out_shape=out_shape,
        in_specs=[vmem] * n_in,
        out_specs=jax.tree.map(lambda _: vmem, out_shape),
        compiler_params=pltpu.CompilerParams(vmem_limit_bytes=VMEM_LIMIT),
        cost_estimate=pl.CostEstimate(**cost),
    )


def hot_rows(target, map_ref, base, chunk):
    rows = target.shape[0]
    lane = lax.broadcasted_iota(jnp.int32, (rows, LANES), 1)
    parts = []
    for lane_base in range(base, base + chunk, LANES):
        parts.append(jnp.where(lane + lane_base == target, 1.0, 0.0).astype(BF16))
    hot = jnp.concatenate(parts, axis=1)
    return jnp.dot(hot, map_ref[base : base + chunk, :], preferred_element_type=F32)


def pick_kernel(core_flip, target_ref, map_ref, out_ref):
    half = target_ref.shape[1] // 2
    positions = map_ref.shape[0]
    chunk = pick_chunk(positions, 1536)
    second = lax.axis_index("tm") != core_flip
    target = jnp.where(second, target_ref[:, half:], target_ref[:, :half])
    target = jnp.transpose(jnp.broadcast_to(target, (LANES, half)))
    picked = None
    for base in range(0, positions, chunk):
        term = hot_rows(target, map_ref, base, chunk)
        picked = term if picked is None else picked + term
    out_ref[...] = picked.astype(BF16)


def coord_kernel(map_width, after_ref, out_ref):
    positions = out_ref.shape[0]
    chunk = pick_chunk(positions, 512)
    lane = lax.broadcasted_iota(jnp.int32, (chunk, LANES), 1)
    local_place = lax.broadcasted_iota(jnp.int32, (chunk, LANES), 0).astype(F32)

    @pl.loop(0, positions // chunk)
    def _(step):
        place = local_place + (step * chunk).astype(F32)
        row = jnp.floor((place + 0.5) * (1.0 / map_width))
        rest = jnp.where(lane == 2, 1.0, 0.0)
        value = jnp.where(lane == 0, place - row * map_width, jnp.where(lane == 1, row, rest))
        out_ref[pl.ds(pl.multiple_of(step * chunk, chunk), chunk), :] = value.astype(BF16)


def split(value):
    pieces = []
    for _ in range(3):
        piece = value.astype(BF16).astype(F32)
        pieces.append(piece)
        value = value - piece
    return pieces


def half_kernel(rows_here, height, width, query_ref, map_ref, coord_ref, out_ref):
    positions, channels = map_ref.shape
    factor = math.log2(math.e) / math.sqrt(channels)
    query = query_ref[...]
    first_row = (lax.axis_index("space") * rows_here).astype(F32)
    chunk = pick_chunk(positions, 2560)

    def score(base):
        keys = map_ref[base : base + chunk, :]
        return lax.dot_general(query, keys, NT, preferred_element_type=F32)

    top = sums = None
    ahead = score(0)
    for base in range(0, positions, chunk):
        scores = ahead
        if base + chunk < positions:
            ahead = score(base + chunk)
        window = slice(base, base + chunk)
        values = jnp.concatenate([map_ref[window, :], coord_ref[window, :]], axis=1)
        new_top = jnp.max(scores, axis=1, keepdims=True) * factor
        if top is not None:
            new_top = jnp.maximum(new_top, top)
        weights = jnp.exp2(scores * factor - new_top).astype(BF16)
        terms = jnp.dot(weights, values, preferred_element_type=F32)
        sums = terms if sums is None else terms + jnp.exp2(top - new_top) * sums
        top = new_top
    feats = sums[:, :channels] / sums[:, channels + 2 : channels + 3]
    extra = sums[:, channels:]
    lane = lax.broadcasted_iota(jnp.int32, extra.shape, 1)
    extra = jnp.transpose(jnp.where(lane == 3, top, extra))
    total = extra[2:3]
    across = extra[0:1] / total / width
    down = (extra[1:2] / total + first_row) / height
    store_block(out_ref, feats, [extra[3:4], total, across, down])


def store_block(out_ref, feats, lines):
    queries = feats.shape[0]
    out_ref[:queries, :] = feats
    rows = [piece for line in lines for piece in split(line)]
    sub = lax.broadcasted_iota(jnp.int32, (PIECE_ROWS, queries), 0)
    aux = jnp.zeros((PIECE_ROWS, queries), F32)
    for index, row in enumerate(rows):
        aux = jnp.where(sub == index, row, aux)
    for tile in range(queries // LANES):
        base = queries + tile * PIECE_ROWS
        out_ref[base : base + PIECE_ROWS, :] = aux[:, tile * LANES : (tile + 1) * LANES]


def merged(bit, own_ref, came_ref):
    queries = own_ref.shape[0] * LANES // (LANES + PIECE_ROWS)
    high = (lax.axis_index("space") & bit) != 0
    own, came = own_ref[...].astype(F32), came_ref[...].astype(F32)
    pair = [jnp.where(high, came, own), jnp.where(high, own, came)]
    feats, lines = [], []
    for tile in range(queries // LANES):
        base = queries + tile * PIECE_ROWS
        parts = []
        for block in pair:
            aux = block[base : base + PIECE_ROWS]
            parts.append(
                [aux[i : i + 1] + aux[i + 1 : i + 2] + aux[i + 2 : i + 3] for i in (0, 3, 6, 9)]
            )
        (top_a, total_a, *place_a), (top_b, total_b, *place_b) = parts
        top = jnp.maximum(top_a, top_b)
        weight_a, weight_b = jnp.exp2(top_a - top) * total_a, jnp.exp2(top_b - top) * total_b
        total = weight_a + weight_b
        share_a, share_b = weight_a / total, weight_b / total
        places = [share_a * a + share_b * b for a, b in zip(place_a, place_b)]
        lines.append([top, total, *places])
        sub = lax.broadcasted_iota(jnp.int32, (8, LANES), 0)
        table = jnp.transpose(jnp.where(sub == 0, share_a, jnp.where(sub == 1, share_b, 0.0)))
        window = slice(tile * LANES, (tile + 1) * LANES)
        feats.append(table[:, 0:1] * pair[0][window] + table[:, 1:2] * pair[1][window])
    return jnp.concatenate(feats, axis=0), [jnp.concatenate(v, axis=1) for v in zip(*lines)]


def my_bit(step, n_space):
    bits = n_space.bit_length() - 1
    return jnp.left_shift(1, lax.rem(lax.axis_index("tm") + step, bits))


def merge_kernel(n_space, step, own_ref, came_ref, out_ref):
    store_block(out_ref, *merged(my_bit(step, n_space), own_ref, came_ref))


def last_merge_kernel(n_space, step, decay_ref, own_ref, came_ref, out_ref, place_ref):
    feats, lines = merged(my_bit(step, n_space), own_ref, came_ref)
    out_ref[: feats.shape[0], :] = feats.astype(BF16)
    place_ref[0:1, :] = lines[2]
    place_ref[1:2, :] = lines[3]
    sub = lax.broadcasted_iota(jnp.int32, (PIECE_ROWS, LANES), 0)
    rows = jnp.zeros((PIECE_ROWS, LANES), F32)
    for index, piece in enumerate(split(decay_ref[...])):
        rows = jnp.where(sub == index, piece, rows)
    out_ref[feats.shape[0] :, :] = rows.astype(BF16)


def track_kernel(
    dw_ref, pw_ref, ow_ref, near_place, far_place, near_mine, far_mine, near_came, far_came, out_ref
):
    early = lax.axis_index("tm") == 0
    half = near_place.shape[1]

    def retention(ref):
        rows = ref[half:, :].astype(F32)
        return rows[0:1] + rows[1:2] + rows[2:3]

    decay_mine, decay_theirs = retention(near_mine), retention(near_came)
    mine = jnp.concatenate([near_mine[:half, :], far_mine[:half, :]], axis=0).astype(F32)
    theirs = jnp.concatenate([far_came[:half, :], near_came[:half, :]], axis=0).astype(F32)
    attended = [jnp.where(early, mine, theirs), jnp.where(early, theirs, mine)]
    decay = [
        jnp.where(early, decay_mine, decay_theirs),
        jnp.where(early, decay_theirs, decay_mine),
    ]
    taps = dw_ref.shape[0]
    refined = []
    for frame in range(2):
        depth = None
        for tap in range(taps):
            source = frame + tap - taps // 2
            if 0 <= source < 2:
                term = dw_ref[tap : tap + 1, :] * attended[source]
                depth = term if depth is None else depth + term
        hidden = jax.nn.gelu(depth).astype(BF16)
        mixed = jnp.dot(hidden, pw_ref[...], preferred_element_type=F32)
        refined.append(attended[frame] + mixed)
    first = (1.0 - decay[0]) * refined[0]
    second = decay[1] * first + (1.0 - decay[1]) * refined[1]
    memory = jnp.where(early, first, second)
    n_out = ow_ref.shape[0]
    weights = jnp.concatenate(split(ow_ref[...]), axis=0).astype(BF16)
    line = jnp.concatenate([near_place[...], far_place[...]], axis=1)
    for piece in split(memory)[:2]:
        terms = lax.dot_general(weights, piece.astype(BF16), NT, preferred_element_type=F32)
        line = line + terms[:n_out] + terms[n_out : 2 * n_out] + terms[2 * n_out :]
    low, high = line[:, :half], line[:, half:]
    out_ref[0, :, :half] = jnp.where(early, low, high)
    out_ref[0, :, half:] = jnp.where(early, high, low)


def swap(value, axis, bit):
    return lax.ppermute(value, axis, [(i, i ^ bit) for i in range(lax.axis_size(axis))])


def all_sum(value, axis):
    count = lax.axis_size(axis)
    if count & (count - 1):
        return lax.psum(value, axis)
    bit = 1
    while bit < count:
        value = value + swap(value, axis, bit)
        bit *= 2
    return value


def local_general(
    feature_maps, query_frame, query_row, query_col, ema_decay, dw_kernel, pw_weight, out_weight
):
    frames_here, rows_here, map_width, channels = feature_maps.shape
    assert frames_here == 1 and channels == LANES
    queries = query_frame.shape[0]
    n_tm, n_space = lax.axis_size("tm"), lax.axis_size("space")
    n_groups = n_tm * n_space
    group = queries // n_groups
    height = rows_here * n_space
    positions = rows_here * map_width
    maps = feature_maps.reshape(positions, channels)
    halves = 2 if n_tm == 2 else 1
    part = jax.ShapeDtypeStruct((queries // halves, channels), BF16)

    picked = call(
        functools.partial(gather_kernel, rows_here, map_width),
        [part] * halves,
        4,
        flops=2 * queries * positions * channels,
        bytes_accessed=2 * positions * channels,
        transcendentals=0,
    )(query_frame[None], query_row[None], query_col[None], maps)

    place = jnp.arange(positions, dtype=jnp.int32)[:, None]
    lane = jnp.arange(LANES, dtype=jnp.int32)[None, :]
    coords = jnp.where(
        lane == 0,
        place % map_width,
        jnp.where(lane == 1, place // map_width, jnp.where(lane == 2, 1, 0)),
    ).astype(BF16)

    if halves == 2:
        mine = picked[0] + swap(picked[1], "tm", 1)
        mine = all_sum(mine, "space")
        feats = [mine, swap(mine, "tm", 1)]
    else:
        feats = [all_sum(all_sum(picked[0], "tm"), "space")]

    feat_rows = -(-group // 8) * 8
    blocks = call(
        functools.partial(volume_kernel, n_groups, rows_here, height, map_width),
        jax.ShapeDtypeStruct((n_groups, feat_rows + AUX_ROWS, LANES), F32),
        halves + 3,
        flops=6 * queries * positions * channels,
        bytes_accessed=4 * positions * channels,
        transcendentals=queries * positions,
    )(*feats, maps, coords, ema_decay)

    blocks = lax.all_to_all(blocks, ("tm", "space"), 0, 0, tiled=True)

    n_out = out_weight.shape[0]
    out_rows = -(-n_tm * n_out // 8) * 8
    lines = call(
        functools.partial(tail_kernel, n_tm, n_space, group),
        jax.ShapeDtypeStruct((out_rows, LANES), F32),
        4,
        flops=2 * n_tm * group * channels * channels,
        bytes_accessed=4 * n_groups * (feat_rows + AUX_ROWS) * LANES,
        transcendentals=n_tm * group * channels,
    )(dw_kernel, pw_weight, out_weight, blocks)

    lines = lax.all_gather(lines, ("tm", "space"), axis=0)
    own = lax.dynamic_slice_in_dim(lines, lax.axis_index("tm") * n_out, n_out, axis=1)
    own = own[:, :, :group]
    return jnp.transpose(own, (1, 0, 2)).reshape(1, n_out, queries)


def core_swap(value):
    return lax.ppermute(value, "tm", [(0, 1), (1, 0)])


def space_swap(value, step):
    n_space = lax.axis_size("space")
    bits = n_space.bit_length() - 1
    pairs = []
    for tm in range(2):
        for space in range(n_space):
            to = space ^ (1 << (tm + step) % bits)
            pairs.append((tm * n_space + space, tm * n_space + to))
    return lax.ppermute(value, ("tm", "space"), pairs)


def local_pair(
    feature_maps, query_frame, query_row, query_col, ema_decay, dw_kernel, pw_weight, out_weight
):
    _, rows_here, map_width, channels = feature_maps.shape
    queries = query_frame.shape[0]
    n_space = lax.axis_size("space")
    half = queries // 2
    height = rows_here * n_space
    positions = rows_here * map_width
    maps = feature_maps.reshape(positions, channels)

    row = query_row - lax.axis_index("space") * rows_here
    here = (query_frame == lax.axis_index("tm")) & (row >= 0) & (row < rows_here)
    target = jnp.where(here, row * map_width + query_col, -1)[None]

    def pick(core_flip):
        return call(
            functools.partial(pick_kernel, core_flip),
            jax.ShapeDtypeStruct((half, channels), BF16),
            2,
            flops=queries * positions * channels,
            bytes_accessed=2 * positions * channels,
            transcendentals=0,
        )(target, maps)

    arrived = core_swap(pick(1))
    coords = call(
        functools.partial(coord_kernel, map_width),
        jax.ShapeDtypeStruct((positions, LANES), BF16),
        1,
        flops=8 * positions * LANES,
        bytes_accessed=2 * positions * LANES,
        transcendentals=0,
    )(target)
    mine = pick(0) + arrived
    steps = n_space.bit_length() - 1
    for step in range(steps):
        mine = mine + space_swap(mine, step)
    theirs = core_swap(mine)

    block = jax.ShapeDtypeStruct((half + half // LANES * PIECE_ROWS, LANES), F32)

    def blocks_of(feats):
        return call(
            functools.partial(half_kernel, rows_here, height, map_width),
            block,
            3,
            flops=3 * queries * positions * channels,
            bytes_accessed=4 * positions * channels,
            transcendentals=half * positions,
        )(feats, maps, coords)

    def sent(value, step):
        value = lax.optimization_barrier(value.astype(jnp.float16))
        return value.astype(F32), space_swap(value, step).astype(F32)

    def merge(pair, step):
        return call(
            functools.partial(merge_kernel, n_space, step),
            block,
            2,
            flops=0,
            bytes_accessed=0,
            transcendentals=0,
        )(*pair)

    pairs = [sent(blocks_of(mine), 0), sent(blocks_of(theirs), 0)]
    for step in range(1, steps):
        pairs = [sent(merge(pair, step - 1), step) for pair in pairs]

    n_out = out_weight.shape[0]
    attended, places = [], []
    for pair in pairs:
        value, place = call(
            functools.partial(last_merge_kernel, n_space, steps - 1),
            [
                jax.ShapeDtypeStruct((half + PIECE_ROWS, LANES), BF16),
                jax.ShapeDtypeStruct((n_out, half), F32),
            ],
            3,
            flops=0,
            bytes_accessed=0,
            transcendentals=0,
        )(ema_decay, *pair)
        attended.append(value)
        places.append(place)
    return call(
        track_kernel,
        jax.ShapeDtypeStruct((1, n_out, queries), F32),
        9,
        flops=8 * queries * channels * channels,
        bytes_accessed=8 * queries * channels,
        transcendentals=2 * queries * channels,
    )(dw_kernel, pw_weight, out_weight, *places, *attended, *[core_swap(v) for v in attended])


def local(feature_maps, query_frame, *rest):
    n_tm, n_space = lax.axis_size("tm"), lax.axis_size("space")
    paired = n_tm == 2 and n_space > 1 and n_space & (n_space - 1) == 0
    if paired and query_frame.shape[0] % (2 * LANES) == 0:
        return local_pair(feature_maps, query_frame, *rest)
    return local_general(feature_maps, query_frame, *rest)


def solution(mesh):
    placed = (
        P(("video", "tm"), "space", None, None),
        P("video"),
        P("video"),
        P("video"),
        P(("video", "tm"), None),
        P(),
        P(),
        P(),
    )
    return jax.shard_map(
        local, mesh=mesh, in_specs=placed, out_specs=P(("video", "tm"), None, None), check_vma=False
    )
```

```python
import functools
import math

import jax
import jax.numpy as jnp
from jax import lax
from jax.experimental import pallas as pl
from jax.experimental.pallas import tpu as pltpu
from jax.sharding import PartitionSpec as P

F32 = jnp.float32
BF16 = jnp.bfloat16
LANES = 128
AUX_ROWS = 8
PIECE_ROWS = 16
VMEM_LIMIT = 40 * 1024 * 1024
NT = (((1,), (1,)), ((), ()))


def pick_chunk(total, limit):
    best = None
    for size in range(LANES, limit + 1, LANES):
        if total % size == 0 and (best is None or size % 256 == 0 or best % 256):
            best = size
    return best if best is not None else total


def gather_kernel(rows_here, map_width, frame_ref, row_ref, col_ref, map_ref, *out_refs):
    positions = map_ref.shape[0]
    queries = frame_ref.shape[1]
    tm = lax.axis_index("tm")
    row = row_ref[...] - lax.axis_index("space") * rows_here
    here = (frame_ref[...] == tm) & (row >= 0) & (row < rows_here)
    target = jnp.where(here, row * map_width + col_ref[...], -1)
    target = jnp.transpose(jnp.broadcast_to(target, (LANES, queries)))
    chunk = pick_chunk(positions, 1536)
    picked = None
    for base in range(0, positions, chunk):
        parts = []
        for lane_base in range(base, base + chunk, LANES):
            lane = lax.broadcasted_iota(jnp.int32, (queries, LANES), 1) + lane_base
            parts.append(jnp.where(lane == target, 1.0, 0.0).astype(BF16))
        hot = jnp.concatenate(parts, axis=1)
        term = jnp.dot(hot, map_ref[base : base + chunk, :], preferred_element_type=F32)
        picked = term if picked is None else picked + term
    if len(out_refs) == 1:
        out_refs[0][...] = picked.astype(BF16)
        return
    half = queries // 2
    first, second = picked[:half].astype(F32), picked[half:].astype(F32)
    out_refs[0][...] = jnp.where(tm == 0, first, second).astype(BF16)
    out_refs[1][...] = jnp.where(tm == 0, second, first).astype(BF16)


def volume_kernel(n_groups, rows_here, height, width, *refs):
    *query_refs, map_ref, coord_ref, decay_ref, out_ref = refs
    positions, channels = map_ref.shape
    factor = math.log2(math.e) / math.sqrt(channels)
    part_queries = query_refs[0].shape[0]
    n_parts = len(query_refs)
    group = part_queries * n_parts // n_groups
    feat_rows = out_ref.shape[1] - AUX_ROWS
    first_row = (lax.axis_index("space") * rows_here).astype(F32)
    tm = lax.axis_index("tm")
    chunk = pick_chunk(positions, 1280)
    state = [None] * n_parts
    for base in range(0, positions, chunk):
        keys = map_ref[base : base + chunk, :]
        values = jnp.concatenate([keys, coord_ref[base : base + chunk, :]], axis=1)
        for part in range(n_parts):
            scores = lax.dot_general(
                query_refs[part][...], keys, NT, preferred_element_type=F32
            )
            top = jnp.max(scores, axis=1, keepdims=True) * factor
            if state[part] is not None:
                old_top, old_sum = state[part]
                top = jnp.maximum(top, old_top)
            weights = jnp.exp2(scores * factor - top).astype(BF16)
            sums = jnp.dot(weights, values, preferred_element_type=F32)
            if state[part] is not None:
                sums = sums + jnp.exp2(old_top - top) * old_sum
            state[part] = (top, sums)
    decay = [decay_ref[...]]
    sub = lax.broadcasted_iota(jnp.int32, (AUX_ROWS, LANES), 0)
    for part in range(n_parts):
        top, sums = state[part]
        feats = sums[:, :channels] / sums[:, channels + 2 : channels + 3]
        extra = sums[:, channels:]
        lane = lax.broadcasted_iota(jnp.int32, extra.shape, 1)
        extra = jnp.transpose(jnp.where(lane == 3, top, extra))
        total = extra[2:3]
        rows = [extra[3:4]]
        rows += [total, extra[0:1] / total / width, (extra[1:2] / total + first_row) / height]
        aux = jnp.zeros((AUX_ROWS, part_queries), F32)
        wide = lax.broadcasted_iota(jnp.int32, aux.shape, 0)
        for index, values in enumerate(rows):
            aux = jnp.where(wide == index, values, aux)
        where = part if n_parts == 1 else jnp.where(tm == 0, part, 1 - part)
        groups_here = n_groups // n_parts
        for index in range(groups_here):
            shift = (part_queries - index * group) % part_queries
            block = pltpu.roll(aux, shift, 1) if shift else aux
            block = block[:, :LANES]
            for offset, piece in enumerate(decay):
                block = jnp.where(sub == len(rows) + offset, piece, block)
            pieces = [feats[index * group : (index + 1) * group]]
            if feat_rows > group:
                pieces.append(jnp.zeros((feat_rows - group, LANES), F32))
            pieces.append(block)
            out_ref[where * groups_here + index] = jnp.concatenate(pieces, axis=0).astype(
                out_ref.dtype
            )


def tail_kernel(n_tm, n_space, group, dw_ref, pw_ref, ow_ref, in_ref, out_ref):
    feat_rows = in_ref.shape[1] - AUX_ROWS
    n_blocks = n_tm * n_space
    blocks = [in_ref[index].astype(F32) for index in range(n_blocks)]
    aux = [block[feat_rows:] for block in blocks]
    positions, shares, decays = [], [], []
    for frame in range(n_tm):
        mine = aux[frame * n_space : (frame + 1) * n_space]
        top = mine[0][0:1]
        for block in mine[1:]:
            top = jnp.maximum(top, block[0:1])
        weight = [jnp.exp2(b[0:1] - top) * b[1:2] for b in mine]
        total = sum(weight[1:], weight[0])
        share = [w / total for w in weight]
        shares += share
        across = [s * b[2:3] for s, b in zip(share, mine)]
        down = [s * b[3:4] for s, b in zip(share, mine)]
        positions.append((sum(across[1:], across[0]), sum(down[1:], down[0])))
        decays.append(mine[0][4:5])
    pad_blocks = -(-n_blocks // 8) * 8
    table = jnp.zeros((pad_blocks, LANES), F32)
    sub = lax.broadcasted_iota(jnp.int32, table.shape, 0)
    for index, share in enumerate(shares):
        table = jnp.where(sub == index, share, table)
    table = jnp.transpose(table)
    attended = []
    for frame in range(n_tm):
        value = None
        for index in range(frame * n_space, (frame + 1) * n_space):
            term = table[:group, index : index + 1] * blocks[index][:group]
            value = term if value is None else value + term
        attended.append(value.astype(BF16).astype(F32))
    taps = dw_ref.shape[0]
    hidden = []
    for frame in range(n_tm):
        depth = None
        for tap in range(taps):
            source = frame + tap - taps // 2
            if 0 <= source < n_tm:
                term = dw_ref[tap : tap + 1, :] * attended[source]
                depth = term if depth is None else depth + term
        hidden.append(jax.nn.gelu(depth).astype(BF16).astype(F32))
    hidden = jnp.concatenate(hidden, axis=0).astype(BF16)
    mixed = jnp.dot(hidden, pw_ref[...], preferred_element_type=F32)
    memory = None
    out = jnp.zeros(out_ref.shape, F32)
    out_sub = lax.broadcasted_iota(jnp.int32, out.shape, 0)
    n_out = ow_ref.shape[0]
    for frame in range(n_tm):
        refined = attended[frame] + mixed[frame * group : (frame + 1) * group]
        fresh = (1.0 - decays[frame]) * refined
        memory = fresh if memory is None else decays[frame] * memory + fresh
        padded = memory
        if group < LANES:
            padded = jnp.concatenate([memory, jnp.zeros((LANES - group, LANES), F32)], axis=0)
        delta = lax.dot_general(
            ow_ref[...], padded, NT, preferred_element_type=F32, precision=lax.Precision.HIGHEST
        )
        for axis in range(n_out):
            line = positions[frame][axis] + delta[axis : axis + 1]
            out = jnp.where(out_sub == frame * n_out + axis, line, out)
    out_ref[...] = out


def call(kernel, out_shape, n_in, **cost):
    vmem = pl.BlockSpec(memory_space=pltpu.VMEM)
    return pl.pallas_call(
        kernel,
        out_shape=out_shape,
        in_specs=[vmem] * n_in,
        out_specs=jax.tree.map(lambda _: vmem, out_shape),
        compiler_params=pltpu.CompilerParams(vmem_limit_bytes=VMEM_LIMIT),
        cost_estimate=pl.CostEstimate(**cost),
    )


def pick_kernel(core_flip, target_ref, map_ref, out_ref):
    half = target_ref.shape[1] // 2
    positions, channels = map_ref.shape
    size = pick_chunk(positions, 256)
    second = lax.axis_index("tm") != core_flip
    target = jnp.where(second, target_ref[:, half:], target_ref[:, :half])
    tile = jnp.where(target < 0, -1, target // size)
    place = target - tile * size
    tile = jnp.transpose(jnp.broadcast_to(tile, (channels, half)))
    place = jnp.transpose(jnp.broadcast_to(place, (LANES, half)))
    lane = lax.broadcasted_iota(jnp.int32, (half, LANES), 1)
    parts = [
        jnp.where(lane + base == place, 1.0, 0.0).astype(BF16) for base in range(0, size, LANES)
    ]
    hot = jnp.concatenate(parts, axis=1)
    picked = jnp.zeros((half, channels), F32)
    for index in range(positions // size):
        keys = map_ref[index * size : (index + 1) * size, :]
        rows = jnp.dot(hot, keys, preferred_element_type=F32)
        picked = jnp.where(tile == index, rows, picked)
    out_ref[...] = picked.astype(BF16)


def coord_kernel(map_width, after_ref, out_ref):
    positions = out_ref.shape[0]
    chunk = pick_chunk(positions, 512)
    lane = lax.broadcasted_iota(jnp.int32, (chunk, LANES), 1)
    local_place = lax.broadcasted_iota(jnp.int32, (chunk, LANES), 0).astype(F32)

    @pl.loop(0, positions // chunk)
    def _(step):
        place = local_place + (step * chunk).astype(F32)
        row = jnp.floor((place + 0.5) * (1.0 / map_width))
        rest = jnp.where(lane == 2, 1.0, 0.0)
        value = jnp.where(lane == 0, place - row * map_width, jnp.where(lane == 1, row, rest))
        out_ref[pl.ds(pl.multiple_of(step * chunk, chunk), chunk), :] = value.astype(BF16)


def split(value):
    pieces = []
    for _ in range(3):
        piece = value.astype(BF16).astype(F32)
        pieces.append(piece)
        value = value - piece
    return pieces


def half_kernel(rows_here, height, width, query_ref, map_ref, coord_ref, out_ref):
    positions, channels = map_ref.shape
    factor = math.log2(math.e) / math.sqrt(channels)
    query = query_ref[...]
    first_row = (lax.axis_index("space") * rows_here).astype(F32)
    chunk = pick_chunk(positions, 2560)

    def score(base):
        keys = map_ref[base : base + chunk, :]
        return lax.dot_general(query, keys, NT, preferred_element_type=F32)

    top = sums = None
    ahead = score(0)
    for base in range(0, positions, chunk):
        scores = ahead
        if base + chunk < positions:
            ahead = score(base + chunk)
        window = slice(base, base + chunk)
        values = jnp.concatenate([map_ref[window, :], coord_ref[window, :]], axis=1)
        new_top = jnp.max(scores, axis=1, keepdims=True) * factor
        if top is not None:
            new_top = jnp.maximum(new_top, top)
        weights = jnp.exp2(scores * factor - new_top).astype(BF16)
        terms = jnp.dot(weights, values, preferred_element_type=F32)
        sums = terms if sums is None else terms + jnp.exp2(top - new_top) * sums
        top = new_top
    feats = sums[:, :channels] * (1.0 / sums[:, channels + 2 : channels + 3])
    extra = sums[:, channels:]
    lane = lax.broadcasted_iota(jnp.int32, extra.shape, 1)
    extra = jnp.transpose(jnp.where(lane == 3, top, extra))
    total = extra[2:3]
    across = extra[0:1] / total / width
    down = (extra[1:2] / total + first_row) / height
    store_block(out_ref, feats, [extra[3:4], total, across, down])


def store_block(out_ref, feats, lines):
    queries = feats.shape[0]
    out_ref[:queries, :] = feats
    rows = [piece for line in lines for piece in split(line)]
    sub = lax.broadcasted_iota(jnp.int32, (PIECE_ROWS, queries), 0)
    aux = jnp.zeros((PIECE_ROWS, queries), F32)
    for index, row in enumerate(rows):
        aux = jnp.where(sub == index, row, aux)
    for tile in range(queries // LANES):
        base = queries + tile * PIECE_ROWS
        out_ref[base : base + PIECE_ROWS, :] = aux[:, tile * LANES : (tile + 1) * LANES]


def merged(bit, own_ref, came_ref):
    queries = own_ref.shape[0] * LANES // (LANES + PIECE_ROWS)
    high = (lax.axis_index("space") & bit) != 0
    own, came = own_ref[...].astype(F32), came_ref[...].astype(F32)
    pair = [jnp.where(high, came, own), jnp.where(high, own, came)]
    feats, lines = [], []
    for tile in range(queries // LANES):
        base = queries + tile * PIECE_ROWS
        parts = []
        for block in pair:
            aux = block[base : base + PIECE_ROWS]
            parts.append(
                [aux[i : i + 1] + aux[i + 1 : i + 2] + aux[i + 2 : i + 3] for i in (0, 3, 6, 9)]
            )
        (top_a, total_a, *place_a), (top_b, total_b, *place_b) = parts
        top = jnp.maximum(top_a, top_b)
        weight_a, weight_b = jnp.exp2(top_a - top) * total_a, jnp.exp2(top_b - top) * total_b
        total = weight_a + weight_b
        share_a, share_b = weight_a / total, weight_b / total
        places = [share_a * a + share_b * b for a, b in zip(place_a, place_b)]
        lines.append([top, total, *places])
        sub = lax.broadcasted_iota(jnp.int32, (8, LANES), 0)
        table = jnp.transpose(jnp.where(sub == 0, share_a, jnp.where(sub == 1, share_b, 0.0)))
        window = slice(tile * LANES, (tile + 1) * LANES)
        feats.append(table[:, 0:1] * pair[0][window] + table[:, 1:2] * pair[1][window])
    return jnp.concatenate(feats, axis=0), [jnp.concatenate(v, axis=1) for v in zip(*lines)]


def my_bit(step, n_space):
    bits = n_space.bit_length() - 1
    return jnp.left_shift(1, lax.rem(lax.axis_index("tm") + step, bits))


def merge_kernel(n_space, step, own_ref, came_ref, out_ref):
    store_block(out_ref, *merged(my_bit(step, n_space), own_ref, came_ref))


def last_merge_kernel(n_space, step, decay_ref, own_ref, came_ref, out_ref, place_ref):
    feats, lines = merged(my_bit(step, n_space), own_ref, came_ref)
    out_ref[: feats.shape[0], :] = feats.astype(BF16)
    place_ref[0:1, :] = lines[2]
    place_ref[1:2, :] = lines[3]
    sub = lax.broadcasted_iota(jnp.int32, (PIECE_ROWS, LANES), 0)
    rows = jnp.zeros((PIECE_ROWS, LANES), F32)
    for index, piece in enumerate(split(decay_ref[...])):
        rows = jnp.where(sub == index, piece, rows)
    out_ref[feats.shape[0] :, :] = rows.astype(BF16)


def track_kernel(
    dw_ref, pw_ref, ow_ref, near_place, far_place, near_mine, far_mine, near_came, far_came, out_ref
):
    early = lax.axis_index("tm") == 0
    half = near_place.shape[1]

    def retention(ref):
        rows = ref[half:, :].astype(F32)
        return rows[0:1] + rows[1:2] + rows[2:3]

    decay_mine, decay_theirs = retention(near_mine), retention(near_came)
    mine = jnp.concatenate([near_mine[:half, :], far_mine[:half, :]], axis=0).astype(F32)
    theirs = jnp.concatenate([far_came[:half, :], near_came[:half, :]], axis=0).astype(F32)
    attended = [jnp.where(early, mine, theirs), jnp.where(early, theirs, mine)]
    decay = [
        jnp.where(early, decay_mine, decay_theirs),
        jnp.where(early, decay_theirs, decay_mine),
    ]
    taps = dw_ref.shape[0]
    refined = []
    for frame in range(2):
        depth = None
        for tap in range(taps):
            source = frame + tap - taps // 2
            if 0 <= source < 2:
                term = dw_ref[tap : tap + 1, :] * attended[source]
                depth = term if depth is None else depth + term
        hidden = jax.nn.gelu(depth).astype(BF16)
        mixed = jnp.dot(hidden, pw_ref[...], preferred_element_type=F32)
        refined.append(attended[frame] + mixed)
    first = (1.0 - decay[0]) * refined[0]
    second = decay[1] * first + (1.0 - decay[1]) * refined[1]
    memory = jnp.where(early, first, second)
    n_out = ow_ref.shape[0]
    weights = jnp.concatenate(split(ow_ref[...]), axis=0).astype(BF16)
    line = jnp.concatenate([near_place[...], far_place[...]], axis=1)
    for piece in split(memory)[:2]:
        terms = lax.dot_general(weights, piece.astype(BF16), NT, preferred_element_type=F32)
        line = line + terms[:n_out] + terms[n_out : 2 * n_out] + terms[2 * n_out :]
    low, high = line[:, :half], line[:, half:]
    out_ref[0, :, :half] = jnp.where(early, low, high)
    out_ref[0, :, half:] = jnp.where(early, high, low)


def swap(value, axis, bit):
    return lax.ppermute(value, axis, [(i, i ^ bit) for i in range(lax.axis_size(axis))])


def all_sum(value, axis):
    count = lax.axis_size(axis)
    if count & (count - 1):
        return lax.psum(value, axis)
    bit = 1
    while bit < count:
        value = value + swap(value, axis, bit)
        bit *= 2
    return value


def local_general(
    feature_maps, query_frame, query_row, query_col, ema_decay, dw_kernel, pw_weight, out_weight
):
    frames_here, rows_here, map_width, channels = feature_maps.shape
    assert frames_here == 1 and channels == LANES
    queries = query_frame.shape[0]
    n_tm, n_space = lax.axis_size("tm"), lax.axis_size("space")
    n_groups = n_tm * n_space
    group = queries // n_groups
    height = rows_here * n_space
    positions = rows_here * map_width
    maps = feature_maps.reshape(positions, channels)
    halves = 2 if n_tm == 2 else 1
    part = jax.ShapeDtypeStruct((queries // halves, channels), BF16)

    picked = call(
        functools.partial(gather_kernel, rows_here, map_width),
        [part] * halves,
        4,
        flops=2 * queries * positions * channels,
        bytes_accessed=2 * positions * channels,
        transcendentals=0,
    )(query_frame[None], query_row[None], query_col[None], maps)

    place = jnp.arange(positions, dtype=jnp.int32)[:, None]
    lane = jnp.arange(LANES, dtype=jnp.int32)[None, :]
    coords = jnp.where(
        lane == 0,
        place % map_width,
        jnp.where(lane == 1, place // map_width, jnp.where(lane == 2, 1, 0)),
    ).astype(BF16)

    if halves == 2:
        mine = picked[0] + swap(picked[1], "tm", 1)
        mine = all_sum(mine, "space")
        feats = [mine, swap(mine, "tm", 1)]
    else:
        feats = [all_sum(all_sum(picked[0], "tm"), "space")]

    feat_rows = -(-group // 8) * 8
    blocks = call(
        functools.partial(volume_kernel, n_groups, rows_here, height, map_width),
        jax.ShapeDtypeStruct((n_groups, feat_rows + AUX_ROWS, LANES), F32),
        halves + 3,
        flops=6 * queries * positions * channels,
        bytes_accessed=4 * positions * channels,
        transcendentals=queries * positions,
    )(*feats, maps, coords, ema_decay)

    blocks = lax.all_to_all(blocks, ("tm", "space"), 0, 0, tiled=True)

    n_out = out_weight.shape[0]
    out_rows = -(-n_tm * n_out // 8) * 8
    lines = call(
        functools.partial(tail_kernel, n_tm, n_space, group),
        jax.ShapeDtypeStruct((out_rows, LANES), F32),
        4,
        flops=2 * n_tm * group * channels * channels,
        bytes_accessed=4 * n_groups * (feat_rows + AUX_ROWS) * LANES,
        transcendentals=n_tm * group * channels,
    )(dw_kernel, pw_weight, out_weight, blocks)

    lines = lax.all_gather(lines, ("tm", "space"), axis=0)
    own = lax.dynamic_slice_in_dim(lines, lax.axis_index("tm") * n_out, n_out, axis=1)
    own = own[:, :, :group]
    return jnp.transpose(own, (1, 0, 2)).reshape(1, n_out, queries)


def core_swap(value):
    return lax.ppermute(value, "tm", [(0, 1), (1, 0)])


def space_swap(value, step):
    n_space = lax.axis_size("space")
    bits = n_space.bit_length() - 1
    pairs = []
    for tm in range(2):
        for space in range(n_space):
            to = space ^ (1 << (tm + step) % bits)
            pairs.append((tm * n_space + space, tm * n_space + to))
    return lax.ppermute(value, ("tm", "space"), pairs)


def local_pair(
    feature_maps, query_frame, query_row, query_col, ema_decay, dw_kernel, pw_weight, out_weight
):
    _, rows_here, map_width, channels = feature_maps.shape
    queries = query_frame.shape[0]
    n_space = lax.axis_size("space")
    half = queries // 2
    height = rows_here * n_space
    positions = rows_here * map_width
    maps = feature_maps.reshape(positions, channels)

    row = query_row - lax.axis_index("space") * rows_here
    here = (query_frame == lax.axis_index("tm")) & (row >= 0) & (row < rows_here)
    target = jnp.where(here, row * map_width + query_col, -1)[None]

    def pick(core_flip):
        return call(
            functools.partial(pick_kernel, core_flip),
            jax.ShapeDtypeStruct((half, channels), BF16),
            2,
            flops=queries * positions * channels,
            bytes_accessed=2 * positions * channels,
            transcendentals=0,
        )(target, maps)

    arrived = core_swap(pick(1))
    coords = call(
        functools.partial(coord_kernel, map_width),
        jax.ShapeDtypeStruct((positions, LANES), BF16),
        1,
        flops=8 * positions * LANES,
        bytes_accessed=2 * positions * LANES,
        transcendentals=0,
    )(target)
    mine = pick(0) + arrived
    steps = n_space.bit_length() - 1
    for step in range(steps):
        mine = mine + space_swap(mine, step)
    theirs = core_swap(mine)

    block = jax.ShapeDtypeStruct((half + half // LANES * PIECE_ROWS, LANES), F32)

    def blocks_of(feats):
        return call(
            functools.partial(half_kernel, rows_here, height, map_width),
            block,
            3,
            flops=3 * queries * positions * channels,
            bytes_accessed=4 * positions * channels,
            transcendentals=half * positions,
        )(feats, maps, coords)

    def sent(value, step):
        value = lax.optimization_barrier(value.astype(jnp.float16))
        return value.astype(F32), space_swap(value, step).astype(F32)

    def merge(pair, step):
        return call(
            functools.partial(merge_kernel, n_space, step),
            block,
            2,
            flops=0,
            bytes_accessed=0,
            transcendentals=0,
        )(*pair)

    pairs = [sent(blocks_of(mine), 0), sent(blocks_of(theirs), 0)]
    for step in range(1, steps):
        pairs = [sent(merge(pair, step - 1), step) for pair in pairs]

    n_out = out_weight.shape[0]
    attended, places = [], []
    for pair in pairs:
        value, place = call(
            functools.partial(last_merge_kernel, n_space, steps - 1),
            [
                jax.ShapeDtypeStruct((half + PIECE_ROWS, LANES), BF16),
                jax.ShapeDtypeStruct((n_out, half), F32),
            ],
            3,
            flops=0,
            bytes_accessed=0,
            transcendentals=0,
        )(ema_decay, *pair)
        attended.append(value)
        places.append(place)
    return call(
        track_kernel,
        jax.ShapeDtypeStruct((1, n_out, queries), F32),
        9,
        flops=8 * queries * channels * channels,
        bytes_accessed=8 * queries * channels,
        transcendentals=2 * queries * channels,
    )(dw_kernel, pw_weight, out_weight, *places, *attended, *[core_swap(v) for v in attended])


def local(feature_maps, query_frame, *rest):
    n_tm, n_space = lax.axis_size("tm"), lax.axis_size("space")
    paired = n_tm == 2 and n_space > 1 and n_space & (n_space - 1) == 0
    if paired and query_frame.shape[0] % (2 * LANES) == 0:
        return local_pair(feature_maps, query_frame, *rest)
    return local_general(feature_maps, query_frame, *rest)


def solution(mesh):
    placed = (
        P(("video", "tm"), "space", None, None),
        P("video"),
        P("video"),
        P("video"),
        P(("video", "tm"), None),
        P(),
        P(),
        P(),
    )
    return jax.shard_map(
        local, mesh=mesh, in_specs=placed, out_specs=P(("video", "tm"), None, None), check_vma=False
    )
```

```python
import functools
import math

import jax
import jax.numpy as jnp
from jax import lax
from jax.experimental import pallas as pl
from jax.experimental.pallas import tpu as pltpu
from jax.sharding import PartitionSpec as P

F32 = jnp.float32
BF16 = jnp.bfloat16
LANES = 128
AUX_ROWS = 8
PIECE_ROWS = 16
VMEM_LIMIT = 40 * 1024 * 1024
NT = (((1,), (1,)), ((), ()))


def pick_chunk(total, limit):
    best = None
    for size in range(LANES, limit + 1, LANES):
        if total % size == 0 and (best is None or size % 256 == 0 or best % 256):
            best = size
    return best if best is not None else total


def gather_kernel(rows_here, map_width, frame_ref, row_ref, col_ref, map_ref, *out_refs):
    positions = map_ref.shape[0]
    queries = frame_ref.shape[1]
    tm = lax.axis_index("tm")
    row = row_ref[...] - lax.axis_index("space") * rows_here
    here = (frame_ref[...] == tm) & (row >= 0) & (row < rows_here)
    target = jnp.where(here, row * map_width + col_ref[...], -1)
    target = jnp.transpose(jnp.broadcast_to(target, (LANES, queries)))
    chunk = pick_chunk(positions, 1536)
    picked = None
    for base in range(0, positions, chunk):
        parts = []
        for lane_base in range(base, base + chunk, LANES):
            lane = lax.broadcasted_iota(jnp.int32, (queries, LANES), 1) + lane_base
            parts.append(jnp.where(lane == target, 1.0, 0.0).astype(BF16))
        hot = jnp.concatenate(parts, axis=1)
        term = jnp.dot(hot, map_ref[base : base + chunk, :], preferred_element_type=F32)
        picked = term if picked is None else picked + term
    if len(out_refs) == 1:
        out_refs[0][...] = picked.astype(BF16)
        return
    half = queries // 2
    first, second = picked[:half].astype(F32), picked[half:].astype(F32)
    out_refs[0][...] = jnp.where(tm == 0, first, second).astype(BF16)
    out_refs[1][...] = jnp.where(tm == 0, second, first).astype(BF16)


def volume_kernel(n_groups, rows_here, height, width, *refs):
    *query_refs, map_ref, coord_ref, decay_ref, out_ref = refs
    positions, channels = map_ref.shape
    factor = math.log2(math.e) / math.sqrt(channels)
    part_queries = query_refs[0].shape[0]
    n_parts = len(query_refs)
    group = part_queries * n_parts // n_groups
    feat_rows = out_ref.shape[1] - AUX_ROWS
    first_row = (lax.axis_index("space") * rows_here).astype(F32)
    tm = lax.axis_index("tm")
    chunk = pick_chunk(positions, 1280)
    state = [None] * n_parts
    for base in range(0, positions, chunk):
        keys = map_ref[base : base + chunk, :]
        values = jnp.concatenate([keys, coord_ref[base : base + chunk, :]], axis=1)
        for part in range(n_parts):
            scores = lax.dot_general(
                query_refs[part][...], keys, NT, preferred_element_type=F32
            )
            top = jnp.max(scores, axis=1, keepdims=True) * factor
            if state[part] is not None:
                old_top, old_sum = state[part]
                top = jnp.maximum(top, old_top)
            weights = jnp.exp2(scores * factor - top).astype(BF16)
            sums = jnp.dot(weights, values, preferred_element_type=F32)
            if state[part] is not None:
                sums = sums + jnp.exp2(old_top - top) * old_sum
            state[part] = (top, sums)
    decay = [decay_ref[...]]
    sub = lax.broadcasted_iota(jnp.int32, (AUX_ROWS, LANES), 0)
    for part in range(n_parts):
        top, sums = state[part]
        feats = sums[:, :channels] / sums[:, channels + 2 : channels + 3]
        extra = sums[:, channels:]
        lane = lax.broadcasted_iota(jnp.int32, extra.shape, 1)
        extra = jnp.transpose(jnp.where(lane == 3, top, extra))
        total = extra[2:3]
        rows = [extra[3:4]]
        rows += [total, extra[0:1] / total / width, (extra[1:2] / total + first_row) / height]
        aux = jnp.zeros((AUX_ROWS, part_queries), F32)
        wide = lax.broadcasted_iota(jnp.int32, aux.shape, 0)
        for index, values in enumerate(rows):
            aux = jnp.where(wide == index, values, aux)
        where = part if n_parts == 1 else jnp.where(tm == 0, part, 1 - part)
        groups_here = n_groups // n_parts
        for index in range(groups_here):
            shift = (part_queries - index * group) % part_queries
            block = pltpu.roll(aux, shift, 1) if shift else aux
            block = block[:, :LANES]
            for offset, piece in enumerate(decay):
                block = jnp.where(sub == len(rows) + offset, piece, block)
            pieces = [feats[index * group : (index + 1) * group]]
            if feat_rows > group:
                pieces.append(jnp.zeros((feat_rows - group, LANES), F32))
            pieces.append(block)
            out_ref[where * groups_here + index] = jnp.concatenate(pieces, axis=0).astype(
                out_ref.dtype
            )


def tail_kernel(n_tm, n_space, group, dw_ref, pw_ref, ow_ref, in_ref, out_ref):
    feat_rows = in_ref.shape[1] - AUX_ROWS
    n_blocks = n_tm * n_space
    blocks = [in_ref[index].astype(F32) for index in range(n_blocks)]
    aux = [block[feat_rows:] for block in blocks]
    positions, shares, decays = [], [], []
    for frame in range(n_tm):
        mine = aux[frame * n_space : (frame + 1) * n_space]
        top = mine[0][0:1]
        for block in mine[1:]:
            top = jnp.maximum(top, block[0:1])
        weight = [jnp.exp2(b[0:1] - top) * b[1:2] for b in mine]
        total = sum(weight[1:], weight[0])
        share = [w / total for w in weight]
        shares += share
        across = [s * b[2:3] for s, b in zip(share, mine)]
        down = [s * b[3:4] for s, b in zip(share, mine)]
        positions.append((sum(across[1:], across[0]), sum(down[1:], down[0])))
        decays.append(mine[0][4:5])
    pad_blocks = -(-n_blocks // 8) * 8
    table = jnp.zeros((pad_blocks, LANES), F32)
    sub = lax.broadcasted_iota(jnp.int32, table.shape, 0)
    for index, share in enumerate(shares):
        table = jnp.where(sub == index, share, table)
    table = jnp.transpose(table)
    attended = []
    for frame in range(n_tm):
        value = None
        for index in range(frame * n_space, (frame + 1) * n_space):
            term = table[:group, index : index + 1] * blocks[index][:group]
            value = term if value is None else value + term
        attended.append(value.astype(BF16).astype(F32))
    taps = dw_ref.shape[0]
    hidden = []
    for frame in range(n_tm):
        depth = None
        for tap in range(taps):
            source = frame + tap - taps // 2
            if 0 <= source < n_tm:
                term = dw_ref[tap : tap + 1, :] * attended[source]
                depth = term if depth is None else depth + term
        hidden.append(jax.nn.gelu(depth).astype(BF16).astype(F32))
    hidden = jnp.concatenate(hidden, axis=0).astype(BF16)
    mixed = jnp.dot(hidden, pw_ref[...], preferred_element_type=F32)
    memory = None
    out = jnp.zeros(out_ref.shape, F32)
    out_sub = lax.broadcasted_iota(jnp.int32, out.shape, 0)
    n_out = ow_ref.shape[0]
    for frame in range(n_tm):
        refined = attended[frame] + mixed[frame * group : (frame + 1) * group]
        fresh = (1.0 - decays[frame]) * refined
        memory = fresh if memory is None else decays[frame] * memory + fresh
        padded = memory
        if group < LANES:
            padded = jnp.concatenate([memory, jnp.zeros((LANES - group, LANES), F32)], axis=0)
        delta = lax.dot_general(
            ow_ref[...], padded, NT, preferred_element_type=F32, precision=lax.Precision.HIGHEST
        )
        for axis in range(n_out):
            line = positions[frame][axis] + delta[axis : axis + 1]
            out = jnp.where(out_sub == frame * n_out + axis, line, out)
    out_ref[...] = out


def call(kernel, out_shape, n_in, **cost):
    vmem = pl.BlockSpec(memory_space=pltpu.VMEM)
    return pl.pallas_call(
        kernel,
        out_shape=out_shape,
        in_specs=[vmem] * n_in,
        out_specs=jax.tree.map(lambda _: vmem, out_shape),
        compiler_params=pltpu.CompilerParams(vmem_limit_bytes=VMEM_LIMIT),
        cost_estimate=pl.CostEstimate(**cost),
    )


def pick_kernel(core_flip, target_ref, map_ref, out_ref):
    half = target_ref.shape[1] // 2
    positions, channels = map_ref.shape
    size = pick_chunk(positions, 256)
    second = lax.axis_index("tm") != core_flip
    target = jnp.where(second, target_ref[:, half:], target_ref[:, :half])
    tile = jnp.where(target < 0, -1, target // size)
    place = target - tile * size
    tile = jnp.transpose(jnp.broadcast_to(tile, (channels, half)))
    place = jnp.transpose(jnp.broadcast_to(place, (LANES, half)))
    lane = lax.broadcasted_iota(jnp.int32, (half, LANES), 1)
    parts = [
        jnp.where(lane + base == place, 1.0, 0.0).astype(BF16) for base in range(0, size, LANES)
    ]
    hot = jnp.concatenate(parts, axis=1)
    picked = jnp.zeros((half, channels), F32)
    tiles = positions // size
    beside = 2 if tiles % 2 == 0 else 1
    for index in range(tiles // beside):
        chosen = [index + side * (tiles // beside) for side in range(beside)]
        keys = [map_ref[i * size : (i + 1) * size, :] for i in chosen]
        rows = jnp.dot(hot, jnp.concatenate(keys, axis=1), preferred_element_type=F32)
        for side, i in enumerate(chosen):
            part = rows[:, side * channels : (side + 1) * channels]
            picked = jnp.where(tile == i, part, picked)
    out_ref[...] = picked.astype(BF16)


def coord_kernel(map_width, after_ref, out_ref):
    positions = out_ref.shape[0]
    chunk = pick_chunk(positions, 512)
    lane = lax.broadcasted_iota(jnp.int32, (chunk, LANES), 1)
    local_place = lax.broadcasted_iota(jnp.int32, (chunk, LANES), 0).astype(F32)

    @pl.loop(0, positions // chunk)
    def _(step):
        place = local_place + (step * chunk).astype(F32)
        row = jnp.floor((place + 0.5) * (1.0 / map_width))
        rest = jnp.where(lane == 2, 1.0, 0.0)
        value = jnp.where(lane == 0, place - row * map_width, jnp.where(lane == 1, row, rest))
        out_ref[pl.ds(pl.multiple_of(step * chunk, chunk), chunk), :] = value.astype(BF16)


def split(value):
    pieces = []
    for _ in range(3):
        piece = value.astype(BF16).astype(F32)
        pieces.append(piece)
        value = value - piece
    return pieces


def half_kernel(rows_here, height, width, query_ref, map_ref, coord_ref, out_ref):
    positions, channels = map_ref.shape
    factor = math.log2(math.e) / math.sqrt(channels)
    query = query_ref[...]
    first_row = (lax.axis_index("space") * rows_here).astype(F32)
    chunk = pick_chunk(positions, 2560)

    def score(base):
        keys = map_ref[base : base + chunk, :]
        return lax.dot_general(query, keys, NT, preferred_element_type=F32)

    top = sums = None
    ahead = score(0)
    for base in range(0, positions, chunk):
        scores = ahead
        if base + chunk < positions:
            ahead = score(base + chunk)
        window = slice(base, base + chunk)
        values = jnp.concatenate([map_ref[window, :], coord_ref[window, :]], axis=1)
        new_top = jnp.max(scores, axis=1, keepdims=True) * factor
        if top is not None:
            new_top = jnp.maximum(new_top, top)
        weights = jnp.exp2(scores * factor - new_top).astype(BF16)
        terms = jnp.dot(weights, values, preferred_element_type=F32)
        sums = terms if sums is None else terms + jnp.exp2(top - new_top) * sums
        top = new_top
    feats = sums[:, :channels] * (1.0 / sums[:, channels + 2 : channels + 3])
    extra = sums[:, channels:]
    lane = lax.broadcasted_iota(jnp.int32, extra.shape, 1)
    extra = jnp.transpose(jnp.where(lane == 3, top, extra))
    total = extra[2:3]
    across = extra[0:1] / total / width
    down = (extra[1:2] / total + first_row) / height
    store_block(out_ref, feats, [extra[3:4], total, across, down])


def store_block(out_ref, feats, lines):
    queries = feats.shape[0]
    out_ref[:queries, :] = feats
    rows = [piece for line in lines for piece in split(line)]
    sub = lax.broadcasted_iota(jnp.int32, (PIECE_ROWS, queries), 0)
    aux = jnp.zeros((PIECE_ROWS, queries), F32)
    for index, row in enumerate(rows):
        aux = jnp.where(sub == index, row, aux)
    for tile in range(queries // LANES):
        base = queries + tile * PIECE_ROWS
        out_ref[base : base + PIECE_ROWS, :] = aux[:, tile * LANES : (tile + 1) * LANES]


def merged(bit, own_ref, came_ref):
    queries = own_ref.shape[0] * LANES // (LANES + PIECE_ROWS)
    high = (lax.axis_index("space") & bit) != 0
    own, came = own_ref[...].astype(F32), came_ref[...].astype(F32)
    pair = [jnp.where(high, came, own), jnp.where(high, own, came)]
    feats, lines = [], []
    for tile in range(queries // LANES):
        base = queries + tile * PIECE_ROWS
        parts = []
        for block in pair:
            aux = block[base : base + PIECE_ROWS]
            parts.append(
                [aux[i : i + 1] + aux[i + 1 : i + 2] + aux[i + 2 : i + 3] for i in (0, 3, 6, 9)]
            )
        (top_a, total_a, *place_a), (top_b, total_b, *place_b) = parts
        top = jnp.maximum(top_a, top_b)
        weight_a, weight_b = jnp.exp2(top_a - top) * total_a, jnp.exp2(top_b - top) * total_b
        total = weight_a + weight_b
        share_a, share_b = weight_a / total, weight_b / total
        places = [share_a * a + share_b * b for a, b in zip(place_a, place_b)]
        lines.append([top, total, *places])
        sub = lax.broadcasted_iota(jnp.int32, (8, LANES), 0)
        table = jnp.transpose(jnp.where(sub == 0, share_a, jnp.where(sub == 1, share_b, 0.0)))
        window = slice(tile * LANES, (tile + 1) * LANES)
        feats.append(table[:, 0:1] * pair[0][window] + table[:, 1:2] * pair[1][window])
    return jnp.concatenate(feats, axis=0), [jnp.concatenate(v, axis=1) for v in zip(*lines)]


def my_bit(step, n_space):
    bits = n_space.bit_length() - 1
    return jnp.left_shift(1, lax.rem(lax.axis_index("tm") + step, bits))


def merge_kernel(n_space, step, own_ref, came_ref, out_ref):
    store_block(out_ref, *merged(my_bit(step, n_space), own_ref, came_ref))


def last_merge_kernel(n_space, step, decay_ref, own_ref, came_ref, out_ref, place_ref):
    feats, lines = merged(my_bit(step, n_space), own_ref, came_ref)
    out_ref[: feats.shape[0], :] = feats.astype(BF16)
    place_ref[0:1, :] = lines[2]
    place_ref[1:2, :] = lines[3]
    sub = lax.broadcasted_iota(jnp.int32, (PIECE_ROWS, LANES), 0)
    rows = jnp.zeros((PIECE_ROWS, LANES), F32)
    for index, piece in enumerate(split(decay_ref[...])):
        rows = jnp.where(sub == index, piece, rows)
    out_ref[feats.shape[0] :, :] = rows.astype(BF16)


def track_kernel(
    dw_ref, pw_ref, ow_ref, near_place, far_place, near_mine, far_mine, near_came, far_came, out_ref
):
    early = lax.axis_index("tm") == 0
    half = near_place.shape[1]

    def retention(ref):
        rows = ref[half:, :].astype(F32)
        return rows[0:1] + rows[1:2] + rows[2:3]

    decay_mine, decay_theirs = retention(near_mine), retention(near_came)
    mine = jnp.concatenate([near_mine[:half, :], far_mine[:half, :]], axis=0).astype(F32)
    theirs = jnp.concatenate([far_came[:half, :], near_came[:half, :]], axis=0).astype(F32)
    attended = [jnp.where(early, mine, theirs), jnp.where(early, theirs, mine)]
    decay = [
        jnp.where(early, decay_mine, decay_theirs),
        jnp.where(early, decay_theirs, decay_mine),
    ]
    taps = dw_ref.shape[0]
    refined = []
    for frame in range(2):
        depth = None
        for tap in range(taps):
            source = frame + tap - taps // 2
            if 0 <= source < 2:
                term = dw_ref[tap : tap + 1, :] * attended[source]
                depth = term if depth is None else depth + term
        hidden = jax.nn.gelu(depth).astype(BF16)
        mixed = jnp.dot(hidden, pw_ref[...], preferred_element_type=F32)
        refined.append(attended[frame] + mixed)
    first = (1.0 - decay[0]) * refined[0]
    second = decay[1] * first + (1.0 - decay[1]) * refined[1]
    memory = jnp.where(early, first, second)
    n_out = ow_ref.shape[0]
    weights = jnp.concatenate(split(ow_ref[...]), axis=0).astype(BF16)
    line = jnp.concatenate([near_place[...], far_place[...]], axis=1)
    for piece in split(memory)[:2]:
        terms = lax.dot_general(weights, piece.astype(BF16), NT, preferred_element_type=F32)
        line = line + terms[:n_out] + terms[n_out : 2 * n_out] + terms[2 * n_out :]
    low, high = line[:, :half], line[:, half:]
    out_ref[0, :, :half] = jnp.where(early, low, high)
    out_ref[0, :, half:] = jnp.where(early, high, low)


def swap(value, axis, bit):
    return lax.ppermute(value, axis, [(i, i ^ bit) for i in range(lax.axis_size(axis))])


def all_sum(value, axis):
    count = lax.axis_size(axis)
    if count & (count - 1):
        return lax.psum(value, axis)
    bit = 1
    while bit < count:
        value = value + swap(value, axis, bit)
        bit *= 2
    return value


def local_general(
    feature_maps, query_frame, query_row, query_col, ema_decay, dw_kernel, pw_weight, out_weight
):
    frames_here, rows_here, map_width, channels = feature_maps.shape
    assert frames_here == 1 and channels == LANES
    queries = query_frame.shape[0]
    n_tm, n_space = lax.axis_size("tm"), lax.axis_size("space")
    n_groups = n_tm * n_space
    group = queries // n_groups
    height = rows_here * n_space
    positions = rows_here * map_width
    maps = feature_maps.reshape(positions, channels)
    halves = 2 if n_tm == 2 else 1
    part = jax.ShapeDtypeStruct((queries // halves, channels), BF16)

    picked = call(
        functools.partial(gather_kernel, rows_here, map_width),
        [part] * halves,
        4,
        flops=2 * queries * positions * channels,
        bytes_accessed=2 * positions * channels,
        transcendentals=0,
    )(query_frame[None], query_row[None], query_col[None], maps)

    place = jnp.arange(positions, dtype=jnp.int32)[:, None]
    lane = jnp.arange(LANES, dtype=jnp.int32)[None, :]
    coords = jnp.where(
        lane == 0,
        place % map_width,
        jnp.where(lane == 1, place // map_width, jnp.where(lane == 2, 1, 0)),
    ).astype(BF16)

    if halves == 2:
        mine = picked[0] + swap(picked[1], "tm", 1)
        mine = all_sum(mine, "space")
        feats = [mine, swap(mine, "tm", 1)]
    else:
        feats = [all_sum(all_sum(picked[0], "tm"), "space")]

    feat_rows = -(-group // 8) * 8
    blocks = call(
        functools.partial(volume_kernel, n_groups, rows_here, height, map_width),
        jax.ShapeDtypeStruct((n_groups, feat_rows + AUX_ROWS, LANES), F32),
        halves + 3,
        flops=6 * queries * positions * channels,
        bytes_accessed=4 * positions * channels,
        transcendentals=queries * positions,
    )(*feats, maps, coords, ema_decay)

    blocks = lax.all_to_all(blocks, ("tm", "space"), 0, 0, tiled=True)

    n_out = out_weight.shape[0]
    out_rows = -(-n_tm * n_out // 8) * 8
    lines = call(
        functools.partial(tail_kernel, n_tm, n_space, group),
        jax.ShapeDtypeStruct((out_rows, LANES), F32),
        4,
        flops=2 * n_tm * group * channels * channels,
        bytes_accessed=4 * n_groups * (feat_rows + AUX_ROWS) * LANES,
        transcendentals=n_tm * group * channels,
    )(dw_kernel, pw_weight, out_weight, blocks)

    lines = lax.all_gather(lines, ("tm", "space"), axis=0)
    own = lax.dynamic_slice_in_dim(lines, lax.axis_index("tm") * n_out, n_out, axis=1)
    own = own[:, :, :group]
    return jnp.transpose(own, (1, 0, 2)).reshape(1, n_out, queries)


def core_swap(value):
    return lax.ppermute(value, "tm", [(0, 1), (1, 0)])


def space_swap(value, step):
    n_space = lax.axis_size("space")
    bits = n_space.bit_length() - 1
    pairs = []
    for tm in range(2):
        for space in range(n_space):
            to = space ^ (1 << (tm + step) % bits)
            pairs.append((tm * n_space + space, tm * n_space + to))
    return lax.ppermute(value, ("tm", "space"), pairs)


def local_pair(
    feature_maps, query_frame, query_row, query_col, ema_decay, dw_kernel, pw_weight, out_weight
):
    _, rows_here, map_width, channels = feature_maps.shape
    queries = query_frame.shape[0]
    n_space = lax.axis_size("space")
    half = queries // 2
    height = rows_here * n_space
    positions = rows_here * map_width
    maps = feature_maps.reshape(positions, channels)

    row = query_row - lax.axis_index("space") * rows_here
    here = (query_frame == lax.axis_index("tm")) & (row >= 0) & (row < rows_here)
    target = jnp.where(here, row * map_width + query_col, -1)[None]

    def pick(core_flip):
        return call(
            functools.partial(pick_kernel, core_flip),
            jax.ShapeDtypeStruct((half, channels), BF16),
            2,
            flops=queries * positions * channels,
            bytes_accessed=2 * positions * channels,
            transcendentals=0,
        )(target, maps)

    arrived = core_swap(pick(1))
    coords = call(
        functools.partial(coord_kernel, map_width),
        jax.ShapeDtypeStruct((positions, LANES), BF16),
        1,
        flops=8 * positions * LANES,
        bytes_accessed=2 * positions * LANES,
        transcendentals=0,
    )(target)
    mine = pick(0) + arrived
    steps = n_space.bit_length() - 1
    for step in range(steps):
        mine = mine + space_swap(mine, step)
    theirs = core_swap(mine)

    block = jax.ShapeDtypeStruct((half + half // LANES * PIECE_ROWS, LANES), F32)

    def blocks_of(feats):
        return call(
            functools.partial(half_kernel, rows_here, height, map_width),
            block,
            3,
            flops=3 * queries * positions * channels,
            bytes_accessed=4 * positions * channels,
            transcendentals=half * positions,
        )(feats, maps, coords)

    def sent(value, step):
        value = lax.optimization_barrier(value.astype(jnp.float16))
        return value.astype(F32), space_swap(value, step).astype(F32)

    def merge(pair, step):
        return call(
            functools.partial(merge_kernel, n_space, step),
            block,
            2,
            flops=0,
            bytes_accessed=0,
            transcendentals=0,
        )(*pair)

    pairs = [sent(blocks_of(mine), 0), sent(blocks_of(theirs), 0)]
    for step in range(1, steps):
        pairs = [sent(merge(pair, step - 1), step) for pair in pairs]

    n_out = out_weight.shape[0]
    attended, places = [], []
    for pair in pairs:
        value, place = call(
            functools.partial(last_merge_kernel, n_space, steps - 1),
            [
                jax.ShapeDtypeStruct((half + PIECE_ROWS, LANES), BF16),
                jax.ShapeDtypeStruct((n_out, half), F32),
            ],
            3,
            flops=0,
            bytes_accessed=0,
            transcendentals=0,
        )(ema_decay, *pair)
        attended.append(value)
        places.append(place)
    return call(
        track_kernel,
        jax.ShapeDtypeStruct((1, n_out, queries), F32),
        9,
        flops=8 * queries * channels * channels,
        bytes_accessed=8 * queries * channels,
        transcendentals=2 * queries * channels,
    )(dw_kernel, pw_weight, out_weight, *places, *attended, *[core_swap(v) for v in attended])


def local(feature_maps, query_frame, *rest):
    n_tm, n_space = lax.axis_size("tm"), lax.axis_size("space")
    paired = n_tm == 2 and n_space > 1 and n_space & (n_space - 1) == 0
    if paired and query_frame.shape[0] % (2 * LANES) == 0:
        return local_pair(feature_maps, query_frame, *rest)
    return local_general(feature_maps, query_frame, *rest)


def solution(mesh):
    placed = (
        P(("video", "tm"), "space", None, None),
        P("video"),
        P("video"),
        P("video"),
        P(("video", "tm"), None),
        P(),
        P(),
        P(),
    )
    return jax.shard_map(
        local, mesh=mesh, in_specs=placed, out_specs=P(("video", "tm"), None, None), check_vma=False
    )
```

```python
import functools
import math

import jax
import jax.numpy as jnp
from jax import lax
from jax.experimental import pallas as pl
from jax.experimental.pallas import tpu as pltpu
from jax.sharding import PartitionSpec as P

F32 = jnp.float32
BF16 = jnp.bfloat16
LANES = 128
AUX_ROWS = 8
PIECE_ROWS = 16
VMEM_LIMIT = 40 * 1024 * 1024
NT = (((1,), (1,)), ((), ()))


def pick_chunk(total, limit):
    best = None
    for size in range(LANES, limit + 1, LANES):
        if total % size == 0 and (best is None or size % 256 == 0 or best % 256):
            best = size
    return best if best is not None else total


def gather_kernel(rows_here, map_width, frame_ref, row_ref, col_ref, map_ref, *out_refs):
    positions = map_ref.shape[0]
    queries = frame_ref.shape[1]
    tm = lax.axis_index("tm")
    row = row_ref[...] - lax.axis_index("space") * rows_here
    here = (frame_ref[...] == tm) & (row >= 0) & (row < rows_here)
    target = jnp.where(here, row * map_width + col_ref[...], -1)
    target = jnp.transpose(jnp.broadcast_to(target, (LANES, queries)))
    chunk = pick_chunk(positions, 1536)
    picked = None
    for base in range(0, positions, chunk):
        parts = []
        for lane_base in range(base, base + chunk, LANES):
            lane = lax.broadcasted_iota(jnp.int32, (queries, LANES), 1) + lane_base
            parts.append(jnp.where(lane == target, 1.0, 0.0).astype(BF16))
        hot = jnp.concatenate(parts, axis=1)
        term = jnp.dot(hot, map_ref[base : base + chunk, :], preferred_element_type=F32)
        picked = term if picked is None else picked + term
    if len(out_refs) == 1:
        out_refs[0][...] = picked.astype(BF16)
        return
    half = queries // 2
    first, second = picked[:half].astype(F32), picked[half:].astype(F32)
    out_refs[0][...] = jnp.where(tm == 0, first, second).astype(BF16)
    out_refs[1][...] = jnp.where(tm == 0, second, first).astype(BF16)


def volume_kernel(n_groups, rows_here, height, width, *refs):
    *query_refs, map_ref, coord_ref, decay_ref, out_ref = refs
    positions, channels = map_ref.shape
    factor = math.log2(math.e) / math.sqrt(channels)
    part_queries = query_refs[0].shape[0]
    n_parts = len(query_refs)
    group = part_queries * n_parts // n_groups
    feat_rows = out_ref.shape[1] - AUX_ROWS
    first_row = (lax.axis_index("space") * rows_here).astype(F32)
    tm = lax.axis_index("tm")
    chunk = pick_chunk(positions, 1280)
    state = [None] * n_parts
    for base in range(0, positions, chunk):
        keys = map_ref[base : base + chunk, :]
        values = jnp.concatenate([keys, coord_ref[base : base + chunk, :]], axis=1)
        for part in range(n_parts):
            scores = lax.dot_general(
                query_refs[part][...], keys, NT, preferred_element_type=F32
            )
            top = jnp.max(scores, axis=1, keepdims=True) * factor
            if state[part] is not None:
                old_top, old_sum = state[part]
                top = jnp.maximum(top, old_top)
            weights = jnp.exp2(scores * factor - top).astype(BF16)
            sums = jnp.dot(weights, values, preferred_element_type=F32)
            if state[part] is not None:
                sums = sums + jnp.exp2(old_top - top) * old_sum
            state[part] = (top, sums)
    decay = [decay_ref[...]]
    sub = lax.broadcasted_iota(jnp.int32, (AUX_ROWS, LANES), 0)
    for part in range(n_parts):
        top, sums = state[part]
        feats = sums[:, :channels] / sums[:, channels + 2 : channels + 3]
        extra = sums[:, channels:]
        lane = lax.broadcasted_iota(jnp.int32, extra.shape, 1)
        extra = jnp.transpose(jnp.where(lane == 3, top, extra))
        total = extra[2:3]
        rows = [extra[3:4]]
        rows += [total, extra[0:1] / total / width, (extra[1:2] / total + first_row) / height]
        aux = jnp.zeros((AUX_ROWS, part_queries), F32)
        wide = lax.broadcasted_iota(jnp.int32, aux.shape, 0)
        for index, values in enumerate(rows):
            aux = jnp.where(wide == index, values, aux)
        where = part if n_parts == 1 else jnp.where(tm == 0, part, 1 - part)
        groups_here = n_groups // n_parts
        for index in range(groups_here):
            shift = (part_queries - index * group) % part_queries
            block = pltpu.roll(aux, shift, 1) if shift else aux
            block = block[:, :LANES]
            for offset, piece in enumerate(decay):
                block = jnp.where(sub == len(rows) + offset, piece, block)
            pieces = [feats[index * group : (index + 1) * group]]
            if feat_rows > group:
                pieces.append(jnp.zeros((feat_rows - group, LANES), F32))
            pieces.append(block)
            out_ref[where * groups_here + index] = jnp.concatenate(pieces, axis=0).astype(
                out_ref.dtype
            )


def tail_kernel(n_tm, n_space, group, dw_ref, pw_ref, ow_ref, in_ref, out_ref):
    feat_rows = in_ref.shape[1] - AUX_ROWS
    n_blocks = n_tm * n_space
    blocks = [in_ref[index].astype(F32) for index in range(n_blocks)]
    aux = [block[feat_rows:] for block in blocks]
    positions, shares, decays = [], [], []
    for frame in range(n_tm):
        mine = aux[frame * n_space : (frame + 1) * n_space]
        top = mine[0][0:1]
        for block in mine[1:]:
            top = jnp.maximum(top, block[0:1])
        weight = [jnp.exp2(b[0:1] - top) * b[1:2] for b in mine]
        total = sum(weight[1:], weight[0])
        share = [w / total for w in weight]
        shares += share
        across = [s * b[2:3] for s, b in zip(share, mine)]
        down = [s * b[3:4] for s, b in zip(share, mine)]
        positions.append((sum(across[1:], across[0]), sum(down[1:], down[0])))
        decays.append(mine[0][4:5])
    pad_blocks = -(-n_blocks // 8) * 8
    table = jnp.zeros((pad_blocks, LANES), F32)
    sub = lax.broadcasted_iota(jnp.int32, table.shape, 0)
    for index, share in enumerate(shares):
        table = jnp.where(sub == index, share, table)
    table = jnp.transpose(table)
    attended = []
    for frame in range(n_tm):
        value = None
        for index in range(frame * n_space, (frame + 1) * n_space):
            term = table[:group, index : index + 1] * blocks[index][:group]
            value = term if value is None else value + term
        attended.append(value.astype(BF16).astype(F32))
    taps = dw_ref.shape[0]
    hidden = []
    for frame in range(n_tm):
        depth = None
        for tap in range(taps):
            source = frame + tap - taps // 2
            if 0 <= source < n_tm:
                term = dw_ref[tap : tap + 1, :] * attended[source]
                depth = term if depth is None else depth + term
        hidden.append(jax.nn.gelu(depth).astype(BF16).astype(F32))
    hidden = jnp.concatenate(hidden, axis=0).astype(BF16)
    mixed = jnp.dot(hidden, pw_ref[...], preferred_element_type=F32)
    memory = None
    out = jnp.zeros(out_ref.shape, F32)
    out_sub = lax.broadcasted_iota(jnp.int32, out.shape, 0)
    n_out = ow_ref.shape[0]
    for frame in range(n_tm):
        refined = attended[frame] + mixed[frame * group : (frame + 1) * group]
        fresh = (1.0 - decays[frame]) * refined
        memory = fresh if memory is None else decays[frame] * memory + fresh
        padded = memory
        if group < LANES:
            padded = jnp.concatenate([memory, jnp.zeros((LANES - group, LANES), F32)], axis=0)
        delta = lax.dot_general(
            ow_ref[...], padded, NT, preferred_element_type=F32, precision=lax.Precision.HIGHEST
        )
        for axis in range(n_out):
            line = positions[frame][axis] + delta[axis : axis + 1]
            out = jnp.where(out_sub == frame * n_out + axis, line, out)
    out_ref[...] = out


def call(kernel, out_shape, n_in, **cost):
    vmem = pl.BlockSpec(memory_space=pltpu.VMEM)
    return pl.pallas_call(
        kernel,
        out_shape=out_shape,
        in_specs=[vmem] * n_in,
        out_specs=jax.tree.map(lambda _: vmem, out_shape),
        compiler_params=pltpu.CompilerParams(vmem_limit_bytes=VMEM_LIMIT),
        cost_estimate=pl.CostEstimate(**cost),
    )


def pick_kernel(core_flip, target_ref, map_ref, out_ref):
    half = target_ref.shape[1] // 2
    positions, channels = map_ref.shape
    size = pick_chunk(positions, 256)
    second = lax.axis_index("tm") != core_flip
    target = jnp.where(second, target_ref[:, half:], target_ref[:, :half])
    tile = jnp.where(target < 0, -1, target // size)
    place = target - tile * size
    tile = jnp.transpose(jnp.broadcast_to(tile, (channels, half)))
    place = jnp.transpose(jnp.broadcast_to(place, (LANES, half)))
    lane = lax.broadcasted_iota(jnp.int32, (half, LANES), 1)
    parts = [
        jnp.where(lane + base == place, 1.0, 0.0).astype(BF16) for base in range(0, size, LANES)
    ]
    hot = jnp.concatenate(parts, axis=1)
    picked = jnp.zeros((half, channels), F32)
    tiles = positions // size
    beside = 2 if tiles % 2 == 0 else 1
    for index in range(tiles // beside):
        chosen = [index + side * (tiles // beside) for side in range(beside)]
        keys = [map_ref[i * size : (i + 1) * size, :] for i in chosen]
        rows = jnp.dot(hot, jnp.concatenate(keys, axis=1), preferred_element_type=F32)
        for side, i in enumerate(chosen):
            part = rows[:, side * channels : (side + 1) * channels]
            picked = jnp.where(tile == i, part, picked)
    out_ref[...] = picked.astype(BF16)


def coord_kernel(map_width, after_ref, out_ref):
    positions = out_ref.shape[0]
    chunk = pick_chunk(positions, 512)
    lane = lax.broadcasted_iota(jnp.int32, (chunk, LANES), 1)
    local_place = lax.broadcasted_iota(jnp.int32, (chunk, LANES), 0).astype(F32)

    @pl.loop(0, positions // chunk)
    def _(step):
        place = local_place + (step * chunk).astype(F32)
        row = jnp.floor((place + 0.5) * (1.0 / map_width))
        rest = jnp.where(lane == 2, 1.0, 0.0)
        value = jnp.where(lane == 0, place - row * map_width, jnp.where(lane == 1, row, rest))
        out_ref[pl.ds(pl.multiple_of(step * chunk, chunk), chunk), :] = value.astype(BF16)


def split(value):
    pieces = []
    for _ in range(3):
        piece = value.astype(BF16).astype(F32)
        pieces.append(piece)
        value = value - piece
    return pieces


def half_kernel(rows_here, height, width, query_ref, map_ref, coord_ref, out_ref):
    positions, channels = map_ref.shape
    factor = math.log2(math.e) / math.sqrt(channels)
    query = query_ref[...]
    first_row = (lax.axis_index("space") * rows_here).astype(F32)
    chunk = pick_chunk(positions, 3840)

    def score(base):
        keys = map_ref[base : base + chunk, :]
        return lax.dot_general(query, keys, NT, preferred_element_type=F32)

    top = sums = None
    ahead = score(0)
    for base in range(0, positions, chunk):
        scores = ahead
        if base + chunk < positions:
            ahead = score(base + chunk)
        window = slice(base, base + chunk)
        values = jnp.concatenate([map_ref[window, :], coord_ref[window, :]], axis=1)
        new_top = jnp.max(scores, axis=1, keepdims=True) * factor
        if top is not None:
            new_top = jnp.maximum(new_top, top)
        weights = jnp.exp2(scores * factor - new_top).astype(BF16)
        terms = jnp.dot(weights, values, preferred_element_type=F32)
        sums = terms if sums is None else terms + jnp.exp2(top - new_top) * sums
        top = new_top
    feats = sums[:, :channels] * (1.0 / sums[:, channels + 2 : channels + 3])
    extra = sums[:, channels:]
    lane = lax.broadcasted_iota(jnp.int32, extra.shape, 1)
    extra = jnp.transpose(jnp.where(lane == 3, top, extra))
    total = extra[2:3]
    across = extra[0:1] / total / width
    down = (extra[1:2] / total + first_row) / height
    store_block(out_ref, feats, [extra[3:4], total, across, down])


def store_block(out_ref, feats, lines):
    queries = feats.shape[0]
    out_ref[:queries, :] = feats
    rows = [piece for line in lines for piece in split(line)]
    sub = lax.broadcasted_iota(jnp.int32, (PIECE_ROWS, queries), 0)
    aux = jnp.zeros((PIECE_ROWS, queries), F32)
    for index, row in enumerate(rows):
        aux = jnp.where(sub == index, row, aux)
    for tile in range(queries // LANES):
        base = queries + tile * PIECE_ROWS
        out_ref[base : base + PIECE_ROWS, :] = aux[:, tile * LANES : (tile + 1) * LANES]


def merged(bit, own_ref, came_ref):
    queries = own_ref.shape[0] * LANES // (LANES + PIECE_ROWS)
    high = (lax.axis_index("space") & bit) != 0
    own, came = own_ref[...].astype(F32), came_ref[...].astype(F32)
    pair = [jnp.where(high, came, own), jnp.where(high, own, came)]
    feats, lines = [], []
    for tile in range(queries // LANES):
        base = queries + tile * PIECE_ROWS
        parts = []
        for block in pair:
            aux = block[base : base + PIECE_ROWS]
            parts.append(
                [aux[i : i + 1] + aux[i + 1 : i + 2] + aux[i + 2 : i + 3] for i in (0, 3, 6, 9)]
            )
        (top_a, total_a, *place_a), (top_b, total_b, *place_b) = parts
        top = jnp.maximum(top_a, top_b)
        weight_a, weight_b = jnp.exp2(top_a - top) * total_a, jnp.exp2(top_b - top) * total_b
        total = weight_a + weight_b
        share_a, share_b = weight_a / total, weight_b / total
        places = [share_a * a + share_b * b for a, b in zip(place_a, place_b)]
        lines.append([top, total, *places])
        sub = lax.broadcasted_iota(jnp.int32, (8, LANES), 0)
        table = jnp.transpose(jnp.where(sub == 0, share_a, jnp.where(sub == 1, share_b, 0.0)))
        window = slice(tile * LANES, (tile + 1) * LANES)
        feats.append(table[:, 0:1] * pair[0][window] + table[:, 1:2] * pair[1][window])
    return jnp.concatenate(feats, axis=0), [jnp.concatenate(v, axis=1) for v in zip(*lines)]


def my_bit(step, n_space):
    bits = n_space.bit_length() - 1
    return jnp.left_shift(1, lax.rem(lax.axis_index("tm") + step, bits))


def merge_kernel(n_space, step, own_ref, came_ref, out_ref):
    store_block(out_ref, *merged(my_bit(step, n_space), own_ref, came_ref))


def last_merge_kernel(n_space, step, decay_ref, own_ref, came_ref, out_ref, place_ref):
    feats, lines = merged(my_bit(step, n_space), own_ref, came_ref)
    out_ref[: feats.shape[0], :] = feats.astype(BF16)
    place_ref[0:1, :] = lines[2]
    place_ref[1:2, :] = lines[3]
    sub = lax.broadcasted_iota(jnp.int32, (PIECE_ROWS, LANES), 0)
    rows = jnp.zeros((PIECE_ROWS, LANES), F32)
    for index, piece in enumerate(split(decay_ref[...])):
        rows = jnp.where(sub == index, piece, rows)
    out_ref[feats.shape[0] :, :] = rows.astype(BF16)


def track_kernel(
    dw_ref, pw_ref, ow_ref, near_place, far_place, near_mine, far_mine, near_came, far_came, out_ref
):
    early = lax.axis_index("tm") == 0
    half = near_place.shape[1]

    def retention(ref):
        rows = ref[half:, :].astype(F32)
        return rows[0:1] + rows[1:2] + rows[2:3]

    decay_mine, decay_theirs = retention(near_mine), retention(near_came)
    mine = jnp.concatenate([near_mine[:half, :], far_mine[:half, :]], axis=0).astype(F32)
    theirs = jnp.concatenate([far_came[:half, :], near_came[:half, :]], axis=0).astype(F32)
    attended = [jnp.where(early, mine, theirs), jnp.where(early, theirs, mine)]
    decay = [
        jnp.where(early, decay_mine, decay_theirs),
        jnp.where(early, decay_theirs, decay_mine),
    ]
    taps = dw_ref.shape[0]
    refined = []
    for frame in range(2):
        depth = None
        for tap in range(taps):
            source = frame + tap - taps // 2
            if 0 <= source < 2:
                term = dw_ref[tap : tap + 1, :] * attended[source]
                depth = term if depth is None else depth + term
        hidden = jax.nn.gelu(depth).astype(BF16)
        mixed = jnp.dot(hidden, pw_ref[...], preferred_element_type=F32)
        refined.append(attended[frame] + mixed)
    first = (1.0 - decay[0]) * refined[0]
    second = decay[1] * first + (1.0 - decay[1]) * refined[1]
    memory = jnp.where(early, first, second)
    n_out = ow_ref.shape[0]
    weights = jnp.concatenate(split(ow_ref[...]), axis=0).astype(BF16)
    line = jnp.concatenate([near_place[...], far_place[...]], axis=1)
    for piece in split(memory)[:2]:
        terms = lax.dot_general(weights, piece.astype(BF16), NT, preferred_element_type=F32)
        line = line + terms[:n_out] + terms[n_out : 2 * n_out] + terms[2 * n_out :]
    low, high = line[:, :half], line[:, half:]
    out_ref[0, :, :half] = jnp.where(early, low, high)
    out_ref[0, :, half:] = jnp.where(early, high, low)


def swap(value, axis, bit):
    return lax.ppermute(value, axis, [(i, i ^ bit) for i in range(lax.axis_size(axis))])


def all_sum(value, axis):
    count = lax.axis_size(axis)
    if count & (count - 1):
        return lax.psum(value, axis)
    bit = 1
    while bit < count:
        value = value + swap(value, axis, bit)
        bit *= 2
    return value


def local_general(
    feature_maps, query_frame, query_row, query_col, ema_decay, dw_kernel, pw_weight, out_weight
):
    frames_here, rows_here, map_width, channels = feature_maps.shape
    assert frames_here == 1 and channels == LANES
    queries = query_frame.shape[0]
    n_tm, n_space = lax.axis_size("tm"), lax.axis_size("space")
    n_groups = n_tm * n_space
    group = queries // n_groups
    height = rows_here * n_space
    positions = rows_here * map_width
    maps = feature_maps.reshape(positions, channels)
    halves = 2 if n_tm == 2 else 1
    part = jax.ShapeDtypeStruct((queries // halves, channels), BF16)

    picked = call(
        functools.partial(gather_kernel, rows_here, map_width),
        [part] * halves,
        4,
        flops=2 * queries * positions * channels,
        bytes_accessed=2 * positions * channels,
        transcendentals=0,
    )(query_frame[None], query_row[None], query_col[None], maps)

    place = jnp.arange(positions, dtype=jnp.int32)[:, None]
    lane = jnp.arange(LANES, dtype=jnp.int32)[None, :]
    coords = jnp.where(
        lane == 0,
        place % map_width,
        jnp.where(lane == 1, place // map_width, jnp.where(lane == 2, 1, 0)),
    ).astype(BF16)

    if halves == 2:
        mine = picked[0] + swap(picked[1], "tm", 1)
        mine = all_sum(mine, "space")
        feats = [mine, swap(mine, "tm", 1)]
    else:
        feats = [all_sum(all_sum(picked[0], "tm"), "space")]

    feat_rows = -(-group // 8) * 8
    blocks = call(
        functools.partial(volume_kernel, n_groups, rows_here, height, map_width),
        jax.ShapeDtypeStruct((n_groups, feat_rows + AUX_ROWS, LANES), F32),
        halves + 3,
        flops=6 * queries * positions * channels,
        bytes_accessed=4 * positions * channels,
        transcendentals=queries * positions,
    )(*feats, maps, coords, ema_decay)

    blocks = lax.all_to_all(blocks, ("tm", "space"), 0, 0, tiled=True)

    n_out = out_weight.shape[0]
    out_rows = -(-n_tm * n_out // 8) * 8
    lines = call(
        functools.partial(tail_kernel, n_tm, n_space, group),
        jax.ShapeDtypeStruct((out_rows, LANES), F32),
        4,
        flops=2 * n_tm * group * channels * channels,
        bytes_accessed=4 * n_groups * (feat_rows + AUX_ROWS) * LANES,
        transcendentals=n_tm * group * channels,
    )(dw_kernel, pw_weight, out_weight, blocks)

    lines = lax.all_gather(lines, ("tm", "space"), axis=0)
    own = lax.dynamic_slice_in_dim(lines, lax.axis_index("tm") * n_out, n_out, axis=1)
    own = own[:, :, :group]
    return jnp.transpose(own, (1, 0, 2)).reshape(1, n_out, queries)


def core_swap(value):
    return lax.ppermute(value, "tm", [(0, 1), (1, 0)])


def space_swap(value, step):
    n_space = lax.axis_size("space")
    bits = n_space.bit_length() - 1
    pairs = []
    for tm in range(2):
        for space in range(n_space):
            to = space ^ (1 << (tm + step) % bits)
            pairs.append((tm * n_space + space, tm * n_space + to))
    return lax.ppermute(value, ("tm", "space"), pairs)


def local_pair(
    feature_maps, query_frame, query_row, query_col, ema_decay, dw_kernel, pw_weight, out_weight
):
    _, rows_here, map_width, channels = feature_maps.shape
    queries = query_frame.shape[0]
    n_space = lax.axis_size("space")
    half = queries // 2
    height = rows_here * n_space
    positions = rows_here * map_width
    maps = feature_maps.reshape(positions, channels)

    row = query_row - lax.axis_index("space") * rows_here
    here = (query_frame == lax.axis_index("tm")) & (row >= 0) & (row < rows_here)
    target = jnp.where(here, row * map_width + query_col, -1)[None]

    def pick(core_flip):
        return call(
            functools.partial(pick_kernel, core_flip),
            jax.ShapeDtypeStruct((half, channels), BF16),
            2,
            flops=queries * positions * channels,
            bytes_accessed=2 * positions * channels,
            transcendentals=0,
        )(target, maps)

    arrived = core_swap(pick(1))
    coords = call(
        functools.partial(coord_kernel, map_width),
        jax.ShapeDtypeStruct((positions, LANES), BF16),
        1,
        flops=8 * positions * LANES,
        bytes_accessed=2 * positions * LANES,
        transcendentals=0,
    )(target)
    mine = pick(0) + arrived
    steps = n_space.bit_length() - 1
    for step in range(steps):
        mine = mine + space_swap(mine, step)
    theirs = core_swap(mine)

    block = jax.ShapeDtypeStruct((half + half // LANES * PIECE_ROWS, LANES), F32)

    def blocks_of(feats):
        return call(
            functools.partial(half_kernel, rows_here, height, map_width),
            block,
            3,
            flops=3 * queries * positions * channels,
            bytes_accessed=4 * positions * channels,
            transcendentals=half * positions,
        )(feats, maps, coords)

    def sent(value, step):
        value = lax.optimization_barrier(value.astype(jnp.float16))
        return value.astype(F32), space_swap(value, step).astype(F32)

    def merge(pair, step):
        return call(
            functools.partial(merge_kernel, n_space, step),
            block,
            2,
            flops=0,
            bytes_accessed=0,
            transcendentals=0,
        )(*pair)

    pairs = [sent(blocks_of(mine), 0), sent(blocks_of(theirs), 0)]
    for step in range(1, steps):
        pairs = [sent(merge(pair, step - 1), step) for pair in pairs]

    n_out = out_weight.shape[0]
    attended, places = [], []
    for pair in pairs:
        value, place = call(
            functools.partial(last_merge_kernel, n_space, steps - 1),
            [
                jax.ShapeDtypeStruct((half + PIECE_ROWS, LANES), BF16),
                jax.ShapeDtypeStruct((n_out, half), F32),
            ],
            3,
            flops=0,
            bytes_accessed=0,
            transcendentals=0,
        )(ema_decay, *pair)
        attended.append(value)
        places.append(place)
    return call(
        track_kernel,
        jax.ShapeDtypeStruct((1, n_out, queries), F32),
        9,
        flops=8 * queries * channels * channels,
        bytes_accessed=8 * queries * channels,
        transcendentals=2 * queries * channels,
    )(dw_kernel, pw_weight, out_weight, *places, *attended, *[core_swap(v) for v in attended])


def local(feature_maps, query_frame, *rest):
    n_tm, n_space = lax.axis_size("tm"), lax.axis_size("space")
    paired = n_tm == 2 and n_space > 1 and n_space & (n_space - 1) == 0
    if paired and query_frame.shape[0] % (2 * LANES) == 0:
        return local_pair(feature_maps, query_frame, *rest)
    return local_general(feature_maps, query_frame, *rest)


def solution(mesh):
    placed = (
        P(("video", "tm"), "space", None, None),
        P("video"),
        P("video"),
        P("video"),
        P(("video", "tm"), None),
        P(),
        P(),
        P(),
    )
    return jax.shard_map(
        local, mesh=mesh, in_specs=placed, out_specs=P(("video", "tm"), None, None), check_vma=False
    )
```
